32 devices in a mesh: fsdp: 4 (over x, core), ctx: 8 (over z, y).
Axes of the slice: x: 2, y: 2, z: 4, core: 2. Of those that a mesh axis runs over, the one named last changes fastest.
Arguments:
- layer_in: bfloat16 [8, 1024, 768], P('fsdp', 'ctx'), may hold values from -6 to 6
- encoded: bfloat16 [8, 1024, 768], P('fsdp', 'ctx'), may hold values from -6 to 6
- pairing: int32 [8, 2], replicated, may hold values from 0 to 15, as said below
- attn_weight: bfloat16 [6, 768, 768], P(None, 'fsdp'), may hold values from -1 to 1
- out_weight: bfloat16 [2, 768, 768], P(None, 'fsdp'), may hold values from -1.75 to 1.75
- up_weight: bfloat16 [768, 3072], P('fsdp'), may hold values from -0.21875 to 0.21875
- down_weight: bfloat16 [3072, 768], P('fsdp'), may hold values from -0.109375 to 0.109375
- norm_gains: bfloat16 [3, 768], P(None, 'fsdp'), may hold values from 0.5 to 1.5
- bias_rows: bfloat16 [9, 768], P(None, 'fsdp'), may hold values from -2.5 to 2.5
- up_bias: bfloat16 [3072], P('fsdp'), may hold values from -2.5 to 2.5
- down_bias: bfloat16 [768], P('fsdp'), may hold values from -2.5 to 2.5
- out_cotangent: bfloat16 [8, 1024, 768], P('fsdp', 'ctx'), may hold values from -6 to 6
Outputs:
- layer_out: bfloat16 [8, 1024, 768], P('fsdp', 'ctx')
- grad_layer_in: float32 [8, 1024, 768], P('fsdp', 'ctx')
- grad_encoded: float32 [8, 1024, 768], P('fsdp', 'ctx')
- grad_attn_weight: float32 [6, 768, 768], P(None, 'fsdp')
- grad_out_weight: float32 [2, 768, 768], P(None, 'fsdp')
- grad_up_weight: float32 [768, 3072], P('fsdp')
- grad_down_weight: float32 [3072, 768], P('fsdp')
- grad_norm_gains: float32 [3, 768], P(None, 'fsdp')
- grad_bias_rows: float32 [9, 768], P(None, 'fsdp')
- grad_up_bias: float32 [3072], P('fsdp')
- grad_down_bias: float32 [768], P('fsdp')
The draws below stay inside these ranges and needn't reach their ends.
Inputs may be any that keep to these rules, and one draw needn't show every extreme that they name: `pairing`: row r lists two spans c and 15 - c; every span of 0 to 15 appears exactly once in the table.
All inputs are finite; a program needn't handle non-finite values.
Results may differ from the reference program's by a relative error of at most 0.02.
Values may be sent and summed in bfloat16 or wider, within the bound.
No kernel may reach another device: no remote copies, remote signals or barrier semaphores. Data moves between devices by JAX's collectives and lax.ppermute only.
A program may use at most 384 MiB of HBM per device.

```python
import jax
import jax.numpy as jnp
from jax import lax

D = 768
H = 12
HD = 64
FF = 3072
HALF = 64
ENC = 1024
SPANS = 16
SEQ = 1024
SEQS = 8


def draw_pairing(key, part):
    pair_count = SPANS // 2
    order = jax.random.permutation(key, pair_count).astype(jnp.int32)
    swaps = jax.random.randint(jax.random.fold_in(key, 11), (pair_count,), 0, 2).astype(jnp.int32)
    mirror = SPANS - 1 - order
    first_span = jnp.where(swaps == 1, mirror, order)
    second_span = jnp.where(swaps == 1, order, mirror)
    return jnp.stack([first_span, second_span], axis=1).astype(jnp.int32)


def clipped_normal(key, shape, scale):
    values = jax.random.normal(key, shape, jnp.float32)
    return jnp.clip(values, -6.0, 6.0) * scale


def draw_layer_in(key, part):
    key = jax.random.fold_in(key, 21)
    return clipped_normal(key, (SEQS, SEQ, D), 1.0).astype(jnp.bfloat16)


def draw_encoded(key, part):
    key = jax.random.fold_in(key, 22)
    return clipped_normal(key, (SEQS, ENC, D), 1.0).astype(jnp.bfloat16)


def draw_attn_weight(key, part):
    key = jax.random.fold_in(key, 23)
    return clipped_normal(key, (6, D, D), (D // 2) ** (-0.5)).astype(jnp.bfloat16)


def levels(rng, extent, split, smallest, high):
    def one(dim, shards_of):
        heights = jax.random.uniform(jax.random.fold_in(jax.random.fold_in(rng, 6), dim), (shards_of,), jnp.float32, smallest / len(split), high / len(split))
        return jnp.repeat(jnp.exp(heights), extent[dim] // shards_of).reshape((-1,) + (1,) * (len(extent) - dim - 1))

    level = one(*split[0])
    for cut in split[1:]:
        level = level * one(*cut)
    return level


def bell_draw(own_key, shape, deviation, reach, split=(), kind=jnp.bfloat16):
    array = jax.random.normal(own_key, shape, jnp.float32) * deviation
    if len(split) > 0:
        array = levels(own_key, shape, split, -0.22, 0.18) * array
    return jnp.clip(array, min=-reach, max=reach).astype(kind)


def setup_inputs(seed: int = 0) -> dict:
    splits = jax.random.split(jax.random.key(seed), 13)
    layer_in = draw_layer_in(jax.random.fold_in(splits[12], 71), 0)
    encoded = draw_encoded(jax.random.fold_in(splits[12], 71), 0)
    pairing = draw_pairing(jax.random.fold_in(splits[12], 71), 0)
    attn_weight = draw_attn_weight(jax.random.fold_in(splits[12], 71), 0)
    out_weight = bell_draw(splits[4], (2, D, D), (D // 64) ** -0.5, 1.75, ((1, 4),))
    up_weight = bell_draw(splits[5], (D, FF), D ** -0.5, 0.21875, ((0, 4),))
    down_weight = bell_draw(splits[6], (FF, D), FF ** -0.5, 0.109375, ((0, 4),))
    norm_gains = jnp.clip(1.0 + 0.1 * jax.random.normal(splits[7], (3, D), jnp.float32), 0.5, 1.5).astype(jnp.bfloat16)
    bias_rows = bell_draw(splits[8], (9, D), 0.3, 2.5, ((1, 4),))
    up_bias = bell_draw(splits[9], (FF,), 0.3, 2.5, ((0, 4),))
    down_bias = bell_draw(splits[10], (D,), 1.0, 2.5, ((0, 4),))
    out_cotangent = bell_draw(splits[11], (SEQS, SEQ, D), 1.0, 6.0, ((0, 4), (1, 8)))
    return dict(layer_in=layer_in, encoded=encoded, pairing=pairing, attn_weight=attn_weight, out_weight=out_weight, up_weight=up_weight, down_weight=down_weight, norm_gains=norm_gains, bias_rows=bias_rows, up_bias=up_bias, down_bias=down_bias, out_cotangent=out_cotangent)


@jax.custom_vjp
def low(v):
    return lax.optimization_barrier(v.astype(jnp.bfloat16)).astype(jnp.float32)

@jax.custom_vjp
def low_back(v):
    return v

def low_keep(v):
    return (low(v), None)

def low_pass(kept, grad):
    return (grad,)

def back_keep(v):
    return (v, None)

def back_low(kept, grad):
    return (low(grad),)
low.defvjp(low_keep, low_pass)
low_back.defvjp(back_keep, back_low)
SCORE_SCALE = 0.125
MASK_FILL = -1e+30
NORM_EPSILON = 1e-05
TOP_PRECISION = lax.Precision.HIGHEST

def layer_norm(values, gain, shift):
    center = values - lax.optimization_barrier(jnp.mean(values, axis=-1, keepdims=True))
    spread = lax.optimization_barrier(jnp.mean(center * center, axis=-1, keepdims=True))
    return center * lax.rsqrt(spread + NORM_EPSILON) * gain + shift

def matmul(left, right):
    return jnp.dot(left, right, precision=TOP_PRECISION)

def token_places(pairing, half_len):
    offsets = jnp.arange(half_len, dtype=jnp.int32)
    places = pairing[:, :, None] * half_len + offsets[None, None, :]
    return places.reshape(-1).astype(jnp.int32)

def attend(query, keys, values, query_places, key_places, masked):
    query_count = query.shape[0]
    block_size = min(1024, query_count)
    block_count = query_count // block_size
    key_heads = keys.reshape(keys.shape[0], H, HD)
    value_heads = values.reshape(values.shape[0], H, HD)

    def block_fn(block_item):
        query_block, place_block = block_item
        scores = low_back(jnp.einsum('qhd,khd->hqk', query_block, key_heads, precision=TOP_PRECISION) * SCORE_SCALE)
        if masked:
            allowed = key_places[None, None, :] <= place_block[None, :, None]
            scores = jnp.where(allowed, scores, MASK_FILL)
        log_mass = jax.nn.logsumexp(scores, axis=-1, keepdims=True)
        probs = low(jnp.exp(scores - log_mass))
        return jnp.einsum('hqk,khd->qhd', probs, value_heads, precision=TOP_PRECISION)
    blocks = (query.reshape(block_count, block_size, H, HD), query_places.reshape(block_count, block_size))
    mixed = lax.map(jax.checkpoint(block_fn), blocks)
    return mixed.reshape(query_count, H * HD)

def forward(layer_row, encoded_row, attn_weight, out_weight, up_weight, down_weight, norm_gains, bias_rows, up_bias, down_bias, places):
    normed_one = low(layer_norm(layer_row, norm_gains[0], bias_rows[6]))
    query = low(low_back(matmul(normed_one, attn_weight[0]) + bias_rows[0]))
    keys = low(low_back(matmul(normed_one, attn_weight[1])))
    values = low(low_back(matmul(normed_one, attn_weight[2]) + bias_rows[1]))
    mixed = low(low_back(attend(query, keys, values, places, places, True)))
    first_res = layer_row + low_back(matmul(mixed, out_weight[0]) + bias_rows[2])
    normed_two = low(layer_norm(first_res, norm_gains[1], bias_rows[7]))
    cross_query = low(low_back(matmul(normed_two, attn_weight[3]) + bias_rows[3]))
    cross_keys = low(low_back(matmul(encoded_row, attn_weight[4])))
    cross_values = low(low_back(matmul(encoded_row, attn_weight[5]) + bias_rows[4]))
    cross_places = jnp.zeros((encoded_row.shape[0],), jnp.int32)
    cross_mixed = low(low_back(attend(cross_query, cross_keys, cross_values, places, cross_places, False)))
    second_res = first_res + low_back(matmul(cross_mixed, out_weight[1]) + bias_rows[5])
    normed_three = low(layer_norm(second_res, norm_gains[2], bias_rows[8]))
    hidden_pre = low_back(matmul(normed_three, up_weight) + up_bias)
    hidden_act = low(jax.nn.gelu(hidden_pre, approximate=False))
    return second_res + matmul(hidden_act, down_weight) + down_bias

def reference(layer_in, encoded, pairing, attn_weight, out_weight, up_weight, down_weight, norm_gains, bias_rows, up_bias, down_bias, out_cotangent):
    places = token_places(pairing, HALF)

    def total(layer_float, encoded_float, attn_float, out_float, up_float, down_float, gain_float, bias_float, upb_float, downb_float):

        def one_sequence(running, seq_item):
            result = forward(seq_item[0], seq_item[1], attn_float, out_float, up_float, down_float, gain_float, bias_float, upb_float, downb_float, places)
            return (running, result)
        return lax.scan(one_sequence, jnp.zeros((), jnp.float32), (layer_float, encoded_float))[1]
    outputs, pullback = jax.vjp(total, layer_in.astype(jnp.float32), encoded.astype(jnp.float32), attn_weight.astype(jnp.float32), out_weight.astype(jnp.float32), up_weight.astype(jnp.float32), down_weight.astype(jnp.float32), norm_gains.astype(jnp.float32), bias_rows.astype(jnp.float32), up_bias.astype(jnp.float32), down_bias.astype(jnp.float32))
    grads = pullback(out_cotangent.astype(jnp.float32))
    return (outputs.astype(jnp.bfloat16), grads[0], grads[1], grads[2], grads[3], grads[4], grads[5], grads[6], grads[7], grads[8], grads[9])
```

```python
import functools
import math

import jax
import jax.numpy as jnp
from jax import lax
from jax.experimental import pallas as pl
from jax.experimental.pallas import tpu as pltpu
from jax.sharding import Mesh
from jax.sharding import PartitionSpec as P

HEADS = 12
HD = 64
PAIR = 2 * HD
SCORE_SCALE = 0.125
MASK_FILL = -1e30
NORM_EPSILON = 1e-05
LINE = 4
SWAP = [(0, 1), (1, 0)]
BF = jnp.bfloat16
F32 = jnp.float32
VMEM_LIMIT = 48 * 1024 * 1024


def dot(left, right):
    return jnp.dot(left, right, preferred_element_type=F32)


def dot_t(left, right):
    return lax.dot_general(left, right, (((1,), (1,)), ((), ())), preferred_element_type=F32)


def t_dot(left, right):
    return lax.dot_general(left, right, (((0,), (0,)), ((), ())), preferred_element_type=F32)


def split_heads(block):
    lane = lax.broadcasted_iota(jnp.int32, block.shape, 1)
    zero = jnp.zeros_like(block)
    return jnp.concatenate([jnp.where(lane < HD, block, zero), jnp.where(lane < HD, zero, block)], axis=0)


def join_heads(columns):
    rows = columns.shape[1] // 2
    return jnp.concatenate([columns[:HD, :rows], columns[HD:, rows:]], axis=0).T


def forward_kernel(masked, pieces, *refs):
    if masked:
        key_place_ref, query_place_ref, refs = refs[0], refs[1], refs[2:]
    query_ref, kv_refs = refs[0], refs[1 : 1 + pieces]
    out_ref, mass_ref, scores_ref = refs[1 + pieces :]
    query = split_heads(query_ref[...] * jnp.asarray(SCORE_SCALE, BF))
    piece = kv_refs[0].shape[1]
    if masked:
        query_place = query_place_ref[...]
        query_place = jnp.concatenate([query_place, query_place], axis=1)
    top = None
    for i in range(pieces):
        scores = dot_t(kv_refs[i][0], query)
        if masked:
            scores = jnp.where(key_place_ref[pl.ds(i * piece, piece), :] <= query_place, scores, MASK_FILL)
        scores_ref[pl.ds(i * piece, piece), :] = scores
        high = jnp.max(scores, axis=0, keepdims=True)
        top = high if top is None else jnp.maximum(top, high)
    mass = jnp.zeros_like(top)
    mixed = None
    for i in range(pieces):
        probs = jnp.exp(scores_ref[pl.ds(i * piece, piece), :] - top)
        mass = mass + jnp.sum(probs, axis=0, keepdims=True)
        part = t_dot(kv_refs[i][1], probs.astype(BF))
        mixed = part if mixed is None else mixed + part
    out_ref[...] = join_heads(mixed * (1.0 / mass)).astype(BF)
    mass_ref[0] = top + jnp.log(mass)


def backward_kernel(masked, pieces, *refs):
    if masked:
        key_place_ref, query_place_ref, refs = refs[0], refs[1], refs[2:]
    query_ref, dout_ref, out_ref, mass_ref = refs[:4]
    kv_refs = refs[4 : 4 + pieces]
    dquery_ref = refs[4 + pieces]
    dkv_refs = refs[5 + pieces :]
    query = split_heads(query_ref[...] * jnp.asarray(SCORE_SCALE, BF))
    dout = dout_ref[...]
    prod = (dout.astype(F32) * out_ref[...].astype(F32)).T
    delta = jnp.concatenate(
        [jnp.sum(prod[:HD], axis=0, keepdims=True), jnp.sum(prod[HD:], axis=0, keepdims=True)], axis=1
    )
    dout = split_heads(dout)
    log_mass = mass_ref[0]
    piece = kv_refs[0].shape[1]
    if masked:
        query_place = query_place_ref[...]
        query_place = jnp.concatenate([query_place, query_place], axis=1)
    dquery = None
    for i in range(pieces):
        keys = kv_refs[i][0]
        scores = dot_t(keys, query)
        if masked:
            scores = jnp.where(key_place_ref[pl.ds(i * piece, piece), :] <= query_place, scores, MASK_FILL)
        probs = jnp.exp(scores - log_mass)
        dprobs = dot_t(kv_refs[i][1], dout)
        dscores = (probs * (dprobs - delta)).astype(BF)
        dkv_refs[i][0] = dot(dscores, query).astype(BF)
        dkv_refs[i][1] = dot(probs.astype(BF), dout).astype(BF)
        part = t_dot(keys, dscores)
        dquery = part if dquery is None else dquery + part
    dquery_ref[...] = (join_heads(dquery) * SCORE_SCALE).astype(BF)


def place_specs(masked, places):
    if not masked:
        return [], []
    key_places, query_places = places
    return [key_places, query_places], [
        pl.BlockSpec(key_places.shape, lambda h: (0, 0)),
        pl.BlockSpec(query_places.shape, lambda h: (0, 0)),
    ]


def attention(query, kv, places):
    masked = places is not None
    rows, width = query.shape
    piece = kv[0].shape[1]
    extra, extra_specs = place_specs(masked, places)
    keys = piece * len(kv)
    return pl.pallas_call(
        functools.partial(forward_kernel, masked, len(kv)),
        grid=(width // PAIR,),
        in_specs=extra_specs
        + [pl.BlockSpec((rows, PAIR), lambda h: (0, h))]
        + [pl.BlockSpec((2, piece, PAIR), lambda h: (0, 0, h))] * len(kv),
        out_specs=[
            pl.BlockSpec((rows, PAIR), lambda h: (0, h)),
            pl.BlockSpec((1, 1, 2 * rows), lambda h: (h, 0, 0)),
        ],
        out_shape=[
            jax.ShapeDtypeStruct((rows, width), BF),
            jax.ShapeDtypeStruct((width // PAIR, 1, 2 * rows), F32),
        ],
        scratch_shapes=[pltpu.VMEM((keys, 2 * rows), F32)],
        compiler_params=pltpu.CompilerParams(vmem_limit_bytes=VMEM_LIMIT),
        cost_estimate=pl.CostEstimate(
            flops=4 * rows * keys * width * 2,
            bytes_accessed=4 * keys * width,
            transcendentals=rows * keys * HEADS,
        ),
    )(*extra, query, *kv)


def attention_back(query, dout, out, mass, kv, places):
    masked = places is not None
    rows, width = query.shape
    piece = kv[0].shape[1]
    extra, extra_specs = place_specs(masked, places)
    keys = piece * len(kv)
    column = pl.BlockSpec((rows, PAIR), lambda h: (0, h))
    pair = pl.BlockSpec((2, piece, PAIR), lambda h: (0, 0, h))
    res = pl.pallas_call(
        functools.partial(backward_kernel, masked, len(kv)),
        grid=(width // PAIR,),
        in_specs=extra_specs
        + [column, column, column, pl.BlockSpec((1, 1, 2 * rows), lambda h: (h, 0, 0))]
        + [pair] * len(kv),
        out_specs=[column] + [pair] * len(kv),
        out_shape=[jax.ShapeDtypeStruct((rows, width), BF)]
        + [jax.ShapeDtypeStruct((2, piece, width), BF)] * len(kv),
        compiler_params=pltpu.CompilerParams(vmem_limit_bytes=VMEM_LIMIT),
        cost_estimate=pl.CostEstimate(
            flops=10 * rows * keys * width * 2,
            bytes_accessed=8 * keys * width,
            transcendentals=rows * keys * HEADS,
        ),
    )(*extra, query, dout, out, mass, *kv)
    return res[0], list(res[1:])


def deal_perms():
    perms = []
    for r in range(LINE):
        perm = []
        for c in range(2):
            for z in range(LINE):
                k = (r - z) % LINE
                perm.append((c * LINE + z, (k % 2) * LINE + 2 * c + k // 2))
        perms.append(perm)
    return perms


DEAL = deal_perms()


def deal(array):
    rows = array.shape[1]
    chunks = array.reshape(LINE, rows // 2, array.shape[2])
    z = lax.axis_index("z")
    got = []
    for r in range(LINE):
        chunk = lax.dynamic_index_in_dim(chunks, lax.rem(r - z + LINE, LINE), keepdims=False)
        got.append(lax.ppermute(chunk, ("core", "z"), DEAL[r]))
    return jnp.concatenate(got, axis=0)


def undeal(array):
    half = array.shape[0] // LINE
    got = []
    for r in range(LINE):
        got.append(
            lax.ppermute(array[r * half : (r + 1) * half], ("core", "z"), [(b, a) for a, b in DEAL[r]])
        )
    both = jnp.stack(got + got)
    mine = lax.dynamic_slice_in_dim(both, lax.axis_index("z"), LINE, axis=0)
    return mine.reshape(2, 2 * half, array.shape[1])


def group_perm(groups, step):
    return [(i, (i + step) % groups) for i in range(groups)]


def spread(own, groups):
    got = []
    for step in range(groups):
        block = own if step == 0 else lax.ppermute(own, ("o", "y"), group_perm(groups, step))
        got.append(block)
    pieces = []
    for block in got:
        pieces.append(block)
        pieces.append(lax.ppermute(block, "core", SWAP))
    return pieces


def collect(pieces, groups):
    sums = []
    for step in range(groups):
        other = lax.ppermute(pieces[2 * step + 1], "core", SWAP)
        sums.append(pieces[2 * step].astype(F32) + other.astype(F32))
    total = sums[0]
    for step in range(1, groups):
        back = [(b, a) for a, b in group_perm(groups, step)]
        total = total + lax.ppermute(sums[step].astype(BF), ("o", "y"), back).astype(F32)
    return total


def assemble(own, other, axis):
    near = lax.ppermute(own, "core", SWAP)
    far = lax.ppermute(other, "core", SWAP)
    fx, core = lax.axis_index("fx"), lax.axis_index("core")
    shape = list(own.shape)
    step = shape[axis]
    shape[axis] *= 4
    full = jnp.zeros(shape, own.dtype)
    for block, place in (
        (own, 2 * fx + core),
        (near, 2 * fx + 1 - core),
        (other, 2 - 2 * fx + core),
        (far, 3 - 2 * fx - core),
    ):
        full = lax.dynamic_update_slice_in_dim(full, block, place * step, axis)
    return full


def after(value, earlier):
    return lax.optimization_barrier((value, earlier))[0]


def reduce_units(units):
    n, rows, width = units.shape
    shard = rows // 4
    fx, core = lax.axis_index("fx"), lax.axis_index("core")
    y = lax.axis_index("y")
    split = units.reshape(n, 2, 2, shard, width)
    theirs = lax.dynamic_index_in_dim(split, 1 - core, axis=2, keepdims=False)
    mine = lax.dynamic_index_in_dim(split, core, axis=2, keepdims=False)
    mine = (mine.astype(F32) + lax.ppermute(theirs, "core", SWAP).astype(F32)).astype(BF)
    theirs = lax.dynamic_index_in_dim(mine, 1 - fx, axis=1, keepdims=False)
    mine = lax.dynamic_index_in_dim(mine, fx, axis=1, keepdims=False)
    mine = (mine.astype(F32) + lax.ppermute(theirs, "fx", SWAP).astype(F32)).astype(BF)
    if lax.axis_size("o") > 1:
        return lax.psum(mine, ("o", "z", "y")).astype(F32)
    lines = mine.reshape(2, LINE, n * shard // (2 * LINE), width)
    theirs = lax.dynamic_index_in_dim(lines, 1 - y, axis=0, keepdims=False)
    mine = lax.dynamic_index_in_dim(lines, y, axis=0, keepdims=False)
    mine = (mine.astype(F32) + lax.ppermute(theirs, "y", SWAP).astype(F32)).astype(BF)
    parts = lax.all_to_all(mine, "z", 0, 0, tiled=True)
    total = jnp.sum(parts.astype(F32), axis=0, keepdims=True).astype(BF)
    line = lax.all_to_all(jnp.broadcast_to(total, (LINE,) + total.shape[1:]), "z", 0, 0, tiled=True)
    other = lax.ppermute(line, "y", SWAP)
    low = jnp.where(y == 0, line, other)
    high = jnp.where(y == 0, other, line)
    return jnp.concatenate([low, high], axis=0).astype(F32).reshape(n, shard, width)


def standard(values):
    center = values - jnp.mean(values, axis=-1, keepdims=True)
    inverse = lax.rsqrt(jnp.mean(center * center, axis=-1, keepdims=True) + NORM_EPSILON)
    return center * inverse, inverse


def norm_back(dnormed, values, gain):
    z, inverse = standard(values)
    a = dnormed * gain
    dvalues = (
        a - jnp.mean(a, axis=-1, keepdims=True) - z * jnp.mean(a * z, axis=-1, keepdims=True)
    ) * inverse
    return dvalues, jnp.sum(dnormed * z, axis=0), jnp.sum(dnormed, axis=0)


def column_sum(values):
    return jnp.sum(values.astype(F32), axis=0)


def gelu_exact(values):
    return jax.nn.gelu(values, approximate=False)


def per_device(
    layer_in,
    encoded,
    pairing,
    attn_weight,
    out_weight,
    up_weight,
    down_weight,
    norm_gains,
    bias_rows,
    up_bias,
    down_bias,
    out_cotangent,
):
    seqs, local_rows, width = layer_in.shape
    outer = lax.axis_size("o")
    groups = outer * 2
    half = local_rows // 2
    shard = attn_weight.shape[1]
    hidden = up_weight.shape[1]
    blocks = hidden // width

    vectors = jnp.concatenate(
        [norm_gains, bias_rows, up_bias.reshape(blocks, shard), down_bias.reshape(1, shard)], axis=0
    )
    x_bf = deal(layer_in)
    vec_other = lax.ppermute(vectors, "fx", SWAP)
    qkv_shard = attn_weight[:3]
    qkv_other = lax.ppermute(after(qkv_shard, vec_other), "fx", SWAP)
    enc_bf = deal(encoded)
    mid_shard = jnp.concatenate([attn_weight[3:], out_weight], axis=0)
    mid_other = lax.ppermute(after(mid_shard, qkv_other), "fx", SWAP)
    up_other = lax.ppermute(after(up_weight, mid_other), "fx", SWAP)
    down_other = lax.ppermute(after(down_weight, up_other), "fx", SWAP)
    cot = deal(out_cotangent)

    vec = assemble(vectors[None], vec_other[None], 0).astype(F32)
    flat = vec[:, : 3 + 9].transpose(1, 0, 2).reshape(12, width)
    gain, bias = flat[:3], flat[3:]
    up_b = vec[:, 12 : 12 + blocks].reshape(1, hidden)
    down_b = vec[:, 12 + blocks].reshape(1, width)

    z, y, o, core = (lax.axis_index(a) for a in ("z", "y", "o", "core"))
    group = o * 2 + y
    spots = []
    for step in range(groups):
        source = lax.rem(group - step + groups, groups)
        for flip in range(2):
            c = core if flip == 0 else 1 - core
            k = 2 * lax.rem(z, 2) + c
            for r in range(LINE):
                line = lax.rem(r - k + LINE, LINE)
                spots.append((((source // 2) * LINE + line) * 2 + lax.rem(source, 2)) * 2 + c)
    spans = jnp.take(pairing.reshape(-1), jnp.stack(spots), axis=0)
    key_places = (spans[:, None] * half + jnp.arange(half, dtype=jnp.int32)[None, :]).reshape(-1, 1)
    query_places = key_places[: LINE * half].reshape(1, -1)
    places = (key_places, query_places)

    x = x_bf.astype(F32)
    n1 = (standard(x)[0] * gain[0] + bias[6]).astype(BF)
    w_qkv = assemble(qkv_shard, qkv_other, 1)
    key = dot(n1, w_qkv[1]).astype(BF)
    value = (dot(n1, w_qkv[2]) + bias[1]).astype(BF)
    kv_self = spread(jnp.stack([key, value]), groups)
    query = (dot(n1, w_qkv[0]) + bias[0]).astype(BF)

    w_mid = assemble(mid_shard, mid_other, 1)
    ckey = dot(enc_bf, w_mid[1]).astype(BF)
    cvalue = (dot(enc_bf, w_mid[2]) + bias[4]).astype(BF)
    kv_cross = spread(jnp.stack([ckey, cvalue]), groups)

    mixed, mass = attention(query, kv_self, places)
    r1 = x + dot(mixed, w_mid[3]) + bias[2]
    n2 = (standard(r1)[0] * gain[1] + bias[7]).astype(BF)
    cquery = (dot(n2, w_mid[0]) + bias[3]).astype(BF)
    cmixed, cmass = attention(cquery, kv_cross, None)
    r2 = r1 + dot(cmixed, w_mid[4]) + bias[5]
    n3 = (standard(r2)[0] * gain[2] + bias[8]).astype(BF)

    w_up = assemble(up_weight, up_other, 0)
    w_down = assemble(down_weight, down_other, 0)
    pre = dot(n3, w_up) + up_b
    act, gelu_back = jax.vjp(gelu_exact, pre)
    act = act.astype(BF)
    layer_out = undeal((r2 + dot(act, w_down) + down_b).astype(BF))
    dact = dot_t(cot, w_down)
    dpre = gelu_back(dact)[0].astype(BF)
    g_down = t_dot(act, cot).astype(BF)
    g_up = [t_dot(n3, dpre[:, b * width : (b + 1) * width]).astype(BF) for b in range(blocks)]
    g_down = g_down.reshape(4, blocks, shard, width).transpose(1, 0, 2, 3).reshape(blocks, width, width)
    ffn = reduce_units(jnp.concatenate([jnp.stack(g_up), g_down], axis=0))
    dn3 = dot_t(dpre, w_up)
    back3, dgain3, dshift3 = norm_back(dn3, r2, gain[2])
    dr2 = cot.astype(F32) + back3

    gc = dr2.astype(BF)
    doc = dot_t(gc, w_mid[4]).astype(BF)
    dcq, dckv = attention_back(cquery, doc, cmixed, cmass, kv_cross, None)
    dckv = collect(dckv, groups).astype(BF)
    dn2 = dot_t(dcq, w_mid[0])
    back2, dgain2, dshift2 = norm_back(dn2, r1, gain[1])
    dr1 = dr2 + back2
    gs = dr1.astype(BF)
    dos = dot_t(gs, w_mid[3]).astype(BF)
    dq, dkv = attention_back(query, dos, mixed, mass, kv_self, places)
    grad_encoded = undeal((dot_t(dckv[0], w_mid[1]) + dot_t(dckv[1], w_mid[2])).astype(BF))
    cross = reduce_units(
        jnp.stack(
            [
                t_dot(n2, dcq).astype(BF),
                t_dot(enc_bf, dckv[0]).astype(BF),
                t_dot(enc_bf, dckv[1]).astype(BF),
                t_dot(cmixed, gc).astype(BF),
            ]
        )
    )
    dkv = collect(dkv, groups).astype(BF)
    own = reduce_units(
        jnp.stack(
            [
                t_dot(n1, dq).astype(BF),
                t_dot(n1, dkv[0]).astype(BF),
                t_dot(n1, dkv[1]).astype(BF),
                t_dot(mixed, gs).astype(BF),
            ]
        )
    )
    dn1 = dot_t(dq, w_qkv[0]) + dot_t(dkv[0], w_qkv[1]) + dot_t(dkv[1], w_qkv[2])
    back1, dgain1, dshift1 = norm_back(dn1, x, gain[0])
    grad_layer = undeal((dr1 + back1).astype(BF))

    rows = jnp.concatenate(
        [
            jnp.stack(
                [
                    dgain1,
                    dgain2,
                    dgain3,
                    column_sum(dq),
                    column_sum(dkv[1]),
                    column_sum(gs),
                    column_sum(dcq),
                    column_sum(dckv[1]),
                    column_sum(gc),
                    dshift1,
                    dshift2,
                    dshift3,
                ]
            ),
            column_sum(dpre).reshape(blocks, width),
            column_sum(cot).reshape(1, width),
        ],
        axis=0,
    )
    rows = lax.psum(rows, ("fx", "core", "o", "z", "y"))
    me = 2 * lax.axis_index("fx") + core
    by_shard = rows.reshape(rows.shape[0], 4, shard)
    mine = lax.dynamic_index_in_dim(by_shard, me, axis=1, keepdims=False)
    grad_up_bias = lax.dynamic_index_in_dim(
        rows[12 : 12 + blocks].reshape(4, hidden // 4), me, axis=0, keepdims=False
    )
    return (
        layer_out,
        grad_layer.astype(F32),
        grad_encoded.astype(F32),
        jnp.concatenate([own[:3], cross[:3]], axis=0),
        jnp.concatenate([own[3:], cross[3:]], axis=0),
        jnp.concatenate([ffn[b] for b in range(blocks)], axis=1),
        ffn[blocks:].reshape(blocks * shard, width),
        mine[:3],
        mine[3:12],
        grad_up_bias,
        mine[12 + blocks],
    )


def solution(mesh):
    ctx = mesh.shape["ctx"]
    grid = Mesh(mesh.devices.reshape(2, 2, ctx // (2 * LINE), LINE, 2), ("fx", "core", "o", "z", "y"))
    fsdp = ("fx", "core")
    rows = P(fsdp, ("o", "z", "y"), None)
    weights = (
        P(None, fsdp, None),
        P(None, fsdp, None),
        P(fsdp, None),
        P(fsdp, None),
        P(None, fsdp),
        P(None, fsdp),
        P(fsdp),
        P(fsdp),
    )
    return jax.shard_map(
        per_device,
        mesh=grid,
        in_specs=(rows, rows, P()) + weights + (rows,),
        out_specs=(rows, rows, rows) + weights,
        check_vma=False,
    )
```

```python
import functools
import math

import jax
import jax.numpy as jnp
from jax import lax
from jax.experimental import pallas as pl
from jax.experimental.pallas import tpu as pltpu
from jax.sharding import Mesh
from jax.sharding import PartitionSpec as P

HEADS = 12
HD = 64
PAIR = 2 * HD
SCORE_SCALE = 0.125
MASK_FILL = -1e30
NORM_EPSILON = 1e-05
LINE = 4
SWAP = [(0, 1), (1, 0)]
BF = jnp.bfloat16
F32 = jnp.float32
VMEM_LIMIT = 48 * 1024 * 1024


def dot(left, right):
    return jnp.dot(left, right, preferred_element_type=F32)


def dot_t(left, right):
    return lax.dot_general(left, right, (((1,), (1,)), ((), ())), preferred_element_type=F32)


def t_dot(left, right):
    return lax.dot_general(left, right, (((0,), (0,)), ((), ())), preferred_element_type=F32)


def split_heads(block):
    lane = lax.broadcasted_iota(jnp.int32, block.shape, 1)
    zero = jnp.zeros_like(block)
    return jnp.concatenate([jnp.where(lane < HD, block, zero), jnp.where(lane < HD, zero, block)], axis=0)


def join_heads(columns):
    rows = columns.shape[1] // 2
    return jnp.concatenate([columns[:HD, :rows], columns[HD:, rows:]], axis=0).T


def forward_kernel(masked, pieces, *refs):
    if masked:
        key_place_ref, query_place_ref, refs = refs[0], refs[1], refs[2:]
    query_ref, kv_refs = refs[0], refs[1 : 1 + pieces]
    out_ref, mass_ref, scores_ref = refs[1 + pieces :]
    query = split_heads(query_ref[...] * jnp.asarray(SCORE_SCALE, BF))
    piece = kv_refs[0].shape[1]
    if masked:
        query_place = query_place_ref[...]
        query_place = jnp.concatenate([query_place, query_place], axis=1)
    top = None
    for i in range(pieces):
        scores = dot_t(kv_refs[i][0], query)
        if masked:
            scores = jnp.where(key_place_ref[pl.ds(i * piece, piece), :] <= query_place, scores, MASK_FILL)
        scores_ref[pl.ds(i * piece, piece), :] = scores
        high = jnp.max(scores, axis=0, keepdims=True)
        top = high if top is None else jnp.maximum(top, high)
    mass = jnp.zeros_like(top)
    mixed = None
    for i in range(pieces):
        probs = jnp.exp(scores_ref[pl.ds(i * piece, piece), :] - top)
        mass = mass + jnp.sum(probs, axis=0, keepdims=True)
        part = t_dot(kv_refs[i][1], probs.astype(BF))
        mixed = part if mixed is None else mixed + part
    out_ref[...] = join_heads(mixed * (1.0 / mass)).astype(BF)
    mass_ref[0] = top + jnp.log(mass)


def backward_kernel(masked, pieces, *refs):
    if masked:
        key_place_ref, query_place_ref, refs = refs[0], refs[1], refs[2:]
    query_ref, dout_ref, out_ref, mass_ref = refs[:4]
    kv_refs = refs[4 : 4 + pieces]
    dquery_ref, mine_ref, theirs_ref = refs[4 + pieces :]
    query = split_heads(query_ref[...] * jnp.asarray(SCORE_SCALE, BF))
    dout = dout_ref[...]
    prod = (dout.astype(F32) * out_ref[...].astype(F32)).T
    delta = jnp.concatenate(
        [jnp.sum(prod[:HD], axis=0, keepdims=True), jnp.sum(prod[HD:], axis=0, keepdims=True)], axis=1
    )
    dout = split_heads(dout)
    log_mass = mass_ref[0]
    piece = kv_refs[0].shape[1]
    if masked:
        query_place = query_place_ref[...]
        query_place = jnp.concatenate([query_place, query_place], axis=1)
    dquery = None
    for i in range(pieces):
        keys = kv_refs[i][0]
        scores = dot_t(keys, query)
        if masked:
            scores = jnp.where(key_place_ref[pl.ds(i * piece, piece), :] <= query_place, scores, MASK_FILL)
        probs = jnp.exp(scores - log_mass)
        dprobs = dot_t(kv_refs[i][1], dout)
        dscores = (probs * (dprobs - delta)).astype(BF)
        dkv_ref = theirs_ref if i % 2 else mine_ref
        dkv_ref[i // 2, 0] = dot(dscores, query).astype(BF)
        dkv_ref[i // 2, 1] = dot(probs.astype(BF), dout).astype(BF)
        part = t_dot(keys, dscores)
        dquery = part if dquery is None else dquery + part
    dquery_ref[...] = (join_heads(dquery) * SCORE_SCALE).astype(BF)


def place_specs(masked, places):
    if not masked:
        return [], []
    key_places, query_places = places
    return [key_places, query_places], [
        pl.BlockSpec(key_places.shape, lambda h: (0, 0)),
        pl.BlockSpec(query_places.shape, lambda h: (0, 0)),
    ]


def attention(query, kv, places):
    masked = places is not None
    rows, width = query.shape
    piece = kv[0].shape[1]
    extra, extra_specs = place_specs(masked, places)
    keys = piece * len(kv)
    return pl.pallas_call(
        functools.partial(forward_kernel, masked, len(kv)),
        grid=(width // PAIR,),
        in_specs=extra_specs
        + [pl.BlockSpec((rows, PAIR), lambda h: (0, h))]
        + [pl.BlockSpec((2, piece, PAIR), lambda h: (0, 0, h))] * len(kv),
        out_specs=[
            pl.BlockSpec((rows, PAIR), lambda h: (0, h)),
            pl.BlockSpec((1, 1, 2 * rows), lambda h: (h, 0, 0)),
        ],
        out_shape=[
            jax.ShapeDtypeStruct((rows, width), BF),
            jax.ShapeDtypeStruct((width // PAIR, 1, 2 * rows), F32),
        ],
        scratch_shapes=[pltpu.VMEM((keys, 2 * rows), F32)],
        compiler_params=pltpu.CompilerParams(vmem_limit_bytes=VMEM_LIMIT),
        cost_estimate=pl.CostEstimate(
            flops=4 * rows * keys * width * 2,
            bytes_accessed=4 * keys * width,
            transcendentals=rows * keys * HEADS,
        ),
    )(*extra, query, *kv)


def attention_back(query, dout, out, mass, kv, places):
    masked = places is not None
    rows, width = query.shape
    piece = kv[0].shape[1]
    extra, extra_specs = place_specs(masked, places)
    keys = piece * len(kv)
    column = pl.BlockSpec((rows, PAIR), lambda h: (0, h))
    pair = pl.BlockSpec((2, piece, PAIR), lambda h: (0, 0, h))
    groups = len(kv) // 2
    blocks = pl.BlockSpec((groups, 2, piece, PAIR), lambda h: (0, 0, 0, h))
    return pl.pallas_call(
        functools.partial(backward_kernel, masked, len(kv)),
        grid=(width // PAIR,),
        in_specs=extra_specs
        + [column, column, column, pl.BlockSpec((1, 1, 2 * rows), lambda h: (h, 0, 0))]
        + [pair] * len(kv),
        out_specs=[column, blocks, blocks],
        out_shape=[jax.ShapeDtypeStruct((rows, width), BF)]
        + [jax.ShapeDtypeStruct((groups, 2, piece, width), BF)] * 2,
        compiler_params=pltpu.CompilerParams(vmem_limit_bytes=VMEM_LIMIT),
        cost_estimate=pl.CostEstimate(
            flops=10 * rows * keys * width * 2,
            bytes_accessed=8 * keys * width,
            transcendentals=rows * keys * HEADS,
        ),
    )(*extra, query, dout, out, mass, *kv)


def deal(array):
    lead = array.shape[:-3]
    _, rows, width = array.shape[-3:]
    core = lax.axis_index("core")
    parts = array.reshape(lead + (2, 2, rows // 2, width))
    axis = len(lead) + 1
    mine = lax.dynamic_index_in_dim(parts, core, axis, keepdims=False)
    theirs = lax.dynamic_index_in_dim(parts, 1 - core, axis, keepdims=False)
    got = lax.ppermute(theirs, "core", SWAP)
    low, high = jnp.where(core == 0, mine, got), jnp.where(core == 0, got, mine)
    chunks = jnp.concatenate([low, high], axis=len(lead))
    out = lax.all_to_all(chunks, "z", len(lead), len(lead), tiled=True)
    return out.reshape(lead + (2 * rows, width))


def undeal(array):
    lead = array.shape[:-2]
    rows, width = array.shape[-2] // 2, array.shape[-1]
    core = lax.axis_index("core")
    axis = len(lead)
    chunks = lax.all_to_all(
        array.reshape(lead + (LINE, rows // 2, width)), "z", axis, axis, tiled=True
    ).reshape(lead + (2, 2, rows // 2, width))
    mine = lax.dynamic_index_in_dim(chunks, core, axis, keepdims=False)
    theirs = lax.dynamic_index_in_dim(chunks, 1 - core, axis, keepdims=False)
    got = lax.ppermute(theirs, "core", SWAP)
    low, high = jnp.where(core == 0, mine, got), jnp.where(core == 0, got, mine)
    return jnp.stack([low, high], axis=axis + 1).reshape(lead + (2, rows, width))


def group_perm(groups, step):
    return [(i, (i + step) % groups) for i in range(groups)]


def spread(own, groups):
    got = []
    for step in range(groups):
        block = own if step == 0 else lax.ppermute(own, ("o", "y"), group_perm(groups, step))
        got.append(block)
    pieces = []
    for block in got:
        pieces.append(block)
        pieces.append(lax.ppermute(block, "core", SWAP))
    return pieces


def collect(mine, theirs, groups):
    got = lax.ppermute(theirs, "core", SWAP)
    sums = mine.astype(F32) + got.astype(F32)
    total = sums[0]
    for step in range(1, groups):
        back = [(b, a) for a, b in group_perm(groups, step)]
        total = total + lax.ppermute(sums[step].astype(BF), ("o", "y"), back).astype(F32)
    return total


def assemble(own, other, axis):
    near = lax.ppermute(own, "core", SWAP)
    far = lax.ppermute(other, "core", SWAP)
    fx, core = lax.axis_index("fx"), lax.axis_index("core")
    shape = list(own.shape)
    step = shape[axis]
    shape[axis] *= 4
    full = jnp.zeros(shape, own.dtype)
    for block, place in (
        (own, 2 * fx + core),
        (near, 2 * fx + 1 - core),
        (other, 2 - 2 * fx + core),
        (far, 3 - 2 * fx - core),
    ):
        full = lax.dynamic_update_slice_in_dim(full, block, place * step, axis)
    return full


def after(value, earlier):
    return lax.optimization_barrier((value, earlier))[0]


def both(mine, theirs, axis):
    return (mine.astype(F32) + lax.ppermute(theirs, axis, SWAP).astype(F32)).astype(BF)


def split_of(array, axis, name):
    i = lax.axis_index(name)
    mine = lax.dynamic_index_in_dim(array, i, axis=axis, keepdims=False)
    theirs = lax.dynamic_index_in_dim(array, 1 - i, axis=axis, keepdims=False)
    return mine, theirs


def over_cores(units):
    n, rows, width = units.shape
    return both(*split_of(units.reshape(n, 2, 2, rows // 4, width), 2, "core"), "core")


def over_x(sums):
    return both(*split_of(sums, 1, "fx"), "fx")


def over_y(sums):
    n, shard, width = sums.shape
    return both(*split_of(sums.reshape(2, LINE, n * shard // (2 * LINE), width), 0, "y"), "y")


def over_z(sums):
    parts = lax.all_to_all(sums, "z", 0, 0, tiled=True)
    return jnp.sum(parts.astype(F32), axis=0, keepdims=True).astype(BF)


def back_z(total):
    return lax.all_to_all(jnp.broadcast_to(total, (LINE,) + total.shape[1:]), "z", 0, 0, tiled=True)


def back_y(line, shape):
    other = lax.ppermute(line, "y", SWAP)
    y = lax.axis_index("y")
    low = jnp.where(y == 0, line, other)
    high = jnp.where(y == 0, other, line)
    return jnp.concatenate([low, high], axis=0).astype(F32).reshape(shape)


def over_ctx(sums):
    if lax.axis_size("o") > 1:
        return lax.psum(sums, ("o", "z", "y")).astype(F32)
    return back_y(back_z(over_z(over_y(sums))), sums.shape)


def sum_vectors(rows):
    count, width = rows.shape
    n_ctx = lax.axis_size("o") * 2 * LINE
    shard = width // 4
    size = count * shard
    lines = -(-size // (16 * 128)) * 16
    cut = rows.reshape(count, 4, shard).transpose(1, 0, 2).reshape(4, size)
    cut = jnp.pad(cut, ((0, 0), (0, lines * 128 - size))).reshape(4, 1, lines, 128).astype(BF)
    cut = jnp.broadcast_to(cut, (4, n_ctx, lines, 128)).reshape(4 * n_ctx, lines, 128)
    got = lax.all_to_all(cut, ("fx", "core", "o", "z", "y"), 0, 0, tiled=True)
    total = jnp.sum(got.astype(F32), axis=0)
    return total.reshape(-1)[:size].reshape(count, shard)


def standard(values):
    center = values - jnp.mean(values, axis=-1, keepdims=True)
    inverse = lax.rsqrt(jnp.mean(center * center, axis=-1, keepdims=True) + NORM_EPSILON)
    return center * inverse, inverse


def norm_back(dnormed, values, gain):
    z, inverse = standard(values)
    a = dnormed * gain
    dvalues = (
        a - jnp.mean(a, axis=-1, keepdims=True) - z * jnp.mean(a * z, axis=-1, keepdims=True)
    ) * inverse
    return dvalues, jnp.sum(dnormed * z, axis=0), jnp.sum(dnormed, axis=0)


def column_sum(values):
    return jnp.sum(values.astype(F32), axis=0)


def gelu_exact(values):
    return jax.nn.gelu(values, approximate=False)


def per_device(
    layer_in,
    encoded,
    pairing,
    attn_weight,
    out_weight,
    up_weight,
    down_weight,
    norm_gains,
    bias_rows,
    up_bias,
    down_bias,
    out_cotangent,
):
    seqs, local_rows, width = layer_in.shape
    outer = lax.axis_size("o")
    groups = outer * 2
    half = local_rows // 2
    shard = attn_weight.shape[1]
    hidden = up_weight.shape[1]
    blocks = hidden // width

    vectors = jnp.concatenate(
        [norm_gains, bias_rows, up_bias.reshape(blocks, shard), down_bias.reshape(1, shard)], axis=0
    )
    x_bf = deal(layer_in)
    vec = lax.all_to_all(jnp.stack([vectors] * 4), ("fx", "core"), 0, 0, tiled=True).astype(F32)
    qkv_shard = attn_weight[:3]
    qkv_other = lax.ppermute(qkv_shard, "fx", SWAP)
    mid_shard = jnp.concatenate([attn_weight[3:], out_weight], axis=0)
    mid_other = lax.ppermute(after(mid_shard, qkv_other), "fx", SWAP)
    up_other = lax.ppermute(after(up_weight, mid_other), "fx", SWAP)
    down_other = lax.ppermute(after(down_weight, up_other), "fx", SWAP)
    enc_cot = deal(after(jnp.stack([encoded, out_cotangent]), x_bf)) if encoded.shape == layer_in.shape else None
    enc_bf = deal(encoded) if enc_cot is None else enc_cot[0]
    cot = deal(out_cotangent) if enc_cot is None else enc_cot[1]

    flat = vec[:, : 3 + 9].transpose(1, 0, 2).reshape(12, width)
    gain, bias = flat[:3], flat[3:]
    up_b = vec[:, 12 : 12 + blocks].reshape(1, hidden)
    down_b = vec[:, 12 + blocks].reshape(1, width)

    y, o, core = (lax.axis_index(a) for a in ("y", "o", "core"))
    group = o * 2 + y
    spots = []
    for step in range(groups):
        source = lax.rem(group - step + groups, groups)
        for flip in range(2):
            c = core if flip == 0 else 1 - core
            for line in range(LINE):
                spots.append((((source // 2) * LINE + line) * 2 + lax.rem(source, 2)) * 2 + c)
    spans = jnp.take(pairing.reshape(-1), jnp.stack(spots), axis=0)
    key_places = (spans[:, None] * half + jnp.arange(half, dtype=jnp.int32)[None, :]).reshape(-1, 1)
    query_places = key_places[: LINE * half].reshape(1, -1)
    places = (key_places, query_places)

    x = x_bf.astype(F32)
    n1 = (standard(x)[0] * gain[0] + bias[6]).astype(BF)
    w_qkv = assemble(qkv_shard, qkv_other, 1)
    key = dot(n1, w_qkv[1]).astype(BF)
    value = (dot(n1, w_qkv[2]) + bias[1]).astype(BF)
    kv_self = spread(jnp.stack([key, value]), groups)
    query = (dot(n1, w_qkv[0]) + bias[0]).astype(BF)

    w_mid = assemble(mid_shard, mid_other, 1)
    ckey = dot(enc_bf, w_mid[1]).astype(BF)
    cvalue = (dot(enc_bf, w_mid[2]) + bias[4]).astype(BF)
    kv_cross = spread(jnp.stack([ckey, cvalue]), groups)

    mixed, mass = attention(query, kv_self, places)
    r1 = x + dot(mixed, w_mid[3]) + bias[2]
    n2 = (standard(r1)[0] * gain[1] + bias[7]).astype(BF)
    cquery = (dot(n2, w_mid[0]) + bias[3]).astype(BF)
    cmixed, cmass = attention(cquery, kv_cross, None)
    r2 = r1 + dot(cmixed, w_mid[4]) + bias[5]
    n3 = (standard(r2)[0] * gain[2] + bias[8]).astype(BF)

    w_up = assemble(up_weight, up_other, 0)
    w_down = assemble(down_weight, down_other, 0)
    pre = dot(n3, w_up) + up_b
    act, gelu_back = jax.vjp(gelu_exact, pre)
    act = act.astype(BF)
    layer_out = (r2 + dot(act, w_down) + down_b).astype(BF)
    dact = dot_t(cot, w_down)
    dpre = gelu_back(dact)[0].astype(BF)
    g_down = t_dot(act, cot).astype(BF)
    g_up = [t_dot(n3, dpre[:, b * width : (b + 1) * width]).astype(BF) for b in range(blocks)]
    g_down = g_down.reshape(4, blocks, shard, width).transpose(1, 0, 2, 3).reshape(blocks, width, width)
    dn3 = dot_t(dpre, w_up)
    back3, dgain3, dshift3 = norm_back(dn3, r2, gain[2])
    dr2 = cot.astype(F32) + back3
    ffn_a = over_cores(g_down)
    ffn_b = over_cores(jnp.stack(g_up))

    gc = dr2.astype(BF)
    doc = dot_t(gc, w_mid[4]).astype(BF)
    dcq, cmine, ctheirs = attention_back(cquery, doc, cmixed, cmass, kv_cross, None)
    dcq, ffn_a, ffn_b = lax.optimization_barrier((dcq, ffn_a, ffn_b))
    ffn_a = over_x(ffn_a)
    dckv = collect(cmine, ctheirs, groups).astype(BF)
    dn2 = dot_t(dcq, w_mid[0])
    back2, dgain2, dshift2 = norm_back(dn2, r1, gain[1])
    dr1 = dr2 + back2
    gs = dr1.astype(BF)
    dos = dot_t(gs, w_mid[3]).astype(BF)
    dq, mine, theirs = attention_back(query, dos, mixed, mass, kv_self, places)
    mine, theirs, dckv, ffn_a = lax.optimization_barrier((mine, theirs, dckv, ffn_a))
    ffn_b = over_x(ffn_b)
    cross = over_cores(
        jnp.stack(
            [
                t_dot(n2, dcq).astype(BF),
                t_dot(enc_bf, dckv[0]).astype(BF),
                t_dot(enc_bf, dckv[1]).astype(BF),
                t_dot(cmixed, gc).astype(BF),
            ]
        )
    )
    grad_encoded = (dot_t(dckv[0], w_mid[1]) + dot_t(dckv[1], w_mid[2])).astype(BF)
    if grad_encoded.shape == layer_out.shape:
        layer_out, grad_encoded = undeal(jnp.stack([layer_out, grad_encoded]))
    else:
        layer_out, grad_encoded = undeal(layer_out), undeal(grad_encoded)
    dkv = collect(mine, theirs, groups).astype(BF)
    dkv, cross, ffn_b = lax.optimization_barrier((dkv, cross, ffn_b))
    cross = over_x(cross)
    ffn_a, ffn_b = over_ctx(ffn_a), over_ctx(ffn_b)
    own = over_cores(
        jnp.stack(
            [
                t_dot(n1, dq).astype(BF),
                t_dot(n1, dkv[0]).astype(BF),
                t_dot(n1, dkv[1]).astype(BF),
                t_dot(mixed, gs).astype(BF),
            ]
        )
    )
    dn1 = dot_t(dq, w_qkv[0]) + dot_t(dkv[0], w_qkv[1]) + dot_t(dkv[1], w_qkv[2])
    back1, dgain1, dshift1 = norm_back(dn1, x, gain[0])
    grad_layer = undeal((dr1 + back1).astype(BF))
    own = over_ctx(over_x(own))
    cross = over_ctx(cross)

    rows = jnp.concatenate(
        [
            jnp.stack(
                [
                    dgain1,
                    dgain2,
                    dgain3,
                    column_sum(dq),
                    column_sum(dkv[1]),
                    column_sum(gs),
                    column_sum(dcq),
                    column_sum(dckv[1]),
                    column_sum(gc),
                    dshift1,
                    dshift2,
                    dshift3,
                ]
            ),
            column_sum(dpre).reshape(4, blocks, shard).transpose(1, 0, 2).reshape(blocks, width),
            column_sum(cot).reshape(1, width),
        ],
        axis=0,
    )
    mine = sum_vectors(rows)
    return (
        layer_out,
        grad_layer.astype(F32),
        grad_encoded.astype(F32),
        jnp.concatenate([own[:3], cross[:3]], axis=0),
        jnp.concatenate([own[3:], cross[3:]], axis=0),
        jnp.concatenate([ffn_b[b] for b in range(blocks)], axis=1),
        ffn_a.reshape(blocks * shard, width),
        mine[:3],
        mine[3:12],
        mine[12 : 12 + blocks].reshape(-1),
        mine[12 + blocks],
    )


def solution(mesh):
    ctx = mesh.shape["ctx"]
    grid = Mesh(mesh.devices.reshape(2, 2, ctx // (2 * LINE), LINE, 2), ("fx", "core", "o", "z", "y"))
    fsdp = ("fx", "core")
    rows = P(fsdp, ("o", "z", "y"), None)
    weights = (
        P(None, fsdp, None),
        P(None, fsdp, None),
        P(fsdp, None),
        P(fsdp, None),
        P(None, fsdp),
        P(None, fsdp),
        P(fsdp),
        P(fsdp),
    )
    return jax.shard_map(
        per_device,
        mesh=grid,
        in_specs=(rows, rows, P()) + weights + (rows,),
        out_specs=(rows, rows, rows) + weights,
        check_vma=False,
    )
```

```python
import functools
import math

import jax
import jax.numpy as jnp
from jax import lax
from jax.experimental import pallas as pl
from jax.experimental.pallas import tpu as pltpu
from jax.sharding import Mesh
from jax.sharding import PartitionSpec as P

HEADS = 12
HD = 64
PAIR = 2 * HD
SCORE_SCALE = 0.125
MASK_FILL = -1e30
NORM_EPSILON = 1e-05
LINE = 4
SWAP = [(0, 1), (1, 0)]
BF = jnp.bfloat16
F32 = jnp.float32
MIB = 1 << 20


def dot(left, right):
    return jnp.dot(left, right, preferred_element_type=F32)


def dot_t(left, right):
    return lax.dot_general(left, right, (((1,), (1,)), ((), ())), preferred_element_type=F32)


def t_dot(left, right):
    return lax.dot_general(left, right, (((0,), (0,)), ((), ())), preferred_element_type=F32)


def split_heads(block):
    lane = lax.broadcasted_iota(jnp.int32, block.shape, 1)
    zero = jnp.zeros_like(block)
    return jnp.concatenate([jnp.where(lane < HD, block, zero), jnp.where(lane < HD, zero, block)], axis=0)


def join_heads(columns):
    rows = columns.shape[1] // 2
    return jnp.concatenate([columns[:HD, :rows], columns[HD:, rows:]], axis=0).T


def forward_kernel(masked, pieces, *refs):
    if masked:
        key_place_ref, query_place_ref, refs = refs[0], refs[1], refs[2:]
    query_ref, kv_refs = refs[0], refs[1 : 1 + pieces]
    out_ref, mass_ref, scores_ref = refs[1 + pieces :]
    query = split_heads(query_ref[...] * jnp.asarray(SCORE_SCALE, BF))
    piece = kv_refs[0].shape[1]
    if masked:
        query_place = query_place_ref[...]
        query_place = jnp.concatenate([query_place, query_place], axis=1)
    top = None
    for i in range(pieces):
        scores = dot_t(kv_refs[i][0], query)
        if masked:
            scores = jnp.where(key_place_ref[pl.ds(i * piece, piece), :] <= query_place, scores, MASK_FILL)
        scores_ref[pl.ds(i * piece, piece), :] = scores
        high = jnp.max(scores, axis=0, keepdims=True)
        top = high if top is None else jnp.maximum(top, high)
    mass = jnp.zeros_like(top)
    mixed = None
    for i in range(pieces):
        probs = jnp.exp(scores_ref[pl.ds(i * piece, piece), :] - top)
        mass = mass + jnp.sum(probs, axis=0, keepdims=True)
        part = t_dot(kv_refs[i][1], probs.astype(BF))
        mixed = part if mixed is None else mixed + part
    out_ref[...] = join_heads(mixed * (1.0 / mass)).astype(BF)
    mass_ref[0] = top + jnp.log(mass)


def backward_kernel(masked, pieces, *refs):
    if masked:
        key_place_ref, query_place_ref, refs = refs[0], refs[1], refs[2:]
    query_ref, dout_ref, out_ref, mass_ref = refs[:4]
    kv_refs = refs[4 : 4 + pieces]
    dquery_ref, mine_ref, theirs_ref = refs[4 + pieces :]
    query = split_heads(query_ref[...] * jnp.asarray(SCORE_SCALE, BF))
    dout = dout_ref[...]
    prod = (dout.astype(F32) * out_ref[...].astype(F32)).T
    delta = jnp.concatenate(
        [jnp.sum(prod[:HD], axis=0, keepdims=True), jnp.sum(prod[HD:], axis=0, keepdims=True)], axis=1
    )
    dout = split_heads(dout)
    log_mass = mass_ref[0]
    piece = kv_refs[0].shape[1]
    if masked:
        query_place = query_place_ref[...]
        query_place = jnp.concatenate([query_place, query_place], axis=1)
    dquery = None
    for i in range(pieces):
        keys = kv_refs[i][0]
        scores = dot_t(keys, query)
        if masked:
            scores = jnp.where(key_place_ref[pl.ds(i * piece, piece), :] <= query_place, scores, MASK_FILL)
        probs = jnp.exp(scores - log_mass)
        dprobs = dot_t(kv_refs[i][1], dout)
        dscores = (probs * (dprobs - delta)).astype(BF)
        dkv_ref = theirs_ref if i % 2 else mine_ref
        dkv_ref[i // 2, 0] = dot(dscores, query).astype(BF)
        dkv_ref[i // 2, 1] = dot(probs.astype(BF), dout).astype(BF)
        part = t_dot(keys, dscores)
        dquery = part if dquery is None else dquery + part
    dquery_ref[...] = (join_heads(dquery) * SCORE_SCALE).astype(BF)


def place_specs(masked, places):
    if not masked:
        return [], []
    key_places, query_places = places
    return [key_places, query_places], [
        pl.BlockSpec(key_places.shape, lambda h: (0, 0)),
        pl.BlockSpec(query_places.shape, lambda h: (0, 0)),
    ]


def attention(query, kv, places):
    masked = places is not None
    rows, width = query.shape
    piece = kv[0].shape[1]
    extra, extra_specs = place_specs(masked, places)
    keys = piece * len(kv)
    return pl.pallas_call(
        functools.partial(forward_kernel, masked, len(kv)),
        grid=(width // PAIR,),
        in_specs=extra_specs
        + [pl.BlockSpec((rows, PAIR), lambda h: (0, h))]
        + [pl.BlockSpec((2, piece, PAIR), lambda h: (0, 0, h))] * len(kv),
        out_specs=[
            pl.BlockSpec((rows, PAIR), lambda h: (0, h)),
            pl.BlockSpec((1, 1, 2 * rows), lambda h: (h, 0, 0)),
        ],
        out_shape=[
            jax.ShapeDtypeStruct((rows, width), BF),
            jax.ShapeDtypeStruct((width // PAIR, 1, 2 * rows), F32),
        ],
        scratch_shapes=[pltpu.VMEM((keys, 2 * rows), F32)],
        compiler_params=pltpu.CompilerParams(vmem_limit_bytes=8 * MIB + 4096 * keys),
        cost_estimate=cost(8 * rows * keys / 2**18),
    )(*extra, query, *kv)


def attention_back(query, dout, out, mass, kv, places):
    masked = places is not None
    rows, width = query.shape
    piece = kv[0].shape[1]
    extra, extra_specs = place_specs(masked, places)
    keys = piece * len(kv)
    column = pl.BlockSpec((rows, PAIR), lambda h: (0, h))
    pair = pl.BlockSpec((2, piece, PAIR), lambda h: (0, 0, h))
    groups = len(kv) // 2
    blocks = pl.BlockSpec((groups, 2, piece, PAIR), lambda h: (0, 0, 0, h))
    return pl.pallas_call(
        functools.partial(backward_kernel, masked, len(kv)),
        grid=(width // PAIR,),
        in_specs=extra_specs
        + [column, column, column, pl.BlockSpec((1, 1, 2 * rows), lambda h: (h, 0, 0))]
        + [pair] * len(kv),
        out_specs=[column, blocks, blocks],
        out_shape=[jax.ShapeDtypeStruct((rows, width), BF)]
        + [jax.ShapeDtypeStruct((groups, 2, piece, width), BF)] * 2,
        compiler_params=pltpu.CompilerParams(vmem_limit_bytes=8 * MIB + 4096 * keys),
        cost_estimate=cost(13 * rows * keys / 2**18),
    )(*extra, query, dout, out, mass, *kv)


def deal_perms():
    perms = []
    for r in range(LINE):
        perm = []
        for c in range(2):
            for z in range(LINE):
                k = (r - z) % LINE
                perm.append((c * LINE + z, (k % 2) * LINE + 2 * c + k // 2))
        perms.append(perm)
    return perms


DEAL = deal_perms()


def deal(arrays):
    if len({array.shape for array in arrays}) > 1:
        return [deal([array])[0] for array in arrays]
    _, rows, width = arrays[0].shape
    chunks = [array.reshape(LINE, rows // 2, width) for array in arrays]
    z = lax.axis_index("z")
    got = []
    for r in range(LINE):
        k = lax.rem(r - z + LINE, LINE)
        chunk = jnp.stack([lax.dynamic_index_in_dim(c, k, keepdims=False) for c in chunks])
        got.append(lax.ppermute(chunk, ("core", "z"), DEAL[r]))
    return [jnp.concatenate([g[i] for g in got], axis=0) for i in range(len(arrays))]


def undeal(arrays, kind):
    count = len(arrays)
    half = arrays[0].shape[0] // LINE
    got = []
    for r in range(LINE):
        chunk = jnp.stack([array[r * half : (r + 1) * half] for array in arrays])
        got.append(lax.ppermute(chunk, ("core", "z"), [(b, a) for a, b in DEAL[r]]))
    z = lax.axis_index("z")
    outs = []
    for i in range(count):
        mine = lax.dynamic_slice_in_dim(jnp.stack([g[i] for g in got + got]), z, LINE, axis=0)
        outs.append(mine.reshape(2, 2 * half, arrays[0].shape[1]).astype(kind[i]))
    return outs


def group_perm(groups, step):
    return [(i, (i + step) % groups) for i in range(groups)]


def to_others(own, groups):
    return [own] + [lax.ppermute(own, ("o", "y"), group_perm(groups, step)) for step in range(1, groups)]


def with_cores(blocks):
    pieces = []
    for block in blocks:
        pieces += [block, lax.ppermute(block, "core", SWAP)]
    return pieces


def collect(mine, got, groups):
    terms = [mine, got]
    for step in range(1, groups):
        back = [(b, a) for a, b in group_perm(groups, step)]
        terms.append(lax.ppermute(add([mine[step], got[step]]), ("o", "y"), back))
    return terms


def between_cores(array):
    return lax.ppermute(array, "core", SWAP)


def gather(own, other):
    return own, lax.ppermute(own, "core", SWAP), other, lax.ppermute(other, "core", SWAP)


def after(value, earlier):
    return lax.optimization_barrier((value, earlier))[0]


def add(terms):
    total = terms[0].astype(F32)
    for term in terms[1:]:
        total = total + term.astype(F32)
    return total.astype(BF)


def over_cores(keep, send):
    return [keep, lax.ppermute(send, "core", SWAP)]


def over_x(terms):
    got = lax.ppermute(add([term[1] for term in terms]), "fx", SWAP)
    return [term[0] for term in terms] + [got]


HALVES = ("y", "z0", "z1")


def exchange(array, name):
    if name == "y":
        return lax.ppermute(array, "y", SWAP)
    flip = 1 if name == "z0" else 2
    return lax.ppermute(array, "z", [(i, i ^ flip) for i in range(LINE)])


def half_index(name):
    z = lax.axis_index("z")
    return lax.axis_index("y") if name == "y" else lax.rem(z, 2) if name == "z0" else lax.div(z, 2)


def cut_rows(terms, order):
    return [term.reshape(2, 2, 2, -1, term.shape[-1]) for term in terms]


def halve(terms, name):
    i = half_index(name)
    theirs = add([lax.dynamic_index_in_dim(term, 1 - i, 0, keepdims=False) for term in terms])
    got = exchange(theirs, name)
    return [lax.dynamic_index_in_dim(term, i, 0, keepdims=False) for term in terms] + [got]


def double(part, name):
    other = exchange(part, name)
    first = half_index(name) == 0
    return jnp.concatenate([jnp.where(first, part, other), jnp.where(first, other, part)], axis=0)


def sum_down(terms, order):
    terms = cut_rows(terms, order)
    for name in order:
        terms = halve(terms, name)
    return add(terms)


def send_back(part, order, shape):
    for name in reversed(order):
        part = double(part, name)
    return part.astype(F32).reshape(shape)


def over_ctx(terms, order, shape):
    if lax.axis_size("o") > 1:
        return lax.psum(add(terms), ("o", "z", "y")).astype(F32).reshape(shape)
    return send_back(sum_down(terms, order), order, shape)


def sum_vectors(cut):
    n_ctx = lax.axis_size("o") * 2 * LINE
    cut = jnp.broadcast_to(cut[:, None], (4, n_ctx) + cut.shape[1:]).reshape((4 * n_ctx,) + cut.shape[1:])
    got = lax.all_to_all(cut, ("fx", "core", "o", "z", "y"), 0, 0, tiled=True)
    return jnp.sum(got.astype(F32), axis=0)


def standard(values):
    center = values - jnp.mean(values, axis=-1, keepdims=True)
    inverse = lax.rsqrt(jnp.mean(center * center, axis=-1, keepdims=True) + NORM_EPSILON)
    return center * inverse, inverse


def norm_back(dnormed, values, gain):
    z, inverse = standard(values)
    a = dnormed * gain
    dvalues = (
        a - jnp.mean(a, axis=-1, keepdims=True) - z * jnp.mean(a * z, axis=-1, keepdims=True)
    ) * inverse
    return dvalues, jnp.sum(dnormed * z, axis=0, keepdims=True), jnp.sum(dnormed, axis=0, keepdims=True)


def column_sum(values):
    return jnp.sum(values.astype(F32), axis=0, keepdims=True)


GAIN, BIAS, UP, DOWN = 0, 3, 12, 13
TABLE = 24
PAIR_AT, REST_AT, LAST_AT = (0, 0, 0, 0), (2, 2, 0, 0), (4, 4, 2, 2)


def vector(vec_ref, row):
    return vec_ref[row : row + 1, :]


def start_packed(pieces, slot_ref, full_ref, sems):
    n, rows = full_ref.shape[0], full_ref.shape[1] // 4
    copies = []
    for j, piece in enumerate(pieces):
        place = pl.ds(pl.multiple_of(slot_ref[j] * rows, rows), rows)
        for i in range(n):
            copy = pltpu.make_async_copy(
                piece.at[pl.ds(i * rows, rows), :], full_ref.at[i, place, :], sems.at[j * n + i]
            )
            copy.start()
            copies.append(copy)
    return copies


def start_copies(pieces, firsts, slot_ref, full_ref, sems, base):
    copies = []
    for j, piece in enumerate(pieces):
        rows = piece.shape[-2]
        place = pl.ds(pl.multiple_of(slot_ref[j] * rows, rows), rows)
        if len(piece.shape) == 3:
            source, target = piece.at[pl.ds(firsts[j], full_ref.shape[0])], full_ref.at[:, place, :]
        else:
            source, target = piece, full_ref.at[place, :]
        copy = pltpu.make_async_copy(source, target, sems.at[base + j])
        copy.start()
        copies.append(copy)
    return copies


def wait_all(copies):
    for copy in copies:
        copy.wait()


def put_grad(unit, turned, right, slot_ref, keep_ref, send_ref):
    rows = turned.shape[0] // 4
    for j in range(4):
        place = pl.ds(pl.multiple_of(slot_ref[j] * rows, rows), rows)
        block = dot(turned[place, :], right).astype(BF)
        target = send_ref if j % 2 else keep_ref
        target[j // 2, unit] = block


def self_in_kernel(slot_ref, x_ref, *refs):
    pieces, (n_ref, query_ref, kv_ref, vec_ref, full_ref, parts_ref, sems) = refs[:4], refs[4:]
    weights, shard = full_ref.shape[0], full_ref.shape[1] // 4
    extra = parts_ref.shape[1]
    small = []
    for j, piece in enumerate(pieces):
        copy = pltpu.make_async_copy(
            piece.at[pl.ds(weights * shard, extra), :], parts_ref.at[j], sems.at[4 * weights + j]
        )
        copy.start()
        small.append(copy)
    copies = start_packed(pieces, slot_ref, full_ref, sems)
    z = standard(x_ref[...].astype(F32))[0]
    wait_all(small)
    parts = [parts_ref[lax.bitwise_xor(slot_ref[0], p)].astype(F32)[:, :shard] for p in range(4)]
    own = parts_ref[0].astype(F32)[:, :shard]
    table = jnp.concatenate(parts, axis=1)
    vec_ref[0:UP, :] = table[0:UP]
    vec_ref[UP:DOWN, :] = jnp.concatenate([own[UP + i : UP + i + 1] for i in range(4)], axis=1)
    vec_ref[DOWN : DOWN + 1, :] = table[UP + 4 : UP + 5]
    normed = (z * table[GAIN : GAIN + 1] + table[BIAS + 6 : BIAS + 7]).astype(BF)
    n_ref[...] = normed
    wait_all(copies)
    kv_ref[0] = dot(normed, full_ref[1]).astype(BF)
    kv_ref[1] = (dot(normed, full_ref[2]) + table[BIAS + 1 : BIAS + 2]).astype(BF)
    query_ref[...] = (dot(normed, full_ref[0]) + table[BIAS : BIAS + 1]).astype(BF)


def cross_in_kernel(slot_ref, vec_ref, enc_ref, *refs):
    pieces, (kv_ref, full_ref, sems) = refs[:4], refs[4:]
    copies = start_copies(pieces, PAIR_AT, slot_ref, full_ref, sems, 0)
    enc = enc_ref[...]
    wait_all(copies)
    kv_ref[0] = dot(enc, full_ref[0]).astype(BF)
    kv_ref[1] = (dot(enc, full_ref[1]) + vector(vec_ref, BIAS + 4)).astype(BF)


def middle_kernel(slot_ref, vec_ref, mixed_ref, x_ref, *refs):
    pieces, (res_ref, n_ref, query_ref, full_ref, sems) = refs[:4], refs[4:]
    copies = start_copies(pieces, REST_AT, slot_ref, full_ref, sems, 0)
    wait_all(copies)
    res = x_ref[...].astype(F32) + dot(mixed_ref[...], full_ref[1]) + vector(vec_ref, BIAS + 2)
    res_ref[...] = res
    normed = (standard(res)[0] * vector(vec_ref, GAIN + 1) + vector(vec_ref, BIAS + 7)).astype(BF)
    n_ref[...] = normed
    query_ref[...] = (dot(normed, full_ref[0]) + vector(vec_ref, BIAS + 3)).astype(BF)


def before_feed_kernel(slot_ref, vec_ref, mixed_ref, res_ref, *refs):
    pieces, (out_ref, n_ref, full_ref, sems) = refs[:4], refs[4:]
    wait_all(start_copies(pieces, LAST_AT, slot_ref, full_ref, sems, 0))
    res = res_ref[...] + dot(mixed_ref[...], full_ref[0]) + vector(vec_ref, BIAS + 5)
    out_ref[...] = res
    n_ref[...] = (standard(res)[0] * vector(vec_ref, GAIN + 2) + vector(vec_ref, BIAS + 8)).astype(BF)


def feed_kernel(vec_ref, up_ref, down_ref, *refs):
    normed_refs, cot_refs = refs[:4], refs[4:8]
    dn_keep, dn_send, out_keep, out_send, act_ref, dpre_ref, rows_ref = refs[8:]
    bias = vector(vec_ref, UP)
    total = None
    for j in (1, 3, 0, 2):
        pre = dot(normed_refs[j][...], up_ref[...]) + bias
        phi = 0.5 * (1.0 + lax.erf(pre * math.sqrt(0.5)))
        slope = phi + pre * (jnp.exp(-0.5 * pre * pre) * (1.0 / math.sqrt(2.0 * math.pi)))
        act = (pre * phi).astype(BF)
        dpre = (dot_t(cot_refs[j][...], down_ref[...]) * slope).astype(BF)
        out, dn = (out_send, dn_send) if j % 2 else (out_keep, dn_keep)
        dn[j // 2] = dot_t(dpre, up_ref[...]).astype(BF)
        out[j // 2] = dot(act, down_ref[...]).astype(BF)
        act_ref[j] = act
        dpre_ref[j] = dpre
        sums = column_sum(dpre)
        total = sums if total is None else total + sums
    rows_ref[0:1, :] = total


def feed_grad_kernel(act_ref, dpre_ref, *refs):
    normed_refs, cot_refs, (cut_ref,) = refs[:4], refs[4:8], refs[8:]
    quarter, half = cut_ref.shape[-2:]

    def put(grad, first):
        for p in range(4):
            for q in range(4):
                rows = grad[(4 * p + q) * quarter : (4 * p + q + 1) * quarter].astype(BF)
                cut_ref[q, 0, first + p] = rows[:, :half]
                cut_ref[q, 1, first + p] = rows[:, half:]

    total = None
    for j in range(4):
        part = t_dot(normed_refs[j][...], dpre_ref[j])
        total = part if total is None else total + part
    put(total, 0)
    total = None
    for j in range(4):
        part = t_dot(act_ref[j], cot_refs[j][...])
        total = part if total is None else total + part
    put(total, 4)


def after_feed_kernel(slot_ref, vec_ref, dn_ref, dn_near_ref, dn_far_ref, res_ref, cot_ref, *refs):
    pieces, (dres_ref, dout_ref, rows_ref, full_ref, sems) = refs[:4], refs[4:]
    copies = start_copies(pieces, LAST_AT, slot_ref, full_ref, sems, 0)
    dn = dn_ref[0].astype(F32) + dn_near_ref[0].astype(F32) + dn_far_ref[...].astype(F32)
    cot = cot_ref[...].astype(F32)
    dvalues, dgain, dshift = norm_back(dn, res_ref[...], vector(vec_ref, GAIN + 2))
    dres = cot + dvalues
    dres_ref[...] = dres
    branch = dres.astype(BF)
    wait_all(copies)
    dout_ref[...] = dot_t(branch, full_ref[0]).astype(BF)
    rows_ref[0:1, :] = dgain
    rows_ref[1:2, :] = dshift
    rows_ref[2:3, :] = column_sum(branch)
    rows_ref[3:4, :] = column_sum(cot)


def middle_back_kernel(slot_ref, vec_ref, dquery_ref, n_ref, res_ref, dres_ref, mixed_ref, cmixed_ref, *refs):
    pieces, (dout_res_ref, dout_ref, keep_ref, send_ref, rows_ref, full_ref, turned_ref, sems) = refs[:4], refs[4:]
    copies = start_copies(pieces, REST_AT, slot_ref, full_ref, sems, 0)
    turned_ref[...] = n_ref[...].T
    dquery = dquery_ref[...]
    put_grad(0, turned_ref, dquery, slot_ref, keep_ref, send_ref)
    wait_all(copies)
    dn = dot_t(dquery, full_ref[0])
    dvalues, dgain, dshift = norm_back(dn, res_ref[...], vector(vec_ref, GAIN + 1))
    turned_ref[...] = cmixed_ref[...].T
    put_grad(2, turned_ref, dres_ref[...].astype(BF), slot_ref, keep_ref, send_ref)
    dres = dres_ref[...] + dvalues
    dout_res_ref[...] = dres
    branch = dres.astype(BF)
    dout_ref[...] = dot_t(branch, full_ref[1]).astype(BF)
    turned_ref[...] = mixed_ref[...].T
    put_grad(1, turned_ref, branch, slot_ref, keep_ref, send_ref)
    rows_ref[0:1, :] = dgain
    rows_ref[1:2, :] = dshift
    rows_ref[2:3, :] = column_sum(dquery)
    rows_ref[3:4, :] = column_sum(branch)


def total_of(parts):
    total = parts[0][0].astype(F32) + parts[1][0].astype(F32)
    for part in parts[2:]:
        total = total + part[...].astype(F32)
    return total.astype(BF)


def cross_back_kernel(count, slot_ref, enc_ref, n_ref, dquery_ref, *refs):
    parts, pieces = refs[:count], refs[count : count + 4]
    denc_ref, keep_ref, send_ref, rows_ref, full_ref, turned_ref, turned_enc_ref, sems = refs[count + 4 :]
    copies = start_copies(pieces, PAIR_AT, slot_ref, full_ref, sems, 0)
    turned_ref[...] = n_ref[...].T
    put_grad(2, turned_ref, dquery_ref[...], slot_ref, keep_ref, send_ref)
    dkv = total_of(parts)
    turned_enc_ref[...] = enc_ref[...].T
    put_grad(0, turned_enc_ref, dkv[0], slot_ref, keep_ref, send_ref)
    put_grad(1, turned_enc_ref, dkv[1], slot_ref, keep_ref, send_ref)
    rows_ref[0:1, :] = column_sum(dkv[1])
    wait_all(copies)
    denc_ref[...] = (dot_t(dkv[0], full_ref[0]) + dot_t(dkv[1], full_ref[1])).astype(BF)


def self_back_kernel(count, slot_ref, vec_ref, x_ref, n_ref, dquery_ref, dres_ref, up_ref, ffn_ref, mid_ref, enc_ref, res_ref, out_ref, out_near_ref, out_far_ref, *refs):
    parts, pieces = refs[:count], refs[count : count + 4]
    dx_ref, layer_ref, keep_ref, send_ref, cut_ref, full_ref, turned_ref, sems = refs[count + 4 :]
    copies = start_packed(pieces, slot_ref, full_ref, sems)
    dkv = total_of(parts)
    dquery = dquery_ref[...]
    turned_ref[...] = n_ref[...].T
    put_grad(0, turned_ref, dkv[0], slot_ref, keep_ref, send_ref)
    put_grad(1, turned_ref, dkv[1], slot_ref, keep_ref, send_ref)
    out = out_ref[0].astype(F32) + out_near_ref[0].astype(F32) + out_far_ref[...].astype(F32)
    layer_ref[...] = (res_ref[...] + out + vector(vec_ref, DOWN)).astype(BF)
    wait_all(copies)
    dn = dot_t(dquery, full_ref[0]) + dot_t(dkv[0], full_ref[1]) + dot_t(dkv[1], full_ref[2])
    dvalues, dgain, dshift = norm_back(dn, x_ref[...].astype(F32), vector(vec_ref, GAIN))
    dx_ref[...] = (dres_ref[...] + dvalues).astype(BF)
    rows = [
        dgain,
        mid_ref[0:1, :],
        ffn_ref[0:1, :],
        column_sum(dquery),
        column_sum(dkv[1]),
        mid_ref[3:4, :],
        mid_ref[2:3, :],
        enc_ref[0:1, :],
        ffn_ref[2:3, :],
        dshift,
        mid_ref[1:2, :],
        ffn_ref[1:2, :],
    ]
    shard = dgain.shape[1] // 4
    common = jnp.concatenate(rows + [ffn_ref[3:4, :]], axis=0)
    pad = jnp.zeros((cut_ref.shape[1] - common.shape[0] - 4, shard), F32)
    for p in range(4):
        up = jnp.where(slot_ref[0] == p, up_ref[0:1, :], 0.0)
        ups = [up[:, i * shard : (i + 1) * shard] for i in range(4)]
        cut_ref[p] = jnp.concatenate([common[:, p * shard : (p + 1) * shard]] + ups + [pad], axis=0).astype(BF)


ROWS_CUT = 32
WHOLE = pl.BlockSpec(memory_space=pltpu.VMEM)
LEFT = pl.BlockSpec(memory_space=pl.ANY)
SCALARS = pl.BlockSpec(memory_space=pltpu.SMEM)


def cost(microseconds):
    return pl.CostEstimate(flops=0, bytes_accessed=int(microseconds * 3.5e6), transcendentals=0)


def dense(kernel, scalars, blocks, pieces, outs, scratch, microseconds, copies=None):
    copies = len(pieces) if copies is None else copies
    held = sum(math.prod(b.shape) * b.dtype.itemsize for b in blocks)
    held += sum(math.prod(shape) * jnp.dtype(kind).itemsize for shape, kind in outs)
    held += sum(math.prod(ref.shape) * jnp.dtype(ref.dtype).itemsize for ref in scratch)
    return pl.pallas_call(
        kernel,
        in_specs=[SCALARS] * len(scalars) + [WHOLE] * len(blocks) + [LEFT] * len(pieces),
        out_specs=[WHOLE] * len(outs),
        out_shape=[jax.ShapeDtypeStruct(shape, kind) for shape, kind in outs],
        scratch_shapes=scratch + ([pltpu.SemaphoreType.DMA((copies,))] if pieces else []),
        compiler_params=pltpu.CompilerParams(vmem_limit_bytes=8 * MIB + held),
        cost_estimate=cost(microseconds),
    )(*scalars, *blocks, *pieces)


def hold(*values):
    return lax.optimization_barrier(values)


def per_device(
    layer_in,
    encoded,
    pairing,
    attn_weight,
    out_weight,
    up_weight,
    down_weight,
    norm_gains,
    bias_rows,
    up_bias,
    down_bias,
    out_cotangent,
):
    seqs, local_rows, width = layer_in.shape
    outer = lax.axis_size("o")
    groups = outer * 2
    half = local_rows // 2
    shard = attn_weight.shape[1]
    hidden = up_weight.shape[1]
    blocks = hidden // width
    rows = LINE * half
    enc_rows = LINE * (encoded.shape[1] // 2)
    fx, y, z, o, core = (lax.axis_index(a) for a in ("fx", "y", "z", "o", "core"))

    vectors = jnp.concatenate(
        [norm_gains, bias_rows, up_bias.reshape(blocks, shard), down_bias.reshape(1, shard)], axis=0
    )
    vectors = jnp.pad(vectors, ((0, ROWS_CUT - vectors.shape[0]), (0, width - shard)))
    slots = jnp.stack([2 * fx + core, 2 * fx + 1 - core, 2 - 2 * fx + core, 3 - 2 * fx - core])
    qkv_shard = jnp.concatenate([attn_weight[:3].reshape(3 * shard, width), vectors], axis=0)
    qkv_other = lax.ppermute(qkv_shard, "fx", SWAP)
    qkv_near = between_cores(qkv_shard)
    x_bf, enc_bf, cot = deal([layer_in, encoded, out_cotangent])

    group = o * 2 + y
    spots = []
    for step in range(groups):
        source = lax.rem(group - step + groups, groups)
        for flip in range(2):
            c = core if flip == 0 else 1 - core
            k = 2 * lax.rem(z, 2) + c
            for r in range(LINE):
                line = lax.rem(r - k + LINE, LINE)
                spots.append((((source // 2) * LINE + line) * 2 + lax.rem(source, 2)) * 2 + c)
    spans = jnp.take(pairing.reshape(-1), jnp.stack(spots), axis=0)
    key_places = (spans[:, None] * half + jnp.arange(half, dtype=jnp.int32)[None, :]).reshape(-1, 1)
    query_places = key_places[:rows].reshape(1, -1)
    places = (key_places, query_places)

    product = 2 * rows * width * width
    square = (width, width)
    act, real = ((rows, width), BF), ((rows, width), F32)
    turned = pltpu.VMEM((width, rows), BF)

    def weights(n):
        return pltpu.VMEM((n,) + square, BF)

    def grads(n):
        return [((2, n, shard, width), BF)] * 2

    note = ((16, width), F32)

    mid_shard = jnp.concatenate([attn_weight[4:], attn_weight[3:4], out_weight], axis=0)
    x_bf, enc_bf, cot, qkv_other, qkv_near, mid_shard, pair_shard, rest_shard, up_weight = hold(
        x_bf, enc_bf, cot, qkv_other, qkv_near, mid_shard, attn_weight[4:], mid_shard[2:], up_weight
    )
    w_qkv = (qkv_shard, qkv_near, qkv_other, between_cores(qkv_other))
    pair_other = lax.ppermute(pair_shard, "fx", SWAP)
    mid_near = between_cores(mid_shard)
    extra = ROWS_CUT
    n1, query, kv, vec = dense(
        self_in_kernel,
        [slots],
        [x_bf],
        w_qkv,
        [act, act, ((2, rows, width), BF), ((TABLE, width), F32)],
        [weights(3), pltpu.VMEM((4, extra, width), BF)],
        4,
        copies=16,
    )
    n1, query, kv, vec = hold(n1, query, kv, vec)
    kv_self = to_others(kv, groups)
    near_self = between_cores(kv)
    pair_other, rest_shard, mid_near = hold(pair_other, rest_shard, mid_near)
    rest_other = lax.ppermute(rest_shard, "fx", SWAP)
    w_pair = (mid_shard, mid_near, pair_other, between_cores(pair_other))
    (kv,) = dense(
        cross_in_kernel, [slots], [vec, enc_bf], w_pair, [((2, enc_rows, width), BF)], [weights(2)], 3.5
    )
    kv_self, near_self, kv = hold(kv_self, near_self, kv)
    kv_cross = to_others(kv, groups)
    near_cross = between_cores(kv)
    kv_self = [kv_self[0], near_self] + with_cores(kv_self[1:])
    mixed, mass = attention(query, kv_self, places)
    up_cut = up_weight.reshape(shard, 4, width).transpose(1, 0, 2)
    mixed, mass, up_cut, rest_other, cot = hold(mixed, mass, up_cut, rest_other, cot)
    w_rest = (mid_shard, mid_near, rest_other, between_cores(rest_other))
    up_own = lax.all_to_all(up_cut, ("fx", "core"), 0, 0, tiled=True).reshape(width, width)
    cot_other = lax.ppermute(cot, "fx", SWAP)
    cot_near = between_cores(cot)
    r1, n2, cquery = dense(middle_kernel, [slots], [vec, mixed, x_bf], w_rest, [real, act, act], [weights(2)], 3.3)
    r1, n2, cquery, kv_cross, near_cross = hold(r1, n2, cquery, kv_cross, near_cross)
    kv_cross = [kv_cross[0], near_cross] + with_cores(kv_cross[1:])
    cmixed, cmass = attention(cquery, kv_cross, None)
    cmixed, cmass, cot_other, cot_near, up_own = hold(cmixed, cmass, cot_other, cot_near, up_own)
    r2, n3 = dense(before_feed_kernel, [slots], [vec, cmixed, r1], w_rest, [real, act], [weights(1)], 2.7)
    n3_other = lax.ppermute(n3, "fx", SWAP)
    cots = (cot, cot_near, cot_other, between_cores(cot_other))
    n3s = (n3, between_cores(n3), n3_other, between_cores(n3_other))
    pair = ((2, rows, width), BF)
    four = ((4, rows, width), BF)
    dn_keep, dn_send, out_keep, out_send, hidden_act, dpre, up_rows = dense(
        feed_kernel,
        [],
        [vec, up_own, down_weight] + list(n3s) + list(cots),
        [],
        [pair, pair, pair, pair, four, four, ((8, width), F32)],
        [],
        8,
    )

    order = ("y", "z0", "z1")
    single = outer == 1

    def step(terms, name):
        return halve(terms, name) if single else terms

    dn_got = between_cores(dn_send)
    dn_keep, dn_got, hidden_act, dpre = hold(dn_keep, dn_got, hidden_act, dpre)
    dn_far = lax.ppermute(add([dn_keep[1], dn_got[1]]), "fx", SWAP)
    (feed,) = dense(
        feed_grad_kernel,
        [],
        [hidden_act, dpre] + list(n3s) + list(cots),
        [],
        [((4, 2, 8, shard // 4, width // 2), BF)],
        [],
        6,
    )
    dn_far, feed, out_keep, out_send = hold(dn_far, feed, out_keep, out_send)
    feed = [feed.reshape((2, 2, 2) + feed.shape[2:])]
    feed = step(feed, "y")
    dr2, doc, ffn_rows = dense(
        after_feed_kernel, [slots], [vec, dn_keep, dn_got, dn_far, r2, cot], w_rest, [real, act, note], [weights(1)], 2.7
    )

    dcq, cmine, ctheirs = attention_back(cquery, doc, cmixed, cmass, kv_cross, None)
    dcq, cmine, ctheirs, feed, dr2, ffn_rows = hold(dcq, cmine, ctheirs, feed, dr2, ffn_rows)
    cgot = between_cores(ctheirs)
    feed = step(feed, "z0")
    dr1, dos, middle_keep, middle_send, mid_rows = dense(
        middle_back_kernel,
        [slots],
        [vec, dcq, n2, r1, dr2, mixed, cmixed],
        w_rest,
        [real, act] + grads(3) + [note],
        [weights(2), turned],
        6,
    )
    dr1, dos, middle_keep, middle_send, mid_rows, cgot, cmine = hold(
        dr1, dos, middle_keep, middle_send, mid_rows, cgot, cmine
    )
    dckv = collect(cmine, cgot, groups)
    middle_got = between_cores(middle_send)
    dq, mine, theirs = attention_back(query, dos, mixed, mass, kv_self, places)
    dq, mine, theirs, dckv, feed, middle_keep, middle_got = hold(dq, mine, theirs, dckv, feed, middle_keep, middle_got)
    got = between_cores(theirs)
    middle = over_x([middle_keep, middle_got])
    feed = step(feed, "z1")
    mine, got, out_keep, out_send = hold(mine, got, out_keep, out_send)
    dkv = collect(mine, got, groups)
    out_got = between_cores(out_send)
    grad_encoded, late_keep, late_send, enc_rows_sum = dense(
        functools.partial(cross_back_kernel, len(dckv)),
        [slots],
        [enc_bf, n1, dq] + dckv,
        w_pair,
        [((enc_rows, width), BF)] + grads(3) + [note],
        [weights(2), turned, pltpu.VMEM((width, enc_rows), BF)],
        6,
    )
    grad_encoded, late_keep, late_send, middle, feed, out_keep, out_got = hold(
        grad_encoded, late_keep, late_send, middle, feed, out_keep, out_got
    )
    out_far = lax.ppermute(add([out_keep[1], out_got[1]]), "fx", SWAP)
    (grad_encoded,) = undeal([grad_encoded], [F32])
    late_got = between_cores(late_send)
    middle = cut_rows(middle, order)
    middle = step(middle, "y")
    dkv, late_keep, late_got, out_far, feed, grad_encoded = hold(dkv, late_keep, late_got, out_far, feed, grad_encoded)
    late = over_x([late_keep, late_got])
    grad_layer, layer_out, keep, send, cut = dense(
        functools.partial(self_back_kernel, len(dkv)),
        [slots],
        [vec, x_bf, n1, dq, dr1, up_rows, ffn_rows, mid_rows, enc_rows_sum, r2, out_keep, out_got, out_far] + dkv,
        w_qkv,
        [act, act] + grads(2) + [((4, ROWS_CUT, shard), BF)],
        [weights(3), turned],
        7,
        copies=12,
    )
    if single:
        feed = add(feed)
        feed_up = lax.all_to_all(feed[:4], ("fx", "core"), 0, 0, tiled=True)
        feed = jnp.concatenate([feed_up, feed[4:]], axis=0)[None]
    grad_layer, layer_out, keep, send, cut, middle, feed, late = hold(
        grad_layer, layer_out, keep, send, cut, middle, feed, late
    )
    if single:
        got = between_cores(send)
        feed = double(feed, "z1")
        middle = halve(middle, "z0")
        late = halve(cut_rows(late, order), "y")
        keep, got, feed, middle, late, grad_layer, layer_out = hold(keep, got, feed, middle, late, grad_layer, layer_out)
        own = over_x([keep, got])
        feed = double(feed, "z0")
        middle = halve(middle, "z1")
        late = halve(late, "z0")
        own, feed, middle, late, grad_layer, layer_out = hold(own, feed, middle, late, grad_layer, layer_out)
        own = add(own).reshape(2 * LINE, -1, width)
        own = lax.all_to_all(own, ("z", "y"), 0, 0, tiled=True)
        feed = double(feed, "y")
        middle = double(add(middle), "z1")
        late = halve(late, "z1")
        own, feed, middle, late, grad_layer, layer_out = hold(own, feed, middle, late, grad_layer, layer_out)
        own = jnp.sum(own.astype(F32), axis=0, keepdims=True).astype(BF)
        own = lax.all_to_all(jnp.broadcast_to(own, (2 * LINE,) + own.shape[1:]), ("z", "y"), 0, 0, tiled=True)
        middle = double(middle, "z0")
        late = double(add(late), "z1")
        own, middle, late, grad_layer, layer_out, cut = hold(own, middle, late, grad_layer, layer_out, cut)
        total = sum_vectors(cut)
        middle = double(middle, "y")
        late = double(late, "z0")
        layer_out, grad_layer = undeal([layer_out, grad_layer], [BF, F32])
        middle, late = hold(middle, late)
        late = double(late, "y").astype(F32).reshape(3, shard, width)
        middle = middle.astype(F32).reshape(3, shard, width)
        own = own.astype(F32).reshape(2, shard, width)
        feed = feed.astype(F32).reshape(2, 2, 2, 8, shard // 4, width // 2)
    else:
        own = over_ctx(over_x(over_cores(keep, send)), (), (2, shard, width))
        total = sum_vectors(cut)
        layer_out, grad_layer = undeal([layer_out, grad_layer], [BF, F32])
        feed = lax.psum(feed[0], ("o", "z", "y"))
        feed_up = feed[:, :, :, :4].transpose(3, 0, 1, 2, 4, 5)
        feed_up = lax.all_to_all(feed_up, ("fx", "core"), 0, 0, tiled=True).transpose(1, 2, 3, 0, 4, 5)
        feed = jnp.concatenate([feed_up, feed[:, :, :, 4:]], axis=3).astype(F32)
        middle = over_ctx([t.reshape(3, shard, width) for t in middle], order, (3, shard, width))
        late = over_ctx(late, order, (3, shard, width))
    g_up = feed[:, :, :, :4].transpose(0, 1, 4, 3, 2, 5).reshape(shard, hidden)
    g_down = feed[:, :, :, 4:].transpose(3, 0, 1, 4, 2, 5).reshape(hidden // 4, width)
    return (
        layer_out,
        grad_layer,
        grad_encoded,
        jnp.concatenate([late[2:], own, middle[:1], late[:2]], axis=0),
        middle[1:],
        g_up,
        g_down,
        total[:3],
        total[3:12],
        total[13 : 13 + blocks].reshape(-1),
        total[12],
    )


def solution(mesh):
    ctx = mesh.shape["ctx"]
    grid = Mesh(mesh.devices.reshape(2, 2, ctx // (2 * LINE), LINE, 2), ("fx", "core", "o", "z", "y"))
    fsdp = ("fx", "core")
    rows = P(fsdp, ("o", "z", "y"), None)
    weights = (
        P(None, fsdp, None),
        P(None, fsdp, None),
        P(fsdp, None),
        P(fsdp, None),
        P(None, fsdp),
        P(None, fsdp),
        P(fsdp),
        P(fsdp),
    )
    return jax.shard_map(
        per_device,
        mesh=grid,
        in_specs=(rows, rows, P()) + weights + (rows,),
        out_specs=(rows, rows, rows) + weights,
        check_vma=False,
    )
```

```python
import functools
import math

import jax
import jax.numpy as jnp
from jax import lax
from jax.experimental import pallas as pl
from jax.experimental.pallas import tpu as pltpu
from jax.sharding import Mesh
from jax.sharding import PartitionSpec as P

HEADS = 12
HD = 64
PAIR = 2 * HD
SCORE_SCALE = 0.125
MASK_FILL = -1e30
NORM_EPSILON = 1e-05
LINE = 4
SWAP = [(0, 1), (1, 0)]
BF = jnp.bfloat16
F32 = jnp.float32
MIB = 1 << 20


def dot(left, right):
    return jnp.dot(left, right, preferred_element_type=F32)


def dot_t(left, right):
    return lax.dot_general(left, right, (((1,), (1,)), ((), ())), preferred_element_type=F32)


def t_dot(left, right):
    return lax.dot_general(left, right, (((0,), (0,)), ((), ())), preferred_element_type=F32)


def split_heads(block):
    lane = lax.broadcasted_iota(jnp.int32, block.shape, 1)
    zero = jnp.zeros_like(block)
    return jnp.concatenate([jnp.where(lane < HD, block, zero), jnp.where(lane < HD, zero, block)], axis=0)


def join_heads(columns):
    rows = columns.shape[1] // 2
    return jnp.concatenate([columns[:HD, :rows], columns[HD:, rows:]], axis=0).T


def forward_kernel(masked, pieces, *refs):
    if masked:
        key_place_ref, query_place_ref, refs = refs[0], refs[1], refs[2:]
    query_ref, kv_refs = refs[0], refs[1 : 1 + pieces]
    out_ref, mass_ref, scores_ref = refs[1 + pieces :]
    query = split_heads(query_ref[...] * jnp.asarray(SCORE_SCALE, BF))
    piece = kv_refs[0].shape[1]
    if masked:
        query_place = query_place_ref[...]
        query_place = jnp.concatenate([query_place, query_place], axis=1)
    top = None
    for i in range(pieces):
        scores = dot_t(kv_refs[i][0], query)
        if masked:
            scores = jnp.where(key_place_ref[pl.ds(i * piece, piece), :] <= query_place, scores, MASK_FILL)
        scores_ref[pl.ds(i * piece, piece), :] = scores
        high = jnp.max(scores, axis=0, keepdims=True)
        top = high if top is None else jnp.maximum(top, high)
    mass = jnp.zeros_like(top)
    mixed = None
    for i in range(pieces):
        probs = jnp.exp(scores_ref[pl.ds(i * piece, piece), :] - top)
        mass = mass + jnp.sum(probs, axis=0, keepdims=True)
        part = t_dot(kv_refs[i][1], probs.astype(BF))
        mixed = part if mixed is None else mixed + part
    out_ref[...] = join_heads(mixed * (1.0 / mass)).astype(BF)
    mass_ref[0] = top + jnp.log(mass)


def backward_kernel(masked, pieces, *refs):
    if masked:
        key_place_ref, query_place_ref, refs = refs[0], refs[1], refs[2:]
    query_ref, dout_ref, out_ref, mass_ref = refs[:4]
    kv_refs = refs[4 : 4 + pieces]
    dquery_ref, mine_ref, theirs_ref = refs[4 + pieces :]
    query = split_heads(query_ref[...] * jnp.asarray(SCORE_SCALE, BF))
    dout = dout_ref[...]
    prod = (dout.astype(F32) * out_ref[...].astype(F32)).T
    delta = jnp.concatenate(
        [jnp.sum(prod[:HD], axis=0, keepdims=True), jnp.sum(prod[HD:], axis=0, keepdims=True)], axis=1
    )
    dout = split_heads(dout)
    log_mass = mass_ref[0]
    piece = kv_refs[0].shape[1]
    if masked:
        query_place = query_place_ref[...]
        query_place = jnp.concatenate([query_place, query_place], axis=1)
    dquery = None
    for i in range(pieces):
        keys = kv_refs[i][0]
        scores = dot_t(keys, query)
        if masked:
            scores = jnp.where(key_place_ref[pl.ds(i * piece, piece), :] <= query_place, scores, MASK_FILL)
        probs = jnp.exp(scores - log_mass)
        dprobs = dot_t(kv_refs[i][1], dout)
        dscores = (probs * (dprobs - delta)).astype(BF)
        dkv_ref = theirs_ref if i % 2 else mine_ref
        dkv_ref[i // 2, 0] = dot(dscores, query).astype(BF)
        dkv_ref[i // 2, 1] = dot(probs.astype(BF), dout).astype(BF)
        part = t_dot(keys, dscores)
        dquery = part if dquery is None else dquery + part
    dquery_ref[...] = (join_heads(dquery) * SCORE_SCALE).astype(BF)


def place_specs(masked, places):
    if not masked:
        return [], []
    key_places, query_places = places
    return [key_places, query_places], [
        pl.BlockSpec(key_places.shape, lambda h: (0, 0)),
        pl.BlockSpec(query_places.shape, lambda h: (0, 0)),
    ]


def attention(query, kv, places):
    masked = places is not None
    rows, width = query.shape
    piece = kv[0].shape[1]
    extra, extra_specs = place_specs(masked, places)
    keys = piece * len(kv)
    return pl.pallas_call(
        functools.partial(forward_kernel, masked, len(kv)),
        grid=(width // PAIR,),
        in_specs=extra_specs
        + [pl.BlockSpec((rows, PAIR), lambda h: (0, h))]
        + [pl.BlockSpec((2, piece, PAIR), lambda h: (0, 0, h))] * len(kv),
        out_specs=[
            pl.BlockSpec((rows, PAIR), lambda h: (0, h)),
            pl.BlockSpec((1, 1, 2 * rows), lambda h: (h, 0, 0)),
        ],
        out_shape=[
            jax.ShapeDtypeStruct((rows, width), BF),
            jax.ShapeDtypeStruct((width // PAIR, 1, 2 * rows), F32),
        ],
        scratch_shapes=[pltpu.VMEM((keys, 2 * rows), F32)],
        compiler_params=pltpu.CompilerParams(vmem_limit_bytes=60 * MIB),
        cost_estimate=cost(8 * rows * keys / 2**18),
    )(*extra, query, *kv)


def attention_back(query, dout, out, mass, kv, places):
    masked = places is not None
    rows, width = query.shape
    piece = kv[0].shape[1]
    extra, extra_specs = place_specs(masked, places)
    keys = piece * len(kv)
    column = pl.BlockSpec((rows, PAIR), lambda h: (0, h))
    pair = pl.BlockSpec((2, piece, PAIR), lambda h: (0, 0, h))
    groups = len(kv) // 2
    blocks = pl.BlockSpec((groups, 2, piece, PAIR), lambda h: (0, 0, 0, h))
    return pl.pallas_call(
        functools.partial(backward_kernel, masked, len(kv)),
        grid=(width // PAIR,),
        in_specs=extra_specs
        + [column, column, column, pl.BlockSpec((1, 1, 2 * rows), lambda h: (h, 0, 0))]
        + [pair] * len(kv),
        out_specs=[column, blocks, blocks],
        out_shape=[jax.ShapeDtypeStruct((rows, width), BF)]
        + [jax.ShapeDtypeStruct((groups, 2, piece, width), BF)] * 2,
        compiler_params=pltpu.CompilerParams(vmem_limit_bytes=60 * MIB),
        cost_estimate=cost(13 * rows * keys / 2**18),
    )(*extra, query, dout, out, mass, *kv)


def deal_perms():
    perms = []
    for r in range(LINE):
        perm = []
        for c in range(2):
            for z in range(LINE):
                k = (r - z) % LINE
                perm.append((c * LINE + z, (k % 2) * LINE + 2 * c + k // 2))
        perms.append(perm)
    return perms


DEAL = deal_perms()


def deal(arrays):
    if len({array.shape for array in arrays}) > 1:
        return [deal([array])[0] for array in arrays]
    _, rows, width = arrays[0].shape
    chunks = [array.reshape(LINE, rows // 2, width) for array in arrays]
    z = lax.axis_index("z")
    got = []
    for r in range(LINE):
        k = lax.rem(r - z + LINE, LINE)
        chunk = jnp.stack([lax.dynamic_index_in_dim(c, k, keepdims=False) for c in chunks])
        got.append(lax.ppermute(chunk, ("core", "z"), DEAL[r]))
    return [jnp.concatenate([g[i] for g in got], axis=0) for i in range(len(arrays))]


def deal_halves(array):
    _, rows, width = array.shape
    parts = array.reshape(2, 2, rows // 2, width)
    core = lax.axis_index("core")
    mine = lax.dynamic_index_in_dim(parts, core, 1, keepdims=False)
    return mine, lax.ppermute(lax.dynamic_index_in_dim(parts, 1 - core, 1, keepdims=False), "core", SWAP)


def deal_line(mine, got):
    core, z = lax.axis_index("core"), lax.axis_index("z")
    first = core == 0
    chunks = jnp.where(first, jnp.concatenate([mine, got], axis=0), jnp.concatenate([got, mine], axis=0))
    chunks = lax.all_to_all(chunks, "z", 0, 0, tiled=True)
    start = lax.rem(LINE - 2 * lax.rem(z, 2) - core, LINE)
    mine = lax.dynamic_slice_in_dim(jnp.concatenate([chunks, chunks], axis=0), start, LINE, axis=0)
    return mine.reshape(-1, mine.shape[-1])


def undeal(arrays, kind):
    count = len(arrays)
    half = arrays[0].shape[0] // LINE
    got = []
    for r in range(LINE):
        chunk = jnp.stack([array[r * half : (r + 1) * half] for array in arrays])
        got.append(lax.ppermute(chunk, ("core", "z"), [(b, a) for a, b in DEAL[r]]))
    z = lax.axis_index("z")
    outs = []
    for i in range(count):
        mine = lax.dynamic_slice_in_dim(jnp.stack([g[i] for g in got + got]), z, LINE, axis=0)
        outs.append(mine.reshape(2, 2 * half, arrays[0].shape[1]).astype(kind[i]))
    return outs


def group_perm(groups, step):
    return [(i, (i + step) % groups) for i in range(groups)]


def to_others(own, groups):
    return [own] + [lax.ppermute(own, ("o", "y"), group_perm(groups, step)) for step in range(1, groups)]


def with_cores(blocks):
    pieces = []
    for block in blocks:
        pieces += [block, lax.ppermute(block, "core", SWAP)]
    return pieces


def collect(mine, got, groups):
    terms = [mine, got]
    for step in range(1, groups):
        back = [(b, a) for a, b in group_perm(groups, step)]
        terms.append(lax.ppermute(add([mine[step], got[step]]), ("o", "y"), back))
    return terms


def between_cores(array):
    return lax.ppermute(array, "core", SWAP)


def gather(own, other):
    return own, lax.ppermute(own, "core", SWAP), other, lax.ppermute(other, "core", SWAP)


def after(value, earlier):
    return lax.optimization_barrier((value, earlier))[0]


def add(terms):
    total = terms[0].astype(F32)
    for term in terms[1:]:
        total = total + term.astype(F32)
    return total.astype(BF)


def over_cores(keep, send):
    return [(keep, ()), (lax.ppermute(send, "core", SWAP), ())]


def over_x(terms):
    got = lax.ppermute(add([array[1] for array, _ in terms]), "fx", SWAP)
    return [(array, (0,)) for array, _ in terms] + [(got, ())]


def part_over_x(terms, first, last):
    return lax.ppermute(add([array[1, first:last] for array, _ in terms]), "fx", SWAP)


HALVES = ("y", "z0", "z1")


def exchange(array, name):
    if name == "y":
        return lax.ppermute(array, "y", SWAP)
    flip = 1 if name == "z0" else 2
    return lax.ppermute(array, "z", [(i, i ^ flip) for i in range(LINE)])


def half_index(name):
    z = lax.axis_index("z")
    return lax.axis_index("y") if name == "y" else lax.rem(z, 2) if name == "z0" else lax.div(z, 2)


def half_of(term, more=()):
    array, names = term
    cut = 1 in names
    if 0 in names and len(names + more) > 1:
        array = array.reshape(2, 2, 2, 2, -1, array.shape[-1])
        cut = True
    for name in names + more:
        if name in (0, 1):
            array = array if name else array[0]
            continue
        name, other = name if isinstance(name, tuple) else (name, False)
        if array.ndim == 3 and not cut:
            array = array.reshape(2, 2, 2, -1, array.shape[-1])
        cut = True
        i = half_index(name)
        array = lax.dynamic_index_in_dim(array, 1 - i if other else i, 0, keepdims=False)
    return array


def halve(terms, name):
    theirs = add([half_of(term, ((name, True),)) for term in terms])
    got = exchange(theirs, name)
    return [(array, names + (name,)) for array, names in terms] + [(got, (1,))]


def both_halves(terms, name):
    mine = add([half_of(term) for term in terms])
    got = exchange(mine, name)
    mine = lax.optimization_barrier(mine)
    return mine, got


def double(part, name):
    other = exchange(part, name)
    first = half_index(name) == 0
    return jnp.where(first, jnp.concatenate([part, other], axis=0), jnp.concatenate([other, part], axis=0))


def standard(values):
    center = values - jnp.mean(values, axis=-1, keepdims=True)
    inverse = lax.rsqrt(jnp.mean(center * center, axis=-1, keepdims=True) + NORM_EPSILON)
    return center * inverse, inverse


def norm_back(dnormed, values, gain):
    z, inverse = standard(values)
    a = dnormed * gain
    dvalues = (
        a - jnp.mean(a, axis=-1, keepdims=True) - z * jnp.mean(a * z, axis=-1, keepdims=True)
    ) * inverse
    return dvalues, jnp.sum(dnormed * z, axis=0, keepdims=True), jnp.sum(dnormed, axis=0, keepdims=True)


def column_sum(values):
    return jnp.sum(values.astype(F32), axis=0, keepdims=True)


GAIN, BIAS, UP, DOWN = 0, 3, 12, 13
TABLE = 24
PAIR_AT, REST_AT, LAST_AT = (0, 0, 0, 0), (2, 2, 0, 0), (4, 4, 2, 2)


def vector(vec_ref, row):
    return vec_ref[row : row + 1, :]


def start_packed(pieces, slot_ref, full_ref, sems):
    n, rows = full_ref.shape[0], full_ref.shape[1] // 4
    copies = []
    for j, piece in enumerate(pieces):
        place = pl.ds(pl.multiple_of(slot_ref[j] * rows, rows), rows)
        for i in range(n):
            copy = pltpu.make_async_copy(
                piece.at[pl.ds(i * rows, rows), :], full_ref.at[i, place, :], sems.at[j * n + i]
            )
            copy.start()
            copies.append(copy)
    return copies


def start_copies(pieces, firsts, slot_ref, full_ref, sems, base):
    copies = []
    for j, piece in enumerate(pieces):
        rows = piece.shape[-2]
        place = pl.ds(pl.multiple_of(slot_ref[j] * rows, rows), rows)
        if len(piece.shape) == 3:
            source, target = piece.at[pl.ds(firsts[j], full_ref.shape[0])], full_ref.at[:, place, :]
        else:
            source, target = piece, full_ref.at[place, :]
        copy = pltpu.make_async_copy(source, target, sems.at[base + j])
        copy.start()
        copies.append(copy)
    return copies


def wait_all(copies):
    for copy in copies:
        copy.wait()


def put_grad(unit, turned, right, slot_ref, keep_ref, send_ref):
    rows = turned.shape[0] // 4
    for j in range(4):
        place = pl.ds(pl.multiple_of(slot_ref[j] * rows, rows), rows)
        block = dot(turned[place, :], right).astype(BF)
        target = send_ref if j % 2 else keep_ref
        target[j // 2, unit] = block


def self_in_kernel(ready, slot_ref, x_ref, *refs):
    pieces, (n_ref, query_ref, kv_ref, vec_ref, full_ref, parts_ref, sems) = refs[:4], refs[4:]
    weights, shard = full_ref.shape[0], full_ref.shape[1] // 4
    extra = parts_ref.shape[1]
    small = []
    for j, piece in enumerate(pieces):
        copy = pltpu.make_async_copy(
            piece.at[pl.ds(weights * shard, extra), :], parts_ref.at[j], sems.at[4 * weights + j]
        )
        copy.start()
        small.append(copy)
    copies = start_packed(pieces, slot_ref, full_ref, sems)
    ready()
    z = standard(x_ref[...].astype(F32))[0]
    wait_all(small)
    parts = [parts_ref[lax.bitwise_xor(slot_ref[0], p)].astype(F32)[:, :shard] for p in range(4)]
    own = parts_ref[0].astype(F32)[:, :shard]
    table = jnp.concatenate(parts, axis=1)
    vec_ref[0:UP, :] = table[0:UP]
    vec_ref[UP:DOWN, :] = jnp.concatenate([own[UP + i : UP + i + 1] for i in range(4)], axis=1)
    vec_ref[DOWN : DOWN + 1, :] = table[UP + 4 : UP + 5]
    normed = (z * table[GAIN : GAIN + 1] + table[BIAS + 6 : BIAS + 7]).astype(BF)
    n_ref[...] = normed
    wait_all(copies)
    kv_ref[0] = dot(normed, full_ref[1]).astype(BF)
    kv_ref[1] = (dot(normed, full_ref[2]) + table[BIAS + 1 : BIAS + 2]).astype(BF)
    query_ref[...] = (dot(normed, full_ref[0]) + table[BIAS : BIAS + 1]).astype(BF)


def cross_in_kernel(ready, slot_ref, vec_ref, enc_ref, *refs):
    pieces, (kv_ref, full_ref, sems) = refs[:4], refs[4:]
    copies = start_copies(pieces, PAIR_AT, slot_ref, full_ref, sems, 0)
    ready()
    enc = enc_ref[...]
    wait_all(copies)
    kv_ref[0] = dot(enc, full_ref[0]).astype(BF)
    kv_ref[1] = (dot(enc, full_ref[1]) + vector(vec_ref, BIAS + 4)).astype(BF)


def middle_kernel(ready, slot_ref, vec_ref, mixed_ref, x_ref, *refs):
    pieces, (res_ref, n_ref, query_ref, full_ref, sems) = refs[:4], refs[4:]
    copies = start_copies(pieces, REST_AT, slot_ref, full_ref, sems, 0)
    ready()
    wait_all(copies)
    res = x_ref[...].astype(F32) + dot(mixed_ref[...], full_ref[1]) + vector(vec_ref, BIAS + 2)
    res_ref[...] = res
    normed = (standard(res)[0] * vector(vec_ref, GAIN + 1) + vector(vec_ref, BIAS + 7)).astype(BF)
    n_ref[...] = normed
    query_ref[...] = (dot(normed, full_ref[0]) + vector(vec_ref, BIAS + 3)).astype(BF)


def before_feed_kernel(ready, slot_ref, vec_ref, mixed_ref, res_ref, *refs):
    pieces, (out_ref, n_ref, full_ref, sems) = refs[:4], refs[4:]
    copies = start_copies(pieces, LAST_AT, slot_ref, full_ref, sems, 0)
    ready()
    wait_all(copies)
    res = res_ref[...] + dot(mixed_ref[...], full_ref[0]) + vector(vec_ref, BIAS + 5)
    out_ref[...] = res
    n_ref[...] = (standard(res)[0] * vector(vec_ref, GAIN + 2) + vector(vec_ref, BIAS + 8)).astype(BF)


def feed_kernel(ready, vec_ref, up_ref, down_ref, *refs):
    normed_refs, cot_refs = refs[:4], refs[4:8]
    dn_keep, dn_send, out_keep, out_send, act_ref, dpre_ref, rows_ref = refs[8:]
    ready()
    bias = vector(vec_ref, UP)
    total = None
    for j in (1, 3, 0, 2):
        pre = dot(normed_refs[j][...], up_ref[...]) + bias
        phi = 0.5 * (1.0 + lax.erf(pre * math.sqrt(0.5)))
        slope = phi + pre * (jnp.exp(-0.5 * pre * pre) * (1.0 / math.sqrt(2.0 * math.pi)))
        act = (pre * phi).astype(BF)
        dpre = (dot_t(cot_refs[j][...], down_ref[...]) * slope).astype(BF)
        out, dn = (out_send, dn_send) if j % 2 else (out_keep, dn_keep)
        dn[j // 2] = dot_t(dpre, up_ref[...]).astype(BF)
        out[j // 2] = dot(act, down_ref[...]).astype(BF)
        act_ref[j] = act
        dpre_ref[j] = dpre
        sums = column_sum(dpre)
        total = sums if total is None else total + sums
    rows_ref[0:1, :] = total


def feed_grad_kernel(ready, act_ref, dpre_ref, *refs):
    normed_refs, cot_refs, (up_ref, down_ref) = refs[:4], refs[4:8], refs[8:]
    quarter, half = up_ref.shape[-2:]
    ready()

    def put(grad, cut_ref):
        for p in range(4):
            for q in range(4):
                rows = grad[(4 * p + q) * quarter : (4 * p + q + 1) * quarter].astype(BF)
                cut_ref[q, 0, p] = rows[:, :half]
                cut_ref[q, 1, p] = rows[:, half:]

    total = None
    for j in range(4):
        part = t_dot(normed_refs[j][...], dpre_ref[j])
        total = part if total is None else total + part
    put(total, up_ref)
    total = None
    for j in range(4):
        part = t_dot(act_ref[j], cot_refs[j][...])
        total = part if total is None else total + part
    put(total, down_ref)


def after_feed_kernel(ready, slot_ref, vec_ref, dn_ref, dn_near_ref, dn_far_ref, res_ref, cot_ref, *refs):
    pieces, (dres_ref, dout_ref, rows_ref, full_ref, sems) = refs[:4], refs[4:]
    copies = start_copies(pieces, LAST_AT, slot_ref, full_ref, sems, 0)
    ready()
    dn = dn_ref[0].astype(F32) + dn_near_ref[0].astype(F32) + dn_far_ref[...].astype(F32)
    cot = cot_ref[...].astype(F32)
    dvalues, dgain, dshift = norm_back(dn, res_ref[...], vector(vec_ref, GAIN + 2))
    dres = cot + dvalues
    dres_ref[...] = dres
    branch = dres.astype(BF)
    wait_all(copies)
    dout_ref[...] = dot_t(branch, full_ref[0]).astype(BF)
    rows_ref[0:1, :] = dgain
    rows_ref[1:2, :] = dshift
    rows_ref[2:3, :] = column_sum(branch)
    rows_ref[3:4, :] = column_sum(cot)


def middle_back_kernel(ready, slot_ref, vec_ref, dquery_ref, n_ref, res_ref, dres_ref, mixed_ref, cmixed_ref, *refs):
    pieces, (dout_res_ref, dout_ref, keep_ref, send_ref, rows_ref, full_ref, turned_ref, sems) = refs[:4], refs[4:]
    copies = start_copies(pieces, REST_AT, slot_ref, full_ref, sems, 0)
    ready()
    turned_ref[...] = n_ref[...].T
    dquery = dquery_ref[...]
    put_grad(0, turned_ref, dquery, slot_ref, keep_ref, send_ref)
    wait_all(copies)
    dn = dot_t(dquery, full_ref[0])
    dvalues, dgain, dshift = norm_back(dn, res_ref[...], vector(vec_ref, GAIN + 1))
    turned_ref[...] = cmixed_ref[...].T
    put_grad(2, turned_ref, dres_ref[...].astype(BF), slot_ref, keep_ref, send_ref)
    dres = dres_ref[...] + dvalues
    dout_res_ref[...] = dres
    branch = dres.astype(BF)
    dout_ref[...] = dot_t(branch, full_ref[1]).astype(BF)
    turned_ref[...] = mixed_ref[...].T
    put_grad(1, turned_ref, branch, slot_ref, keep_ref, send_ref)
    rows_ref[0:1, :] = dgain
    rows_ref[1:2, :] = dshift
    rows_ref[2:3, :] = column_sum(dquery)
    rows_ref[3:4, :] = column_sum(branch)


def total_of(parts):
    total = parts[0][0].astype(F32) + parts[1][0].astype(F32)
    for part in parts[2:]:
        total = total + part[...].astype(F32)
    return total.astype(BF)


def cross_back_kernel(count, ready, slot_ref, vec_ref, enc_ref, n_ref, dquery_ref, res_ref, out_ref, out_near_ref, out_far_ref, *refs):
    parts, pieces = refs[:count], refs[count : count + 4]
    denc_ref, layer_ref, keep_ref, send_ref, rows_ref, full_ref, turned_ref, turned_enc_ref, sems = refs[count + 4 :]
    copies = start_copies(pieces, PAIR_AT, slot_ref, full_ref, sems, 0)
    ready()
    turned_ref[...] = n_ref[...].T
    put_grad(2, turned_ref, dquery_ref[...], slot_ref, keep_ref, send_ref)
    dkv = total_of(parts)
    turned_enc_ref[...] = enc_ref[...].T
    put_grad(0, turned_enc_ref, dkv[0], slot_ref, keep_ref, send_ref)
    put_grad(1, turned_enc_ref, dkv[1], slot_ref, keep_ref, send_ref)
    rows_ref[0:1, :] = column_sum(dkv[1])
    out = out_ref[0].astype(F32) + out_near_ref[0].astype(F32) + out_far_ref[...].astype(F32)
    layer_ref[...] = (res_ref[...] + out + vector(vec_ref, DOWN)).astype(BF)
    wait_all(copies)
    denc_ref[...] = (dot_t(dkv[0], full_ref[0]) + dot_t(dkv[1], full_ref[1])).astype(BF)


def self_back_kernel(count, ready, slot_ref, vec_ref, x_ref, n_ref, dquery_ref, dres_ref, up_ref, ffn_ref, mid_ref, enc_ref, *refs):
    parts, pieces = refs[:count], refs[count : count + 4]
    dx_ref, keep_ref, send_ref, full_ref, turned_ref, sems = refs[count + 4 :]
    copies = start_packed(pieces, slot_ref, full_ref, sems)
    ready()
    dkv = total_of(parts)
    dquery = dquery_ref[...]
    turned_ref[...] = n_ref[...].T
    shard = turned_ref.shape[0] // 4
    for j in range(4):
        place = pl.ds(pl.multiple_of(slot_ref[j] * shard, shard), shard)
        target = send_ref if j % 2 else keep_ref
        target[j // 2, 0:shard] = dot(turned_ref[place, :], dkv[0]).astype(BF)
        target[j // 2, shard : 2 * shard] = dot(turned_ref[place, :], dkv[1]).astype(BF)
    wait_all(copies)
    dn = dot_t(dquery, full_ref[0]) + dot_t(dkv[0], full_ref[1]) + dot_t(dkv[1], full_ref[2])
    dvalues, dgain, dshift = norm_back(dn, x_ref[...].astype(F32), vector(vec_ref, GAIN))
    dx_ref[...] = (dres_ref[...] + dvalues).astype(BF)
    rows = [
        dgain,
        mid_ref[0:1, :],
        ffn_ref[0:1, :],
        column_sum(dquery),
        column_sum(dkv[1]),
        mid_ref[3:4, :],
        mid_ref[2:3, :],
        enc_ref[0:1, :],
        ffn_ref[2:3, :],
        dshift,
        mid_ref[1:2, :],
        ffn_ref[1:2, :],
    ]
    common = jnp.concatenate(rows + [ffn_ref[3:4, :]], axis=0)
    rest = keep_ref.shape[1] - 2 * shard
    for p in range(4):
        up = jnp.where(slot_ref[0] == p, up_ref[0:1, :], 0.0)
        parts = [common[i : i + 1, p * shard : (p + 1) * shard] for i in range(common.shape[0])]
        parts += [up[:, i * shard : (i + 1) * shard] for i in range(4)]
        parts += [jnp.zeros_like(parts[0])] * (-len(parts) % 4)
        lines = [jnp.concatenate(parts[i : i + 4], axis=1) for i in range(0, len(parts), 4)]
        lines.append(jnp.zeros((rest - len(lines), common.shape[1]), F32))
        lines = jnp.concatenate(lines, axis=0).astype(BF)
        flip = lax.bitwise_xor(slot_ref[0], p)

        @pl.when(lax.rem(flip, 2) == 0)
        def _():
            keep_ref[lax.div(flip, 2), 2 * shard :] = lines

        @pl.when(lax.rem(flip, 2) == 1)
        def _():
            send_ref[lax.div(flip, 2), 2 * shard :] = lines


def last_kernel(ready, late_ref, middle_ref, own_ref, attn_ref, out_ref, gain_ref, bias_ref, up_ref, down_ref):
    ready()
    shard = attn_ref.shape[1]

    def part(ref, i):
        return ref[i * shard : (i + 1) * shard, :].astype(F32)

    for i, (ref, j) in enumerate(
        [(late_ref, 2), (own_ref, 0), (own_ref, 1), (middle_ref, 0), (late_ref, 0), (late_ref, 1)]
    ):
        attn_ref[i] = part(ref, j)
    out_ref[0] = part(middle_ref, 1)
    out_ref[1] = part(middle_ref, 2)
    sums = own_ref[2 * shard :, :].astype(F32)

    def row(i):
        return sums[i // 4 : i // 4 + 1, (i % 4) * shard : (i % 4 + 1) * shard]

    gain_ref[...] = jnp.concatenate([row(i) for i in range(3)], axis=0)
    bias_ref[...] = jnp.concatenate([row(i) for i in range(3, 12)], axis=0)
    down_ref[...] = row(12)
    up_ref[...] = jnp.concatenate([row(i) for i in range(13, 17)], axis=1)


ROWS_CUT = 32
ROWS_SUM = 64
WHOLE = pl.BlockSpec(memory_space=pltpu.VMEM)
LEFT = pl.BlockSpec(memory_space=pltpu.HBM)
SCALARS = pl.BlockSpec(memory_space=pltpu.SMEM)


def cost(microseconds):
    return pl.CostEstimate(flops=0, bytes_accessed=int(microseconds * 3.5e6), transcendentals=0)


def dense(kernel, scalars, blocks, pieces, outs, scratch, microseconds, copies=None):
    copies = len(pieces) if copies is None else copies
    held = 2 * sum(math.prod(b.shape) * b.dtype.itemsize for b in blocks)
    held += sum(math.prod(shape) * jnp.dtype(kind).itemsize for shape, kind in outs)
    held += sum(math.prod(ref.shape) * jnp.dtype(ref.dtype).itemsize for ref in scratch)
    n_s, n_b, n_p, n_o = len(scalars), len(blocks), len(pieces), len(outs)

    def body(*refs):
        near, refs = refs[:n_s], refs[n_s:]
        far, refs = refs[:n_b], refs[n_b:]
        rest, refs = refs[: n_p + n_o], refs[n_p + n_o :]
        local, sems, refs = refs[:n_b], refs[n_b], refs[n_b + 1 :]
        fetches = [pltpu.make_async_copy(far[i], local[i], sems.at[i]) for i in range(n_b)]
        for fetch in fetches:
            fetch.start()

        def ready():
            for fetch in fetches:
                fetch.wait()

        kernel(ready, *near, *local, *rest, *refs)

    return pl.pallas_call(
        body,
        in_specs=[SCALARS] * n_s + [LEFT] * (n_b + n_p),
        out_specs=[pl.BlockSpec(shape, lambda d=len(shape): (0,) * d) for shape, _ in outs],
        out_shape=[jax.ShapeDtypeStruct(shape, kind) for shape, kind in outs],
        scratch_shapes=[pltpu.VMEM(b.shape, b.dtype) for b in blocks]
        + [pltpu.SemaphoreType.DMA((n_b,))]
        + scratch
        + ([pltpu.SemaphoreType.DMA((copies,))] if pieces else []),
        compiler_params=pltpu.CompilerParams(vmem_limit_bytes=60 * MIB),
        cost_estimate=cost(microseconds),
    )(*scalars, *blocks, *pieces)


def hold(*values):
    return lax.optimization_barrier(values)


def per_device(
    layer_in,
    encoded,
    pairing,
    attn_weight,
    out_weight,
    up_weight,
    down_weight,
    norm_gains,
    bias_rows,
    up_bias,
    down_bias,
    out_cotangent,
):
    seqs, local_rows, width = layer_in.shape
    outer = lax.axis_size("o")
    groups = outer * 2
    half = local_rows // 2
    shard = attn_weight.shape[1]
    hidden = up_weight.shape[1]
    blocks = hidden // width
    rows = LINE * half
    enc_rows = LINE * (encoded.shape[1] // 2)
    fx, y, z, o, core = (lax.axis_index(a) for a in ("fx", "y", "z", "o", "core"))

    vectors = jnp.concatenate(
        [norm_gains, bias_rows, up_bias.reshape(blocks, shard), down_bias.reshape(1, shard)], axis=0
    )
    vectors = jnp.pad(vectors, ((0, ROWS_CUT - vectors.shape[0]), (0, width - shard)))
    slots = jnp.stack([2 * fx + core, 2 * fx + 1 - core, 2 - 2 * fx + core, 3 - 2 * fx - core])
    qkv_shard = jnp.concatenate([attn_weight[:3].reshape(3 * shard, width), vectors], axis=0)
    qkv_other = lax.ppermute(qkv_shard, "fx", SWAP)
    qkv_near = between_cores(qkv_shard)
    qkv_near, layer_in, encoded = hold(qkv_near, layer_in, encoded)
    x_bf, enc_bf = deal([layer_in, encoded])

    def places_of(pairing):
        group = o * 2 + y
        spots = []
        for step in range(groups):
            source = lax.rem(group - step + groups, groups)
            for flip in range(2):
                c = core if flip == 0 else 1 - core
                k = 2 * lax.rem(z, 2) + c
                for r in range(LINE):
                    line = lax.rem(r - k + LINE, LINE)
                    spots.append((((source // 2) * LINE + line) * 2 + lax.rem(source, 2)) * 2 + c)
        spans = jnp.take(pairing.reshape(-1), jnp.stack(spots), axis=0)
        return (spans[:, None] * half + jnp.arange(half, dtype=jnp.int32)[None, :]).reshape(-1, 1)

    product = 2 * rows * width * width
    square = (width, width)
    act, real = ((rows, width), BF), ((rows, width), F32)
    turned = pltpu.VMEM((width, rows), BF)

    def weights(n):
        return pltpu.VMEM((n,) + square, BF)

    def grads(n):
        return [((2, n, shard, width), BF)] * 2

    note = ((16, width), F32)

    x_bf, enc_bf, qkv_other, qkv_near, attn_weight, out_weight, up_weight, out_cotangent, pairing = hold(
        x_bf, enc_bf, qkv_other, qkv_near, attn_weight, out_weight, up_weight, out_cotangent, pairing
    )
    pair_shard = attn_weight[4:]
    key_places = places_of(pairing)
    mid_shard = jnp.concatenate([attn_weight[4:], attn_weight[3:4], out_weight], axis=0)
    rest_shard = jnp.concatenate([attn_weight[3:4], out_weight], axis=0)
    w_qkv = (qkv_shard, qkv_near, qkv_other, between_cores(qkv_other))
    pair_other = lax.ppermute(pair_shard, "fx", SWAP)
    mid_near = between_cores(mid_shard)
    extra = ROWS_CUT
    n1, query, kv, vec = dense(
        self_in_kernel,
        [slots],
        [x_bf],
        w_qkv,
        [act, act, ((2, rows, width), BF), ((TABLE, width), F32)],
        [weights(3), pltpu.VMEM((4, extra, width), BF)],
        4,
        copies=16,
    )
    n1, query, kv, vec, up_weight, key_places, out_cotangent = hold(
        n1, query, kv, vec, up_weight, key_places, out_cotangent
    )
    places = (key_places, key_places[:rows].reshape(1, -1))
    kv_self = to_others(kv, groups)
    near_self = between_cores(kv)
    up_cut = up_weight.reshape(shard, 4, width).transpose(1, 0, 2)
    cot_halves = deal_halves(out_cotangent)
    pair_other, rest_shard, mid_near = hold(pair_other, rest_shard, mid_near)
    rest_other = lax.ppermute(rest_shard, "fx", SWAP)
    w_pair = (mid_shard, mid_near, pair_other, between_cores(pair_other))
    (kv,) = dense(
        cross_in_kernel, [slots], [vec, enc_bf], w_pair, [((2, enc_rows, width), BF)], [weights(2)], 3.5
    )
    kv_self, near_self, kv, cot_halves, up_cut = hold(kv_self, near_self, kv, cot_halves, up_cut)
    cot = deal_line(*cot_halves)
    kv_cross = to_others(kv, groups)
    near_cross = between_cores(kv)
    kv_self = [kv_self[0], near_self] + with_cores(kv_self[1:])
    mixed, mass = attention(query, kv_self, places)
    mixed, mass, up_cut, rest_other, kv_cross, near_cross, cot = hold(
        mixed, mass, up_cut, rest_other, kv_cross, near_cross, cot
    )
    w_rest = (mid_shard, mid_near, rest_other, between_cores(rest_other))
    kv_cross = [kv_cross[0], near_cross] + with_cores(kv_cross[1:])
    r1, n2, cquery = dense(middle_kernel, [slots], [vec, mixed, x_bf], w_rest, [real, act, act], [weights(2)], 3.3)
    r1, n2, cquery, kv_cross, up_cut = hold(r1, n2, cquery, kv_cross, up_cut)
    up_own = lax.all_to_all(up_cut, ("fx", "core"), 0, 0, tiled=True).reshape(width, width)
    cot_other = lax.ppermute(cot, "fx", SWAP)
    cot_near = between_cores(cot)
    cmixed, cmass = attention(cquery, kv_cross, None)
    cmixed, cmass, cot_other, cot_near = hold(cmixed, cmass, cot_other, cot_near)
    r2, n3 = dense(before_feed_kernel, [slots], [vec, cmixed, r1], w_rest, [real, act], [weights(1)], 2.7)
    r2, n3, cot_other = hold(r2, n3, cot_other)
    n3_other = lax.ppermute(n3, "fx", SWAP)
    cots = (cot, cot_near, cot_other, between_cores(cot_other))
    n3s = (n3, between_cores(n3), n3_other, between_cores(n3_other))
    pair = ((2, rows, width), BF)
    four = ((4, rows, width), BF)
    dn_keep, dn_send, out_keep, out_send, hidden_act, dpre, up_rows = dense(
        feed_kernel,
        [],
        [vec, up_own, down_weight] + list(n3s) + list(cots),
        [],
        [pair, pair, pair, pair, four, four, ((8, width), F32)],
        [],
        8,
    )

    single = outer == 1

    def step(terms, name):
        return halve(terms, name) if single else terms

    def hold_all(*values):
        flat = hold([[term[0] for term in v] if isinstance(v, list) else v for v in values])[0]
        return [
            [(array, term[1]) for array, term in zip(new, old)] if isinstance(old, list) else new
            for new, old in zip(flat, values)
        ]

    dn_got = between_cores(dn_send)
    dn_keep, dn_got, hidden_act, dpre = hold(dn_keep, dn_got, hidden_act, dpre)
    dn_far = lax.ppermute(add([dn_keep[1], dn_got[1]]), "fx", SWAP)
    cut = ((4, 2, 4, shard // 4, width // 2), BF)
    up, down = dense(feed_grad_kernel, [], [hidden_act, dpre] + list(n3s) + list(cots), [], [cut, cut], [], 6)
    dn_far, up, down, out_keep, out_send = hold(dn_far, up, down, out_keep, out_send)
    up, down = ([(part.reshape((2, 2, 2) + part.shape[2:]), ())] for part in (up, down))
    up, down = step(up, "y"), step(down, "z0")
    out_got = between_cores(out_send)
    dr2, doc, ffn_rows = dense(
        after_feed_kernel, [slots], [vec, dn_keep, dn_got, dn_far, r2, cot], w_rest, [real, act, note], [weights(1)], 2.7
    )

    dcq, cmine, ctheirs = attention_back(cquery, doc, cmixed, cmass, kv_cross, None)
    dcq, cmine, ctheirs, dr2, ffn_rows, out_keep, out_got, up, down = hold_all(
        dcq, cmine, ctheirs, dr2, ffn_rows, out_keep, out_got, up, down
    )
    cgot = between_cores(ctheirs)
    dr1, dos, middle_keep, middle_send, mid_rows = dense(
        middle_back_kernel,
        [slots],
        [vec, dcq, n2, r1, dr2, mixed, cmixed],
        w_rest,
        [real, act] + grads(3) + [note],
        [weights(2), turned],
        6,
    )
    dr1, dos, middle_keep, middle_send, mid_rows, cgot, cmine, up, down, out_keep, out_got = hold_all(
        dr1, dos, middle_keep, middle_send, mid_rows, cgot, cmine, up, down, out_keep, out_got
    )
    dckv = collect(cmine, cgot, groups)
    middle = over_cores(middle_keep, middle_send)
    up, down = step(up, "z0"), step(down, "z1")
    out_far = lax.ppermute(add([out_keep[1], out_got[1]]), "fx", SWAP)
    dq, mine, theirs = attention_back(query, dos, mixed, mass, kv_self, places)
    dq, mine, theirs, middle, up, down, out_far, dckv_a = hold_all(dq, mine, theirs, middle, up, down, out_far, dckv[-1])
    dckv = dckv[:-1] + [dckv_a]
    got = between_cores(theirs)
    middle_a = part_over_x(middle, 0, 1)
    grad_encoded, layer_out, late_keep, late_send, enc_rows_sum = dense(
        functools.partial(cross_back_kernel, len(dckv)),
        [slots],
        [vec, enc_bf, n1, dq, r2, out_keep, out_got, out_far] + dckv,
        w_pair,
        [((enc_rows, width), BF), act] + grads(3) + [note],
        [weights(2), turned, pltpu.VMEM((width, enc_rows), BF)],
        6,
    )
    mine, got, grad_encoded, layer_out, late_keep, late_send, enc_rows_sum, up, down, middle, middle_a = hold_all(
        mine, got, grad_encoded, layer_out, late_keep, late_send, enc_rows_sum, up, down, middle, middle_a
    )
    dkv = collect(mine, got, groups)
    late = over_cores(late_keep, late_send)
    late, up, down, middle = hold_all(late, up, down, middle)
    middle_b = part_over_x(middle, 1, 3)
    if single:
        up, down = both_halves(up, "z1"), both_halves(down, "y")
        dkv_last, up, down, late, middle_b = hold(dkv[-1], up, down, [t[0] for t in late], middle_b)
        late = [(array, ()) for array in late]
    else:
        dkv_last, late, middle_b = hold_all(dkv[-1], late, middle_b)
    dkv = dkv[:-1] + [dkv_last]
    middle = [(array, (0,)) for array, _ in middle] + [(jnp.concatenate([middle_a, middle_b], axis=0), ())]
    late_a = part_over_x(late, 0, 1)
    if single:
        up, down = add(up), add(down)
        up = lax.all_to_all(up, ("fx", "core"), 1, 1, tiled=True)
    grad_layer, keep, send = dense(
        functools.partial(self_back_kernel, len(dkv)),
        [slots],
        [vec, x_bf, n1, dq, dr1, up_rows, ffn_rows, mid_rows, enc_rows_sum] + dkv,
        w_qkv,
        [act] + [((2, 2 * shard + ROWS_SUM, width), BF)] * 2,
        [weights(3), turned],
        7,
        copies=12,
    )
    grad_layer, keep, send, middle, late, late_a, up, down = hold_all(
        grad_layer, keep, send, middle, late, late_a, up, down
    )
    own = over_cores(keep, send)
    late_b = part_over_x(late, 1, 3)
    if single:
        up, down = double(up, "z0"), double(down, "z1")
        middle = halve(middle, "y")
        own, up, down, middle, late, late_b = hold_all(own, up, down, middle, late, late_b)
    late = [(array, (0,)) for array, _ in late] + [(jnp.concatenate([late_a, late_b], axis=0), ())]
    if single:
        own = add([half_of(term) for term in own])
        own = jnp.where(fx == 0, own, own[::-1]).reshape(4 * LINE, -1, width)
        own = lax.all_to_all(own, ("fx", "z", "y"), 0, 0, tiled=True)
        up, down = double(up, "y"), double(down, "z0")
        late, middle = halve(late, "y"), halve(middle, "z0")
        late, middle, up, down, grad_layer = hold_all(late, middle, up, down, grad_layer)
        late, middle = halve(late, "z0"), both_halves(middle, "z1")
        late, middle = hold_all(late, [(part, ()) for part in middle])
        middle = [part for part, _ in middle]
        late, middle = both_halves(late, "z1"), double(add(middle), "z0")
        own, late, middle = hold(own, late, middle)
        own = jnp.sum(own.astype(F32), axis=0, keepdims=True).astype(BF)
        own = lax.all_to_all(jnp.broadcast_to(own, (2 * LINE,) + own.shape[1:]), ("z", "y"), 0, 0, tiled=True)
        late, middle = double(add(late), "z0"), double(middle, "y")
        late, middle, grad_layer, grad_encoded, layer_out = hold(late, middle, grad_layer, grad_encoded, layer_out)
        late = double(late, "y")
        grad_encoded, layer_out, grad_layer = undeal([grad_encoded, layer_out, grad_layer], [F32, BF, F32])
        grad_attn, grad_out, *total = dense(
            last_kernel,
            [],
            [part.reshape(-1, width) for part in (late, middle, own)],
            [],
            [((6, shard, width), F32), ((2, shard, width), F32), ((3, shard), F32), ((9, shard), F32)]
            + [((1, blocks * shard), F32), ((1, shard), F32)],
            [],
            3,
        )
        up, down = (part.astype(F32).reshape(2, 2, 2, 4, shard // 4, width // 2) for part in (up, down))
    else:
        (grad_layer,) = undeal([grad_layer], [F32])
        (grad_encoded,), (layer_out,) = undeal([grad_encoded], [F32]), undeal([layer_out], [BF])

        def over_ctx(terms, n):
            total = add([array[0] if 0 in names else array for array, names in terms])
            return lax.psum(total, ("o", "z", "y")).astype(F32).reshape(n, -1, width)

        own, middle, late = over_ctx(over_x(own), 1)[0], over_ctx(middle, 3), over_ctx(late, 3)
        up, down = (lax.psum(part[0][0], ("o", "z", "y")).astype(F32) for part in (up, down))
        up = lax.all_to_all(up.astype(BF), ("fx", "core"), 3, 3, tiled=True).astype(F32)
        total = own[2 * shard : 2 * shard + 5].reshape(-1, shard)
        total = [total[:3], total[3:12], total[13 : 13 + blocks].reshape(1, -1), total[12:13]]
        own = own[: 2 * shard].reshape(2, shard, width)
        grad_attn = jnp.concatenate([late[2:], own, middle[:1], late[:2]], axis=0)
        grad_out = middle[1:]
    g_up = up.transpose(0, 1, 4, 3, 2, 5).reshape(shard, hidden)
    g_down = down.transpose(3, 0, 1, 4, 2, 5).reshape(hidden // 4, width)
    return (
        layer_out,
        grad_layer,
        grad_encoded,
        grad_attn,
        grad_out,
        g_up,
        g_down,
        total[0],
        total[1],
        total[2].reshape(-1),
        total[3].reshape(-1),
    )


def solution(mesh):
    ctx = mesh.shape["ctx"]
    grid = Mesh(mesh.devices.reshape(2, 2, ctx // (2 * LINE), LINE, 2), ("fx", "core", "o", "z", "y"))
    fsdp = ("fx", "core")
    rows = P(fsdp, ("o", "z", "y"), None)
    weights = (
        P(None, fsdp, None),
        P(None, fsdp, None),
        P(fsdp, None),
        P(fsdp, None),
        P(None, fsdp),
        P(None, fsdp),
        P(fsdp),
        P(fsdp),
    )
    return jax.shard_map(
        per_device,
        mesh=grid,
        in_specs=(rows, rows, P()) + weights + (rows,),
        out_specs=(rows, rows, rows) + weights,
        check_vma=False,
    )
```

```python
import functools
import math

import jax
import jax.numpy as jnp
from jax import lax
from jax.experimental import pallas as pl
from jax.experimental.pallas import tpu as pltpu
from jax.sharding import Mesh
from jax.sharding import PartitionSpec as P

HEADS = 12
HD = 64
PAIR = 2 * HD
SCORE_SCALE = 0.125
MASK_FILL = -1e30
NORM_EPSILON = 1e-05
LINE = 4
SWAP = [(0, 1), (1, 0)]
BF = jnp.bfloat16
F32 = jnp.float32
MIB = 1 << 20


def dot(left, right):
    return jnp.dot(left, right, preferred_element_type=F32)


def dot_t(left, right):
    return lax.dot_general(left, right, (((1,), (1,)), ((), ())), preferred_element_type=F32)


def t_dot(left, right):
    return lax.dot_general(left, right, (((0,), (0,)), ((), ())), preferred_element_type=F32)


def split_heads(block):
    lane = lax.broadcasted_iota(jnp.int32, block.shape, 1)
    zero = jnp.zeros_like(block)
    return jnp.concatenate([jnp.where(lane < HD, block, zero), jnp.where(lane < HD, zero, block)], axis=0)


def join_heads(columns):
    rows = columns.shape[1] // 2
    return jnp.concatenate([columns[:HD, :rows], columns[HD:, rows:]], axis=0).T


def forward_kernel(masked, pieces, *refs):
    if masked:
        key_place_ref, query_place_ref, refs = refs[0], refs[1], refs[2:]
    query_ref, kv_refs = refs[0], refs[1 : 1 + pieces]
    out_ref, mass_ref, scores_ref = refs[1 + pieces :]
    query = split_heads(query_ref[...] * jnp.asarray(SCORE_SCALE, BF))
    piece = kv_refs[0].shape[1]
    if masked:
        query_place = query_place_ref[...]
        query_place = jnp.concatenate([query_place, query_place], axis=1)
    top = None
    for i in range(pieces):
        scores = dot_t(kv_refs[i][0], query)
        if masked:
            scores = jnp.where(key_place_ref[pl.ds(i * piece, piece), :] <= query_place, scores, MASK_FILL)
        scores_ref[pl.ds(i * piece, piece), :] = scores
        high = jnp.max(scores, axis=0, keepdims=True)
        top = high if top is None else jnp.maximum(top, high)
    mass = jnp.zeros_like(top)
    mixed = None
    for i in range(pieces):
        probs = jnp.exp(scores_ref[pl.ds(i * piece, piece), :] - top)
        mass = mass + jnp.sum(probs, axis=0, keepdims=True)
        part = t_dot(kv_refs[i][1], probs.astype(BF))
        mixed = part if mixed is None else mixed + part
    out_ref[...] = join_heads(mixed * (1.0 / mass)).astype(BF)
    mass_ref[0] = top + jnp.log(mass)


def backward_kernel(masked, pieces, *refs):
    if masked:
        key_place_ref, query_place_ref, refs = refs[0], refs[1], refs[2:]
    query_ref, dout_ref, out_ref, mass_ref = refs[:4]
    kv_refs = refs[4 : 4 + pieces]
    dquery_ref, mine_ref, theirs_ref = refs[4 + pieces :]
    query = split_heads(query_ref[...] * jnp.asarray(SCORE_SCALE, BF))
    dout = dout_ref[...]
    prod = (dout.astype(F32) * out_ref[...].astype(F32)).T
    delta = jnp.concatenate(
        [jnp.sum(prod[:HD], axis=0, keepdims=True), jnp.sum(prod[HD:], axis=0, keepdims=True)], axis=1
    )
    dout = split_heads(dout)
    log_mass = mass_ref[0]
    piece = kv_refs[0].shape[1]
    if masked:
        query_place = query_place_ref[...]
        query_place = jnp.concatenate([query_place, query_place], axis=1)
    dquery = None
    for i in range(pieces):
        keys = kv_refs[i][0]
        scores = dot_t(keys, query)
        if masked:
            scores = jnp.where(key_place_ref[pl.ds(i * piece, piece), :] <= query_place, scores, MASK_FILL)
        probs = jnp.exp(scores - log_mass)
        dprobs = dot_t(kv_refs[i][1], dout)
        dscores = (probs * (dprobs - delta)).astype(BF)
        dkv_ref = theirs_ref if i % 2 else mine_ref
        dkv_ref[i // 2, 0] = dot(dscores, query).astype(BF)
        dkv_ref[i // 2, 1] = dot(probs.astype(BF), dout).astype(BF)
        part = t_dot(keys, dscores)
        dquery = part if dquery is None else dquery + part
    dquery_ref[...] = (join_heads(dquery) * SCORE_SCALE).astype(BF)


def place_specs(masked, places):
    if not masked:
        return [], []
    key_places, query_places = places
    return [key_places, query_places], [
        pl.BlockSpec(key_places.shape, lambda h: (0, 0)),
        pl.BlockSpec(query_places.shape, lambda h: (0, 0)),
    ]


def attention(query, kv, places):
    masked = places is not None
    rows, width = query.shape
    piece = kv[0].shape[1]
    extra, extra_specs = place_specs(masked, places)
    keys = piece * len(kv)
    return pl.pallas_call(
        functools.partial(forward_kernel, masked, len(kv)),
        grid=(width // PAIR,),
        in_specs=extra_specs
        + [pl.BlockSpec((rows, PAIR), lambda h: (0, h))]
        + [pl.BlockSpec((2, piece, PAIR), lambda h: (0, 0, h))] * len(kv),
        out_specs=[
            pl.BlockSpec((rows, PAIR), lambda h: (0, h)),
            pl.BlockSpec((1, 1, 2 * rows), lambda h: (h, 0, 0)),
        ],
        out_shape=[
            jax.ShapeDtypeStruct((rows, width), BF),
            jax.ShapeDtypeStruct((width // PAIR, 1, 2 * rows), F32),
        ],
        scratch_shapes=[pltpu.VMEM((keys, 2 * rows), F32)],
        compiler_params=pltpu.CompilerParams(vmem_limit_bytes=60 * MIB),
        cost_estimate=cost(8 * rows * keys / 2**18),
    )(*extra, query, *kv)


def attention_back(query, dout, out, mass, kv, places):
    masked = places is not None
    rows, width = query.shape
    piece = kv[0].shape[1]
    extra, extra_specs = place_specs(masked, places)
    keys = piece * len(kv)
    column = pl.BlockSpec((rows, PAIR), lambda h: (0, h))
    pair = pl.BlockSpec((2, piece, PAIR), lambda h: (0, 0, h))
    groups = len(kv) // 2
    blocks = pl.BlockSpec((groups, 2, piece, PAIR), lambda h: (0, 0, 0, h))
    return pl.pallas_call(
        functools.partial(backward_kernel, masked, len(kv)),
        grid=(width // PAIR,),
        in_specs=extra_specs
        + [column, column, column, pl.BlockSpec((1, 1, 2 * rows), lambda h: (h, 0, 0))]
        + [pair] * len(kv),
        out_specs=[column, blocks, blocks],
        out_shape=[jax.ShapeDtypeStruct((rows, width), BF)]
        + [jax.ShapeDtypeStruct((groups, 2, piece, width), BF)] * 2,
        compiler_params=pltpu.CompilerParams(vmem_limit_bytes=60 * MIB),
        cost_estimate=cost(13 * rows * keys / 2**18),
    )(*extra, query, dout, out, mass, *kv)


def deal_perms():
    perms = []
    for r in range(LINE):
        perm = []
        for c in range(2):
            for z in range(LINE):
                k = (r - z) % LINE
                perm.append((c * LINE + z, (k % 2) * LINE + 2 * c + k // 2))
        perms.append(perm)
    return perms


DEAL = deal_perms()


def deal(arrays):
    if len({array.shape for array in arrays}) > 1:
        return [deal([array])[0] for array in arrays]
    _, rows, width = arrays[0].shape
    chunks = [array.reshape(LINE, rows // 2, width) for array in arrays]
    z = lax.axis_index("z")
    got = []
    for r in range(LINE):
        k = lax.rem(r - z + LINE, LINE)
        chunk = jnp.stack([lax.dynamic_index_in_dim(c, k, keepdims=False) for c in chunks])
        got.append(lax.ppermute(chunk, ("core", "z"), DEAL[r]))
    return [jnp.concatenate([g[i] for g in got], axis=0) for i in range(len(arrays))]


def undeal_line(arrays):
    core, z = lax.axis_index("core"), lax.axis_index("z")
    chunks = jnp.stack([array.reshape(LINE, -1, array.shape[-1]) for array in arrays], axis=1)
    start = lax.rem(2 * lax.rem(z, 2) + core, LINE)
    chunks = lax.dynamic_slice_in_dim(jnp.concatenate([chunks, chunks], axis=0), start, LINE, axis=0)
    return lax.all_to_all(chunks, "z", 0, 0, tiled=True)


def undeal_cores(chunks):
    core = lax.axis_index("core")
    chunks = chunks.reshape((2, 2) + chunks.shape[1:])
    mine = lax.dynamic_index_in_dim(chunks, core, 0, keepdims=False)
    return mine, lax.ppermute(lax.dynamic_index_in_dim(chunks, 1 - core, 0, keepdims=False), "core", SWAP)


def undealt(halves, kinds):
    first = lax.axis_index("core") == 0
    outs = []
    for i, kind in enumerate(kinds):
        mine, got = (half[:, i].astype(kind) for half in halves)
        both = jnp.where(first, jnp.stack([mine, got], axis=1), jnp.stack([got, mine], axis=1))
        outs.append(both.reshape(2, -1, both.shape[-1]))
    return outs


def deal_halves(array):
    _, rows, width = array.shape
    parts = array.reshape(2, 2, rows // 2, width)
    core = lax.axis_index("core")
    mine = lax.dynamic_index_in_dim(parts, core, 1, keepdims=False)
    return mine, lax.ppermute(lax.dynamic_index_in_dim(parts, 1 - core, 1, keepdims=False), "core", SWAP)


def deal_line(mine, got):
    first = lax.axis_index("core") == 0
    chunks = jnp.where(first, jnp.concatenate([mine, got], axis=0), jnp.concatenate([got, mine], axis=0))
    return lax.all_to_all(chunks, "z", 0, 0, tiled=True)


def deal_order(chunks):
    core, z = lax.axis_index("core"), lax.axis_index("z")
    start = lax.rem(LINE - 2 * lax.rem(z, 2) - core, LINE)
    mine = lax.dynamic_slice_in_dim(jnp.concatenate([chunks, chunks], axis=0), start, LINE, axis=0)
    return mine.reshape(-1, mine.shape[-1])


def undeal(arrays, kind):
    count = len(arrays)
    half = arrays[0].shape[0] // LINE
    got = []
    for r in range(LINE):
        chunk = jnp.stack([array[r * half : (r + 1) * half] for array in arrays])
        got.append(lax.ppermute(chunk, ("core", "z"), [(b, a) for a, b in DEAL[r]]))
    z = lax.axis_index("z")
    outs = []
    for i in range(count):
        mine = lax.dynamic_slice_in_dim(jnp.stack([g[i] for g in got + got]), z, LINE, axis=0)
        outs.append(mine.reshape(2, 2 * half, arrays[0].shape[1]).astype(kind[i]))
    return outs


def group_perm(groups, step):
    return [(i, (i + step) % groups) for i in range(groups)]


def to_others(own, groups):
    return [own] + [lax.ppermute(own, ("o", "y"), group_perm(groups, step)) for step in range(1, groups)]


def with_cores(blocks):
    pieces = []
    for block in blocks:
        pieces += [block, lax.ppermute(block, "core", SWAP)]
    return pieces


def collect(mine, got, groups):
    terms = [mine, got]
    for step in range(1, groups):
        back = [(b, a) for a, b in group_perm(groups, step)]
        terms.append(lax.ppermute(add([mine[step], got[step]]), ("o", "y"), back))
    return terms


def between_cores(array):
    return lax.ppermute(array, "core", SWAP)


def gather(own, other):
    return own, lax.ppermute(own, "core", SWAP), other, lax.ppermute(other, "core", SWAP)


def after(value, earlier):
    return lax.optimization_barrier((value, earlier))[0]


def add(terms):
    total = terms[0].astype(F32)
    for term in terms[1:]:
        total = total + term.astype(F32)
    return total.astype(BF)


def over_cores(keep, send):
    return [(keep, ()), (lax.ppermute(send, "core", SWAP), ())]


def over_x(terms):
    got = lax.ppermute(add([array[1] for array, _ in terms]), "fx", SWAP)
    return [(array, (0,)) for array, _ in terms] + [(got, ())]


def part_over_x(terms, first, last):
    return lax.ppermute(add([array[1, first:last] for array, _ in terms]), "fx", SWAP)


def pick(array, *path):
    for axis, index in path:
        array = lax.dynamic_index_in_dim(array, index, axis, keepdims=False)
    return array


HALVES = ("y", "z0", "z1")


def exchange(array, name):
    if name == "y":
        return lax.ppermute(array, "y", SWAP)
    flip = 1 if name == "z0" else 2
    return lax.ppermute(array, "z", [(i, i ^ flip) for i in range(LINE)])


def half_index(name):
    z = lax.axis_index("z")
    return lax.axis_index("y") if name == "y" else lax.rem(z, 2) if name == "z0" else lax.div(z, 2)


def half_of(term, more=()):
    array, names = term
    cut = 1 in names
    if 0 in names and 1 not in names and len(names + more) > 1:
        array = array.reshape(2, 2, 2, 2, -1, array.shape[-1])
        cut = True
    for name in names + more:
        if name in (0, 1):
            array = array if name else array[0]
            continue
        if name[0] == "at":
            array = pick(array, name[1:])
            continue
        name, other = name if isinstance(name, tuple) else (name, False)
        if array.ndim == 3 and not cut:
            array = array.reshape(2, 2, 2, -1, array.shape[-1])
        cut = True
        i = half_index(name)
        array = lax.dynamic_index_in_dim(array, 1 - i if other else i, 0, keepdims=False)
    return array


def halve(terms, name):
    theirs = add([half_of(term, ((name, True),)) for term in terms])
    got = exchange(theirs, name)
    return [(array, names + (name,)) for array, names in terms] + [(got, (1,))]


def both_halves(terms, name):
    mine = add([half_of(term) for term in terms])
    got = exchange(mine, name)
    mine = lax.optimization_barrier(mine)
    return mine, got


def double(part, name):
    other = exchange(part, name)
    first = half_index(name) == 0
    return jnp.where(first, jnp.concatenate([part, other], axis=0), jnp.concatenate([other, part], axis=0))


def standard(values):
    center = values - jnp.mean(values, axis=-1, keepdims=True)
    inverse = lax.rsqrt(jnp.mean(center * center, axis=-1, keepdims=True) + NORM_EPSILON)
    return center * inverse, inverse


def norm_back(dnormed, values, gain):
    z, inverse = standard(values)
    a = dnormed * gain
    dvalues = (
        a - jnp.mean(a, axis=-1, keepdims=True) - z * jnp.mean(a * z, axis=-1, keepdims=True)
    ) * inverse
    return dvalues, jnp.sum(dnormed * z, axis=0, keepdims=True), jnp.sum(dnormed, axis=0, keepdims=True)


def column_sum(values):
    return jnp.sum(values.astype(F32), axis=0, keepdims=True)


GAIN, BIAS, UP, DOWN = 0, 3, 12, 13
TABLE = 24
PAIR_AT, REST_AT, LAST_AT = (0, 0, 0, 0), (2, 2, 0, 0), (4, 4, 2, 2)


def vector(vec_ref, row):
    return vec_ref[row : row + 1, :]


def start_packed(pieces, slot_ref, full_ref, sems):
    n, rows = full_ref.shape[0], full_ref.shape[1] // 4
    copies = []
    for j, piece in enumerate(pieces):
        place = pl.ds(pl.multiple_of(slot_ref[j] * rows, rows), rows)
        for i in range(n):
            copy = pltpu.make_async_copy(
                piece.at[pl.ds(i * rows, rows), :], full_ref.at[i, place, :], sems.at[j * n + i]
            )
            copy.start()
            copies.append(copy)
    return copies


def start_copies(pieces, firsts, slot_ref, full_ref, sems, base):
    copies = []
    for j, piece in enumerate(pieces):
        rows = piece.shape[-2]
        place = pl.ds(pl.multiple_of(slot_ref[j] * rows, rows), rows)
        if len(piece.shape) == 3:
            source, target = piece.at[pl.ds(firsts[j], full_ref.shape[0])], full_ref.at[:, place, :]
        else:
            source, target = piece, full_ref.at[place, :]
        copy = pltpu.make_async_copy(source, target, sems.at[base + j])
        copy.start()
        copies.append(copy)
    return copies


def wait_all(copies):
    for copy in copies:
        copy.wait()


def put_grad(unit, turned, right, slot_ref, keep_ref, send_ref):
    rows = turned.shape[0] // 4
    for j in range(4):
        place = pl.ds(pl.multiple_of(slot_ref[j] * rows, rows), rows)
        block = dot(turned[place, :], right).astype(BF)
        target = send_ref if j % 2 else keep_ref
        target[j // 2, unit] = block


def self_in_kernel(ready, slot_ref, x_ref, *refs):
    pieces, (n_ref, query_ref, kv_ref, vec_ref, full_ref, parts_ref, sems) = refs[:4], refs[4:]
    weights, shard = full_ref.shape[0], full_ref.shape[1] // 4
    extra = parts_ref.shape[1]
    small = []
    for j, piece in enumerate(pieces):
        copy = pltpu.make_async_copy(
            piece.at[pl.ds(weights * shard, extra), :], parts_ref.at[j], sems.at[4 * weights + j]
        )
        copy.start()
        small.append(copy)
    copies = start_packed(pieces, slot_ref, full_ref, sems)
    ready()
    z = standard(x_ref[...].astype(F32))[0]
    wait_all(small)
    parts = [parts_ref[lax.bitwise_xor(slot_ref[0], p)].astype(F32)[:, :shard] for p in range(4)]
    own = parts_ref[0].astype(F32)[:, :shard]
    table = jnp.concatenate(parts, axis=1)
    vec_ref[0:UP, :] = table[0:UP]
    vec_ref[UP:DOWN, :] = jnp.concatenate([own[UP + i : UP + i + 1] for i in range(4)], axis=1)
    vec_ref[DOWN : DOWN + 1, :] = table[UP + 4 : UP + 5]
    normed = (z * table[GAIN : GAIN + 1] + table[BIAS + 6 : BIAS + 7]).astype(BF)
    n_ref[...] = normed
    wait_all(copies)
    kv_ref[0] = dot(normed, full_ref[1]).astype(BF)
    kv_ref[1] = (dot(normed, full_ref[2]) + table[BIAS + 1 : BIAS + 2]).astype(BF)
    query_ref[...] = (dot(normed, full_ref[0]) + table[BIAS : BIAS + 1]).astype(BF)


def cross_in_kernel(ready, slot_ref, vec_ref, enc_ref, *refs):
    pieces, (kv_ref, full_ref, sems) = refs[:4], refs[4:]
    copies = start_copies(pieces, PAIR_AT, slot_ref, full_ref, sems, 0)
    ready()
    enc = enc_ref[...]
    wait_all(copies)
    kv_ref[0] = dot(enc, full_ref[0]).astype(BF)
    kv_ref[1] = (dot(enc, full_ref[1]) + vector(vec_ref, BIAS + 4)).astype(BF)


def middle_kernel(ready, slot_ref, vec_ref, mixed_ref, x_ref, *refs):
    pieces, (res_ref, n_ref, query_ref, full_ref, sems) = refs[:4], refs[4:]
    copies = start_copies(pieces, REST_AT, slot_ref, full_ref, sems, 0)
    ready()
    wait_all(copies)
    res = x_ref[...].astype(F32) + dot(mixed_ref[...], full_ref[1]) + vector(vec_ref, BIAS + 2)
    res_ref[...] = res
    normed = (standard(res)[0] * vector(vec_ref, GAIN + 1) + vector(vec_ref, BIAS + 7)).astype(BF)
    n_ref[...] = normed
    query_ref[...] = (dot(normed, full_ref[0]) + vector(vec_ref, BIAS + 3)).astype(BF)


def before_feed_kernel(ready, slot_ref, vec_ref, mixed_ref, res_ref, *refs):
    pieces, (out_ref, n_ref, full_ref, sems) = refs[:4], refs[4:]
    copies = start_copies(pieces, LAST_AT, slot_ref, full_ref, sems, 0)
    ready()
    wait_all(copies)
    res = res_ref[...] + dot(mixed_ref[...], full_ref[0]) + vector(vec_ref, BIAS + 5)
    out_ref[...] = res
    n_ref[...] = (standard(res)[0] * vector(vec_ref, GAIN + 2) + vector(vec_ref, BIAS + 8)).astype(BF)


def feed_kernel(ready, vec_ref, up_ref, down_ref, *refs):
    normed_refs, cot_refs = refs[:4], refs[4:8]
    dn_keep, dn_send, out_keep, out_send, act_ref, dpre_ref, rows_ref = refs[8:]
    ready()
    bias = vector(vec_ref, UP)
    total = None
    for j in (1, 3, 0, 2):
        pre = dot(normed_refs[j][...], up_ref[...]) + bias
        phi = 0.5 * (1.0 + lax.erf(pre * math.sqrt(0.5)))
        slope = phi + pre * (jnp.exp(-0.5 * pre * pre) * (1.0 / math.sqrt(2.0 * math.pi)))
        act = (pre * phi).astype(BF)
        dpre = (dot_t(cot_refs[j][...], down_ref[...]) * slope).astype(BF)
        out, dn = (out_send, dn_send) if j % 2 else (out_keep, dn_keep)
        dn[j // 2] = dot_t(dpre, up_ref[...]).astype(BF)
        out[j // 2] = dot(act, down_ref[...]).astype(BF)
        act_ref[j] = act
        dpre_ref[j] = dpre
        sums = column_sum(dpre)
        total = sums if total is None else total + sums
    rows_ref[0:1, :] = total


def feed_grad_kernel(ready, act_ref, dpre_ref, *refs):
    normed_refs, cot_refs, (up_ref, down_ref) = refs[:4], refs[4:8], refs[8:]
    quarter, half = up_ref.shape[-2:]
    ready()

    def put(grad, cut_ref):
        for p in range(4):
            for q in range(4):
                rows = grad[(4 * p + q) * quarter : (4 * p + q + 1) * quarter].astype(BF)
                cut_ref[q, 0, p] = rows[:, :half]
                cut_ref[q, 1, p] = rows[:, half:]

    total = None
    for j in range(4):
        part = t_dot(normed_refs[j][...], dpre_ref[j])
        total = part if total is None else total + part
    put(total, up_ref)
    total = None
    for j in range(4):
        part = t_dot(act_ref[j], cot_refs[j][...])
        total = part if total is None else total + part
    put(total, down_ref)


def after_feed_kernel(ready, slot_ref, vec_ref, dn_ref, dn_near_ref, dn_far_ref, res_ref, cot_ref, *refs):
    pieces, (dres_ref, dout_ref, rows_ref, full_ref, sems) = refs[:4], refs[4:]
    copies = start_copies(pieces, LAST_AT, slot_ref, full_ref, sems, 0)
    ready()
    dn = dn_ref[0].astype(F32) + dn_near_ref[0].astype(F32) + dn_far_ref[...].astype(F32)
    cot = cot_ref[...].astype(F32)
    dvalues, dgain, dshift = norm_back(dn, res_ref[...], vector(vec_ref, GAIN + 2))
    dres = cot + dvalues
    dres_ref[...] = dres
    branch = dres.astype(BF)
    wait_all(copies)
    dout_ref[...] = dot_t(branch, full_ref[0]).astype(BF)
    rows_ref[0:1, :] = dgain
    rows_ref[1:2, :] = dshift
    rows_ref[2:3, :] = column_sum(branch)
    rows_ref[3:4, :] = column_sum(cot)


def middle_back_kernel(ready, slot_ref, vec_ref, dquery_ref, n_ref, res_ref, dres_ref, mixed_ref, cmixed_ref, *refs):
    pieces, (dout_res_ref, dout_ref, keep_ref, send_ref, rows_ref, full_ref, turned_ref, sems) = refs[:4], refs[4:]
    copies = start_copies(pieces, REST_AT, slot_ref, full_ref, sems, 0)
    ready()
    turned_ref[...] = n_ref[...].T
    dquery = dquery_ref[...]
    put_grad(0, turned_ref, dquery, slot_ref, keep_ref, send_ref)
    wait_all(copies)
    dn = dot_t(dquery, full_ref[0])
    dvalues, dgain, dshift = norm_back(dn, res_ref[...], vector(vec_ref, GAIN + 1))
    turned_ref[...] = cmixed_ref[...].T
    put_grad(2, turned_ref, dres_ref[...].astype(BF), slot_ref, keep_ref, send_ref)
    dres = dres_ref[...] + dvalues
    dout_res_ref[...] = dres
    branch = dres.astype(BF)
    dout_ref[...] = dot_t(branch, full_ref[1]).astype(BF)
    turned_ref[...] = mixed_ref[...].T
    put_grad(1, turned_ref, branch, slot_ref, keep_ref, send_ref)
    rows_ref[0:1, :] = dgain
    rows_ref[1:2, :] = dshift
    rows_ref[2:3, :] = column_sum(dquery)
    rows_ref[3:4, :] = column_sum(branch)


def total_of(parts):
    total = parts[0][0].astype(F32) + parts[1][0].astype(F32)
    for part in parts[2:]:
        total = total + part[...].astype(F32)
    return total.astype(BF)


def cross_back_kernel(count, ready, slot_ref, vec_ref, enc_ref, n_ref, dquery_ref, res_ref, out_ref, out_near_ref, out_far_ref, *refs):
    parts, pieces = refs[:count], refs[count : count + 4]
    denc_ref, layer_ref, keep_ref, send_ref, rows_ref, full_ref, turned_ref, turned_enc_ref, sems = refs[count + 4 :]
    copies = start_copies(pieces, PAIR_AT, slot_ref, full_ref, sems, 0)
    ready()
    turned_ref[...] = n_ref[...].T
    put_grad(2, turned_ref, dquery_ref[...], slot_ref, keep_ref, send_ref)
    dkv = total_of(parts)
    turned_enc_ref[...] = enc_ref[...].T
    put_grad(0, turned_enc_ref, dkv[0], slot_ref, keep_ref, send_ref)
    put_grad(1, turned_enc_ref, dkv[1], slot_ref, keep_ref, send_ref)
    rows_ref[0:1, :] = column_sum(dkv[1])
    out = out_ref[0].astype(F32) + out_near_ref[0].astype(F32) + out_far_ref[...].astype(F32)
    layer_ref[...] = (res_ref[...] + out + vector(vec_ref, DOWN)).astype(BF)
    wait_all(copies)
    denc_ref[...] = (dot_t(dkv[0], full_ref[0]) + dot_t(dkv[1], full_ref[1])).astype(BF)


def self_back_kernel(count, ready, slot_ref, vec_ref, x_ref, n_ref, dquery_ref, dres_ref, up_ref, ffn_ref, mid_ref, enc_ref, *refs):
    parts, pieces = refs[:count], refs[count : count + 4]
    dx_ref, keep_ref, send_ref, full_ref, turned_ref, sems = refs[count + 4 :]
    copies = start_packed(pieces, slot_ref, full_ref, sems)
    ready()
    dkv = total_of(parts)
    dquery = dquery_ref[...]
    turned_ref[...] = n_ref[...].T
    shard = turned_ref.shape[0] // 4
    for j in range(4):
        place = pl.ds(pl.multiple_of(slot_ref[j] * shard, shard), shard)
        target = send_ref if j % 2 else keep_ref
        target[j // 2, 0:shard] = dot(turned_ref[place, :], dkv[0]).astype(BF)
        target[j // 2, shard : 2 * shard] = dot(turned_ref[place, :], dkv[1]).astype(BF)
    wait_all(copies)
    dn = dot_t(dquery, full_ref[0]) + dot_t(dkv[0], full_ref[1]) + dot_t(dkv[1], full_ref[2])
    dvalues, dgain, dshift = norm_back(dn, x_ref[...].astype(F32), vector(vec_ref, GAIN))
    dx_ref[...] = (dres_ref[...] + dvalues).astype(BF)
    rows = [
        dgain,
        mid_ref[0:1, :],
        ffn_ref[0:1, :],
        column_sum(dquery),
        column_sum(dkv[1]),
        mid_ref[3:4, :],
        mid_ref[2:3, :],
        enc_ref[0:1, :],
        ffn_ref[2:3, :],
        dshift,
        mid_ref[1:2, :],
        ffn_ref[1:2, :],
    ]
    common = jnp.concatenate(rows + [ffn_ref[3:4, :]], axis=0)
    rest = keep_ref.shape[1] - 2 * shard
    for p in range(4):
        up = jnp.where(slot_ref[0] == p, up_ref[0:1, :], 0.0)
        parts = [common[i : i + 1, p * shard : (p + 1) * shard] for i in range(common.shape[0])]
        parts += [up[:, i * shard : (i + 1) * shard] for i in range(4)]
        parts += [jnp.zeros_like(parts[0])] * (-len(parts) % 4)
        lines = [jnp.concatenate(parts[i : i + 4], axis=1) for i in range(0, len(parts), 4)]
        lines.append(jnp.zeros((rest - len(lines), common.shape[1]), F32))
        lines = jnp.concatenate(lines, axis=0).astype(BF)
        flip = lax.bitwise_xor(slot_ref[0], p)

        @pl.when(lax.rem(flip, 2) == 0)
        def _():
            keep_ref[lax.div(flip, 2), 2 * shard :] = lines

        @pl.when(lax.rem(flip, 2) == 1)
        def _():
            send_ref[lax.div(flip, 2), 2 * shard :] = lines


def last_kernel(ready, late_ref, middle_ref, own_ref, attn_ref, out_ref, gain_ref, bias_ref, up_ref, down_ref):
    ready()
    shard = attn_ref.shape[1]

    def part(ref, i):
        return ref[i * shard : (i + 1) * shard, :].astype(F32)

    for i, (ref, j) in enumerate(
        [(late_ref, 2), (own_ref, 0), (own_ref, 1), (middle_ref, 0), (late_ref, 0), (late_ref, 1)]
    ):
        attn_ref[i] = part(ref, j)
    out_ref[0] = part(middle_ref, 1)
    out_ref[1] = part(middle_ref, 2)
    sums = own_ref[2 * shard :, :].astype(F32)

    def row(i):
        return sums[i // 4 : i // 4 + 1, (i % 4) * shard : (i % 4 + 1) * shard]

    gain_ref[...] = jnp.concatenate([row(i) for i in range(3)], axis=0)
    bias_ref[...] = jnp.concatenate([row(i) for i in range(3, 12)], axis=0)
    down_ref[...] = row(12)
    up_ref[...] = jnp.concatenate([row(i) for i in range(13, 17)], axis=1)


ROWS_CUT = 32
ROWS_SUM = 64
WHOLE = pl.BlockSpec(memory_space=pltpu.VMEM)
LEFT = pl.BlockSpec(memory_space=pltpu.HBM)
SCALARS = pl.BlockSpec(memory_space=pltpu.SMEM)


def cost(microseconds):
    return pl.CostEstimate(flops=0, bytes_accessed=int(microseconds * 3.5e6), transcendentals=0)


def dense(kernel, scalars, blocks, pieces, outs, scratch, microseconds, copies=None):
    copies = len(pieces) if copies is None else copies
    held = 2 * sum(math.prod(b.shape) * b.dtype.itemsize for b in blocks)
    held += sum(math.prod(shape) * jnp.dtype(kind).itemsize for shape, kind in outs)
    held += sum(math.prod(ref.shape) * jnp.dtype(ref.dtype).itemsize for ref in scratch)
    n_s, n_b, n_p, n_o = len(scalars), len(blocks), len(pieces), len(outs)

    def body(*refs):
        near, refs = refs[:n_s], refs[n_s:]
        far, refs = refs[:n_b], refs[n_b:]
        rest, refs = refs[: n_p + n_o], refs[n_p + n_o :]
        local, sems, refs = refs[:n_b], refs[n_b], refs[n_b + 1 :]
        fetches = [pltpu.make_async_copy(far[i], local[i], sems.at[i]) for i in range(n_b)]
        for fetch in fetches:
            fetch.start()

        def ready():
            for fetch in fetches:
                fetch.wait()

        kernel(ready, *near, *local, *rest, *refs)

    return pl.pallas_call(
        body,
        in_specs=[SCALARS] * n_s + [LEFT] * (n_b + n_p),
        out_specs=[pl.BlockSpec(shape, lambda d=len(shape): (0,) * d) for shape, _ in outs],
        out_shape=[jax.ShapeDtypeStruct(shape, kind) for shape, kind in outs],
        scratch_shapes=[pltpu.VMEM(b.shape, b.dtype) for b in blocks]
        + [pltpu.SemaphoreType.DMA((n_b,))]
        + scratch
        + ([pltpu.SemaphoreType.DMA((copies,))] if pieces else []),
        compiler_params=pltpu.CompilerParams(vmem_limit_bytes=60 * MIB),
        cost_estimate=cost(microseconds),
    )(*scalars, *blocks, *pieces)


def hold(*values):
    return lax.optimization_barrier(values)


def per_device(
    layer_in,
    encoded,
    pairing,
    attn_weight,
    out_weight,
    up_weight,
    down_weight,
    norm_gains,
    bias_rows,
    up_bias,
    down_bias,
    out_cotangent,
):
    seqs, local_rows, width = layer_in.shape
    outer = lax.axis_size("o")
    groups = outer * 2
    half = local_rows // 2
    shard = attn_weight.shape[1]
    hidden = up_weight.shape[1]
    blocks = hidden // width
    rows = LINE * half
    enc_rows = LINE * (encoded.shape[1] // 2)
    fx, y, z, o, core = (lax.axis_index(a) for a in ("fx", "y", "z", "o", "core"))

    vectors = jnp.concatenate(
        [norm_gains, bias_rows, up_bias.reshape(blocks, shard), down_bias.reshape(1, shard)], axis=0
    )
    vectors = jnp.pad(vectors, ((0, ROWS_CUT - vectors.shape[0]), (0, width - shard)))
    slots = jnp.stack([2 * fx + core, 2 * fx + 1 - core, 2 - 2 * fx + core, 3 - 2 * fx - core])
    qkv_shard = jnp.concatenate([attn_weight[:3].reshape(3 * shard, width), vectors], axis=0)
    qkv_other = lax.ppermute(qkv_shard, "fx", SWAP)
    qkv_near = between_cores(qkv_shard)
    qkv_near, layer_in, encoded = hold(qkv_near, layer_in, encoded)
    x_bf, enc_bf = deal([layer_in, encoded])

    def places_of(pairing):
        group = o * 2 + y
        spots = []
        for step in range(groups):
            source = lax.rem(group - step + groups, groups)
            for flip in range(2):
                c = core if flip == 0 else 1 - core
                k = 2 * lax.rem(z, 2) + c
                for r in range(LINE):
                    line = lax.rem(r - k + LINE, LINE)
                    spots.append((((source // 2) * LINE + line) * 2 + lax.rem(source, 2)) * 2 + c)
        spans = jnp.take(pairing.reshape(-1), jnp.stack(spots), axis=0)
        return (spans[:, None] * half + jnp.arange(half, dtype=jnp.int32)[None, :]).reshape(-1, 1)

    product = 2 * rows * width * width
    square = (width, width)
    act, real = ((rows, width), BF), ((rows, width), F32)
    turned = pltpu.VMEM((width, rows), BF)

    def weights(n):
        return pltpu.VMEM((n,) + square, BF)

    def grads(n):
        return [((2, n, shard, width), BF)] * 2

    note = ((16, width), F32)

    x_bf, enc_bf, qkv_other, qkv_near, attn_weight, out_weight, up_weight, out_cotangent, pairing = hold(
        x_bf, enc_bf, qkv_other, qkv_near, attn_weight, out_weight, up_weight, out_cotangent, pairing
    )
    pair_shard = attn_weight[4:]
    key_places = places_of(pairing)
    mid_shard = jnp.concatenate([attn_weight[4:], attn_weight[3:4], out_weight], axis=0)
    rest_shard = jnp.concatenate([attn_weight[3:4], out_weight], axis=0)
    w_qkv = (qkv_shard, qkv_near, qkv_other, between_cores(qkv_other))
    pair_other = lax.ppermute(pair_shard, "fx", SWAP)
    mid_near = between_cores(mid_shard)
    extra = ROWS_CUT
    n1, query, kv, vec = dense(
        self_in_kernel,
        [slots],
        [x_bf],
        w_qkv,
        [act, act, ((2, rows, width), BF), ((TABLE, width), F32)],
        [weights(3), pltpu.VMEM((4, extra, width), BF)],
        4,
        copies=16,
    )
    n1, query, kv, vec, up_weight, key_places, out_cotangent = hold(
        n1, query, kv, vec, up_weight, key_places, out_cotangent
    )
    places = (key_places, key_places[:rows].reshape(1, -1))
    kv_self = to_others(kv, groups)
    near_self = between_cores(kv)
    up_cut = up_weight.reshape(shard, 4, width).transpose(1, 0, 2)
    cot_halves = deal_halves(out_cotangent)
    pair_other, rest_shard, mid_near = hold(pair_other, rest_shard, mid_near)
    rest_other = lax.ppermute(rest_shard, "fx", SWAP)
    w_pair = (mid_shard, mid_near, pair_other, between_cores(pair_other))
    (kv,) = dense(
        cross_in_kernel, [slots], [vec, enc_bf], w_pair, [((2, enc_rows, width), BF)], [weights(2)], 3.5
    )
    kv_self, near_self, kv, cot_halves, up_cut = hold(kv_self, near_self, kv, cot_halves, up_cut)
    cot = deal_line(*cot_halves)
    kv_cross = to_others(kv, groups)
    near_cross = between_cores(kv)
    kv_self = [kv_self[0], near_self] + with_cores(kv_self[1:])
    mixed, mass = attention(query, kv_self, places)
    mixed, mass, up_cut, rest_other, kv_cross, near_cross, cot = hold(
        mixed, mass, up_cut, rest_other, kv_cross, near_cross, cot
    )
    cot = deal_order(cot)
    w_rest = (mid_shard, mid_near, rest_other, between_cores(rest_other))
    kv_cross = [kv_cross[0], near_cross] + with_cores(kv_cross[1:])
    r1, n2, cquery = dense(middle_kernel, [slots], [vec, mixed, x_bf], w_rest, [real, act, act], [weights(2)], 3.3)
    r1, n2, cquery, kv_cross, up_cut = hold(r1, n2, cquery, kv_cross, up_cut)
    up_own = lax.all_to_all(up_cut, ("fx", "core"), 0, 0, tiled=True).reshape(width, width)
    cot_other = lax.ppermute(cot, "fx", SWAP)
    cot_near = between_cores(cot)
    cmixed, cmass = attention(cquery, kv_cross, None)
    cmixed, cmass, cot_other, cot_near = hold(cmixed, cmass, cot_other, cot_near)
    r2, n3 = dense(before_feed_kernel, [slots], [vec, cmixed, r1], w_rest, [real, act], [weights(1)], 2.7)
    r2, n3, cot_other = hold(r2, n3, cot_other)
    n3_other = lax.ppermute(n3, "fx", SWAP)
    cots = (cot, cot_near, cot_other, between_cores(cot_other))
    n3s = (n3, between_cores(n3), n3_other, between_cores(n3_other))
    pair = ((2, rows, width), BF)
    four = ((4, rows, width), BF)
    dn_keep, dn_send, out_keep, out_send, hidden_act, dpre, up_rows = dense(
        feed_kernel,
        [],
        [vec, up_own, down_weight] + list(n3s) + list(cots),
        [],
        [pair, pair, pair, pair, four, four, ((8, width), F32)],
        [],
        8,
    )

    single = outer == 1

    def step(terms, name):
        return halve(terms, name) if single else terms

    def hold_all(*values):
        flat = hold([[term[0] for term in v] if isinstance(v, list) else v for v in values])[0]
        return [
            [(array, term[1]) for array, term in zip(new, old)] if isinstance(old, list) else new
            for new, old in zip(flat, values)
        ]

    dn_got = between_cores(dn_send)
    dn_keep, dn_got, hidden_act, dpre = hold(dn_keep, dn_got, hidden_act, dpre)
    dn_far = lax.ppermute(add([dn_keep[1], dn_got[1]]), "fx", SWAP)
    cut = ((4, 2, 4, shard // 4, width // 2), BF)
    up, down = dense(feed_grad_kernel, [], [hidden_act, dpre] + list(n3s) + list(cots), [], [cut, cut], [], 6)
    dn_far, up, down, out_keep, out_send = hold(dn_far, up, down, out_keep, out_send)
    up, down = ([(part.reshape((2, 2, 2) + part.shape[2:]), ())] for part in (up, down))
    up, down = step(up, "y"), step(down, "z0")
    out_got = between_cores(out_send)
    dr2, doc, ffn_rows = dense(
        after_feed_kernel, [slots], [vec, dn_keep, dn_got, dn_far, r2, cot], w_rest, [real, act, note], [weights(1)], 2.7
    )

    dcq, cmine, ctheirs = attention_back(cquery, doc, cmixed, cmass, kv_cross, None)
    dcq, cmine, ctheirs, dr2, ffn_rows, out_keep, out_got, up, down = hold_all(
        dcq, cmine, ctheirs, dr2, ffn_rows, out_keep, out_got, up, down
    )
    cgot = between_cores(ctheirs)
    dr1, dos, middle_keep, middle_send, mid_rows = dense(
        middle_back_kernel,
        [slots],
        [vec, dcq, n2, r1, dr2, mixed, cmixed],
        w_rest,
        [real, act] + grads(3) + [note],
        [weights(2), turned],
        6,
    )
    dr1, dos, middle_keep, middle_send, mid_rows, cgot, cmine, up, down, out_keep, out_got = hold_all(
        dr1, dos, middle_keep, middle_send, mid_rows, cgot, cmine, up, down, out_keep, out_got
    )
    dckv = collect(cmine, cgot, groups)
    middle = over_cores(middle_keep, middle_send)
    up, down = step(up, "z0"), step(down, "z1")
    out_far = lax.ppermute(add([out_keep[1], out_got[1]]), "fx", SWAP)
    dq, mine, theirs = attention_back(query, dos, mixed, mass, kv_self, places)
    dq, mine, theirs, middle, up, down, out_far, dckv_a = hold_all(dq, mine, theirs, middle, up, down, out_far, dckv[-1])
    dckv = dckv[:-1] + [dckv_a]
    got = between_cores(theirs)
    grad_encoded, layer_out, late_keep, late_send, enc_rows_sum = dense(
        functools.partial(cross_back_kernel, len(dckv)),
        [slots],
        [vec, enc_bf, n1, dq, r2, out_keep, out_got, out_far] + dckv,
        w_pair,
        [((enc_rows, width), BF), act] + grads(3) + [note],
        [weights(2), turned, pltpu.VMEM((width, enc_rows), BF)],
        6,
    )
    mine, got, grad_encoded, layer_out, late_keep, late_send, enc_rows_sum, up, down, middle = hold_all(
        mine, got, grad_encoded, layer_out, late_keep, late_send, enc_rows_sum, up, down, middle
    )
    dkv = collect(mine, got, groups)
    late = over_cores(late_keep, late_send)
    late = over_x(late)
    if single:
        at = {name: half_index(name) for name in HALVES}
        middle = [array.reshape(2, 2, 2, 2, -1, width) for array, _ in middle]
        middle_z0 = exchange(add([pick(array, (1, 1 - at["z0"])) for array in middle]), "z0")
        up, down = both_halves(up, "z1"), both_halves(down, "y")
        dkv_last, up, down, late, middle, middle_z0 = hold_all(
            dkv[-1], [(part, ()) for part in up], [(part, ()) for part in down], late, [(part, ()) for part in middle], middle_z0
        )
        home = undeal_line([grad_encoded, layer_out])
        middle = [(array, (1, ("at", 1, at["z0"]))) for array, _ in middle] + [(middle_z0, (1,))]
        middle_x = lax.ppermute(add([half_of(term)[1] for term in middle]), "fx", SWAP)
        late = halve(late, "y")
    else:
        middle = over_x(middle)
        dkv_last, late, middle = hold_all(dkv[-1], late, middle)
    dkv = dkv[:-1] + [dkv_last]
    grad_layer, keep, send = dense(
        functools.partial(self_back_kernel, len(dkv)),
        [slots],
        [vec, x_bf, n1, dq, dr1, up_rows, ffn_rows, mid_rows, enc_rows_sum] + dkv,
        w_qkv,
        [act] + [((2, 2 * shard + ROWS_SUM, width), BF)] * 2,
        [weights(3), turned],
        7,
        copies=12,
    )
    if single:
        grad_layer, keep, send, late, up, down, middle_x, home = hold_all(
            grad_layer, keep, send, late, up, down, middle_x, home
        )
        up, down = (add([part for part, _ in parts]) for parts in (up, down))
        up = lax.all_to_all(up, ("fx", "core"), 1, 1, tiled=True)
        own = over_cores(keep, send)
        middle = [(array, names + (0,)) for array, names in middle] + [(middle_x, (1,))]
        home = undeal_cores(home)
        down, late, middle = double(down, "z1"), halve(late, "z0"), halve(middle, "y")
        own, up, late, middle, home, down, grad_layer = hold_all(
            own, up, late, middle, [(p, ()) for p in home], down, grad_layer
        )
        own = over_x(own)
        last = undeal_line([grad_layer])
        up = double(up, "z0")
        late, middle = both_halves(late, "z1"), both_halves(middle, "z1")
        own, late, middle, home, up, down, last = hold_all(
            own, [(p, ()) for p in late], [(p, ()) for p in middle], home, up, down, last
        )
        grad_encoded, layer_out = undealt([p for p, _ in home], [F32, BF])
        last = undeal_cores(last)
        late, middle = (add([part for part, _ in parts]) for parts in (late, middle))
        own = add([array[0] if 0 in names else array for array, names in own]).reshape(2 * LINE, -1, width)
        own = lax.all_to_all(own, ("z", "y"), 0, 0, tiled=True)
        late, middle = double(late, "z0"), double(middle, "y")
        up, down = double(up, "y"), double(down, "z0")
        own, late, middle, up, down, last = hold(own, late, middle, up, down, last)
        own = jnp.sum(own.astype(F32), axis=0, keepdims=True).astype(BF)
        own = lax.all_to_all(jnp.broadcast_to(own, (2 * LINE,) + own.shape[1:]), ("z", "y"), 0, 0, tiled=True)
        late, middle = double(late, "y"), double(middle, "z0")
        (grad_layer,) = undealt(last, [F32])
        grad_attn, grad_out, *total = dense(
            last_kernel,
            [],
            [part.reshape(-1, width) for part in (late, middle, own)],
            [],
            [((6, shard, width), F32), ((2, shard, width), F32), ((3, shard), F32), ((9, shard), F32)]
            + [((1, blocks * shard), F32), ((1, shard), F32)],
            [],
            3,
        )
        up, down = (part.astype(F32).reshape(2, 2, 2, 4, shard // 4, width // 2) for part in (up, down))
    else:
        own = over_cores(keep, send)
        (grad_layer,) = undeal([grad_layer], [F32])
        (grad_encoded,), (layer_out,) = undeal([grad_encoded], [F32]), undeal([layer_out], [BF])

        def over_ctx(terms, n):
            total = add([array[0] if 0 in names else array for array, names in terms])
            return lax.psum(total, ("o", "z", "y")).astype(F32).reshape(n, -1, width)

        own, middle, late = over_ctx(over_x(own), 1)[0], over_ctx(middle, 3), over_ctx(late, 3)
        up, down = (lax.psum(part[0][0], ("o", "z", "y")).astype(F32) for part in (up, down))
        up = lax.all_to_all(up.astype(BF), ("fx", "core"), 3, 3, tiled=True).astype(F32)
        total = own[2 * shard : 2 * shard + 5].reshape(-1, shard)
        total = [total[:3], total[3:12], total[13 : 13 + blocks].reshape(1, -1), total[12:13]]
        own = own[: 2 * shard].reshape(2, shard, width)
        grad_attn = jnp.concatenate([late[2:], own, middle[:1], late[:2]], axis=0)
        grad_out = middle[1:]
    g_up = up.transpose(0, 1, 4, 3, 2, 5).reshape(shard, hidden)
    g_down = down.transpose(3, 0, 1, 4, 2, 5).reshape(hidden // 4, width)
    return (
        layer_out,
        grad_layer,
        grad_encoded,
        grad_attn,
        grad_out,
        g_up,
        g_down,
        total[0],
        total[1],
        total[2].reshape(-1),
        total[3].reshape(-1),
    )


def solution(mesh):
    ctx = mesh.shape["ctx"]
    grid = Mesh(mesh.devices.reshape(2, 2, ctx // (2 * LINE), LINE, 2), ("fx", "core", "o", "z", "y"))
    fsdp = ("fx", "core")
    rows = P(fsdp, ("o", "z", "y"), None)
    weights = (
        P(None, fsdp, None),
        P(None, fsdp, None),
        P(fsdp, None),
        P(fsdp, None),
        P(None, fsdp),
        P(None, fsdp),
        P(fsdp),
        P(fsdp),
    )
    return jax.shard_map(
        per_device,
        mesh=grid,
        in_specs=(rows, rows, P()) + weights + (rows,),
        out_specs=(rows, rows, rows) + weights,
        check_vma=False,
    )
```

```python
import functools
import math

import jax
import jax.numpy as jnp
from jax import lax
from jax.experimental import pallas as pl
from jax.experimental.pallas import tpu as pltpu
from jax.sharding import Mesh
from jax.sharding import PartitionSpec as P

HEADS = 12
HD = 64
PAIR = 2 * HD
SCORE_SCALE = 0.125
MASK_FILL = -1e30
NORM_EPSILON = 1e-05
LINE = 4
SWAP = [(0, 1), (1, 0)]
BF = jnp.bfloat16
F32 = jnp.float32
MIB = 1 << 20


def dot(left, right):
    return jnp.dot(left, right, preferred_element_type=F32)


def dot_t(left, right):
    return lax.dot_general(left, right, (((1,), (1,)), ((), ())), preferred_element_type=F32)


def t_dot(left, right):
    return lax.dot_general(left, right, (((0,), (0,)), ((), ())), preferred_element_type=F32)


def split_heads(block):
    lane = lax.broadcasted_iota(jnp.int32, block.shape, 1)
    zero = jnp.zeros_like(block)
    return jnp.concatenate([jnp.where(lane < HD, block, zero), jnp.where(lane < HD, zero, block)], axis=0)


def join_heads(columns):
    rows = columns.shape[1] // 2
    return jnp.concatenate([columns[:HD, :rows], columns[HD:, rows:]], axis=0).T


def forward_kernel(masked, pieces, *refs):
    if masked:
        key_place_ref, query_place_ref, refs = refs[0], refs[1], refs[2:]
    query_ref, kv_refs = refs[0], refs[1 : 1 + pieces]
    out_ref, mass_ref, scores_ref = refs[1 + pieces :]
    query = split_heads(query_ref[...] * jnp.asarray(SCORE_SCALE, BF))
    piece = kv_refs[0].shape[1]
    if masked:
        query_place = query_place_ref[...]
        query_place = jnp.concatenate([query_place, query_place], axis=1)
    top = None
    for i in range(pieces):
        scores = dot_t(kv_refs[i][0], query)
        if masked:
            scores = jnp.where(key_place_ref[pl.ds(i * piece, piece), :] <= query_place, scores, MASK_FILL)
        scores_ref[pl.ds(i * piece, piece), :] = scores
        high = jnp.max(scores, axis=0, keepdims=True)
        top = high if top is None else jnp.maximum(top, high)
    mass = jnp.zeros_like(top)
    mixed = None
    for i in range(pieces):
        probs = jnp.exp(scores_ref[pl.ds(i * piece, piece), :] - top)
        mass = mass + jnp.sum(probs, axis=0, keepdims=True)
        part = t_dot(kv_refs[i][1], probs.astype(BF))
        mixed = part if mixed is None else mixed + part
    out_ref[...] = join_heads(mixed * (1.0 / mass)).astype(BF)
    mass_ref[0] = top + jnp.log(mass)


def backward_kernel(masked, pieces, *refs):
    if masked:
        key_place_ref, query_place_ref, refs = refs[0], refs[1], refs[2:]
    query_ref, dout_ref, out_ref, mass_ref = refs[:4]
    kv_refs = refs[4 : 4 + pieces]
    dquery_ref, mine_ref, theirs_ref = refs[4 + pieces :]
    query = split_heads(query_ref[...] * jnp.asarray(SCORE_SCALE, BF))
    dout = dout_ref[...]
    prod = (dout.astype(F32) * out_ref[...].astype(F32)).T
    delta = jnp.concatenate(
        [jnp.sum(prod[:HD], axis=0, keepdims=True), jnp.sum(prod[HD:], axis=0, keepdims=True)], axis=1
    )
    dout = split_heads(dout)
    log_mass = mass_ref[0]
    piece = kv_refs[0].shape[1]
    if masked:
        query_place = query_place_ref[...]
        query_place = jnp.concatenate([query_place, query_place], axis=1)
    dquery = None
    for i in range(pieces):
        keys = kv_refs[i][0]
        scores = dot_t(keys, query)
        if masked:
            scores = jnp.where(key_place_ref[pl.ds(i * piece, piece), :] <= query_place, scores, MASK_FILL)
        probs = jnp.exp(scores - log_mass)
        dprobs = dot_t(kv_refs[i][1], dout)
        dscores = (probs * (dprobs - delta)).astype(BF)
        dkv_ref = theirs_ref if i % 2 else mine_ref
        dkv_ref[i // 2, 0] = dot(dscores, query).astype(BF)
        dkv_ref[i // 2, 1] = dot(probs.astype(BF), dout).astype(BF)
        part = t_dot(keys, dscores)
        dquery = part if dquery is None else dquery + part
    dquery_ref[...] = (join_heads(dquery) * SCORE_SCALE).astype(BF)


def place_specs(masked, places):
    if not masked:
        return [], []
    key_places, query_places = places
    return [key_places, query_places], [
        pl.BlockSpec(key_places.shape, lambda h: (0, 0)),
        pl.BlockSpec(query_places.shape, lambda h: (0, 0)),
    ]


def attention(query, kv, places):
    masked = places is not None
    rows, width = query.shape
    piece = kv[0].shape[1]
    extra, extra_specs = place_specs(masked, places)
    keys = piece * len(kv)
    return pl.pallas_call(
        functools.partial(forward_kernel, masked, len(kv)),
        grid=(width // PAIR,),
        in_specs=extra_specs
        + [pl.BlockSpec((rows, PAIR), lambda h: (0, h))]
        + [pl.BlockSpec((2, piece, PAIR), lambda h: (0, 0, h))] * len(kv),
        out_specs=[
            pl.BlockSpec((rows, PAIR), lambda h: (0, h)),
            pl.BlockSpec((1, 1, 2 * rows), lambda h: (h, 0, 0)),
        ],
        out_shape=[
            jax.ShapeDtypeStruct((rows, width), BF),
            jax.ShapeDtypeStruct((width // PAIR, 1, 2 * rows), F32),
        ],
        scratch_shapes=[pltpu.VMEM((keys, 2 * rows), F32)],
        compiler_params=pltpu.CompilerParams(vmem_limit_bytes=60 * MIB),
        cost_estimate=cost(8 * rows * keys / 2**18),
    )(*extra, query, *kv)


def attention_back(query, dout, out, mass, kv, places):
    masked = places is not None
    rows, width = query.shape
    piece = kv[0].shape[1]
    extra, extra_specs = place_specs(masked, places)
    keys = piece * len(kv)
    column = pl.BlockSpec((rows, PAIR), lambda h: (0, h))
    pair = pl.BlockSpec((2, piece, PAIR), lambda h: (0, 0, h))
    groups = len(kv) // 2
    blocks = pl.BlockSpec((groups, 2, piece, PAIR), lambda h: (0, 0, 0, h))
    return pl.pallas_call(
        functools.partial(backward_kernel, masked, len(kv)),
        grid=(width // PAIR,),
        in_specs=extra_specs
        + [column, column, column, pl.BlockSpec((1, 1, 2 * rows), lambda h: (h, 0, 0))]
        + [pair] * len(kv),
        out_specs=[column, blocks, blocks],
        out_shape=[jax.ShapeDtypeStruct((rows, width), BF)]
        + [jax.ShapeDtypeStruct((groups, 2, piece, width), BF)] * 2,
        compiler_params=pltpu.CompilerParams(vmem_limit_bytes=60 * MIB),
        cost_estimate=cost(13 * rows * keys / 2**18),
    )(*extra, query, dout, out, mass, *kv)


def deal_perms():
    perms = []
    for r in range(LINE):
        perm = []
        for c in range(2):
            for z in range(LINE):
                k = (r - z) % LINE
                perm.append((c * LINE + z, (k % 2) * LINE + 2 * c + k // 2))
        perms.append(perm)
    return perms


DEAL = deal_perms()


def deal(arrays):
    if len({array.shape for array in arrays}) > 1:
        return [deal([array])[0] for array in arrays]
    _, rows, width = arrays[0].shape
    chunks = [array.reshape(LINE, rows // 2, width) for array in arrays]
    z = lax.axis_index("z")
    got = []
    for r in range(LINE):
        k = lax.rem(r - z + LINE, LINE)
        chunk = jnp.stack([lax.dynamic_index_in_dim(c, k, keepdims=False) for c in chunks])
        got.append(lax.ppermute(chunk, ("core", "z"), DEAL[r]))
    return [jnp.concatenate([g[i] for g in got], axis=0) for i in range(len(arrays))]


def undeal_line(arrays):
    core, z = lax.axis_index("core"), lax.axis_index("z")
    chunks = jnp.stack([array.reshape(LINE, -1, array.shape[-1]) for array in arrays], axis=1)
    start = lax.rem(2 * lax.rem(z, 2) + core, LINE)
    chunks = lax.dynamic_slice_in_dim(jnp.concatenate([chunks, chunks], axis=0), start, LINE, axis=0)
    return lax.all_to_all(chunks, "z", 0, 0, tiled=True)


def undeal_cores(chunks):
    core = lax.axis_index("core")
    chunks = chunks.reshape((2, 2) + chunks.shape[1:])
    mine = lax.dynamic_index_in_dim(chunks, core, 0, keepdims=False)
    return mine, lax.ppermute(lax.dynamic_index_in_dim(chunks, 1 - core, 0, keepdims=False), "core", SWAP)


def undealt(halves, kinds):
    first = lax.axis_index("core") == 0
    outs = []
    for i, kind in enumerate(kinds):
        mine, got = (half[:, i].astype(kind) for half in halves)
        both = jnp.where(first, jnp.stack([mine, got], axis=1), jnp.stack([got, mine], axis=1))
        outs.append(both.reshape(2, -1, both.shape[-1]))
    return outs


def deal_halves(array):
    _, rows, width = array.shape
    parts = array.reshape(2, 2, rows // 2, width)
    core = lax.axis_index("core")
    mine = lax.dynamic_index_in_dim(parts, core, 1, keepdims=False)
    return mine, lax.ppermute(lax.dynamic_index_in_dim(parts, 1 - core, 1, keepdims=False), "core", SWAP)


def deal_line(mine, got):
    first = lax.axis_index("core") == 0
    chunks = jnp.where(first, jnp.concatenate([mine, got], axis=0), jnp.concatenate([got, mine], axis=0))
    return lax.all_to_all(chunks, "z", 0, 0, tiled=True)


def deal_order(chunks):
    core, z = lax.axis_index("core"), lax.axis_index("z")
    start = lax.rem(LINE - 2 * lax.rem(z, 2) - core, LINE)
    mine = lax.dynamic_slice_in_dim(jnp.concatenate([chunks, chunks], axis=0), start, LINE, axis=0)
    return mine.reshape(-1, mine.shape[-1])


def undeal(arrays, kind):
    count = len(arrays)
    half = arrays[0].shape[0] // LINE
    got = []
    for r in range(LINE):
        chunk = jnp.stack([array[r * half : (r + 1) * half] for array in arrays])
        got.append(lax.ppermute(chunk, ("core", "z"), [(b, a) for a, b in DEAL[r]]))
    z = lax.axis_index("z")
    outs = []
    for i in range(count):
        mine = lax.dynamic_slice_in_dim(jnp.stack([g[i] for g in got + got]), z, LINE, axis=0)
        outs.append(mine.reshape(2, 2 * half, arrays[0].shape[1]).astype(kind[i]))
    return outs


def group_perm(groups, step):
    return [(i, (i + step) % groups) for i in range(groups)]


def to_others(own, groups):
    return [own] + [lax.ppermute(own, ("o", "y"), group_perm(groups, step)) for step in range(1, groups)]


def with_cores(blocks):
    pieces = []
    for block in blocks:
        pieces += [block, lax.ppermute(block, "core", SWAP)]
    return pieces


def collect(mine, got, groups):
    terms = [mine, got]
    for step in range(1, groups):
        back = [(b, a) for a, b in group_perm(groups, step)]
        terms.append(lax.ppermute(add([mine[step], got[step]]), ("o", "y"), back))
    return terms


def between_cores(array):
    return lax.ppermute(array, "core", SWAP)


def gather(own, other):
    return own, lax.ppermute(own, "core", SWAP), other, lax.ppermute(other, "core", SWAP)


def after(value, earlier):
    return lax.optimization_barrier((value, earlier))[0]


def add(terms):
    total = terms[0].astype(F32)
    for term in terms[1:]:
        total = total + term.astype(F32)
    return total.astype(BF)


def over_cores(keep, send):
    return [(keep, ()), (lax.ppermute(send, "core", SWAP), ())]


def over_x(terms):
    got = lax.ppermute(add([array[1] for array, _ in terms]), "fx", SWAP)
    return [(array, (0,)) for array, _ in terms] + [(got, ())]


def part_over_x(terms, first, last):
    return lax.ppermute(add([array[1, first:last] for array, _ in terms]), "fx", SWAP)


def pick(array, *path):
    for axis, index in path:
        array = lax.dynamic_index_in_dim(array, index, axis, keepdims=False)
    return array


HALVES = ("y", "z0", "z1")


def exchange(array, name):
    if name == "y":
        return lax.ppermute(array, "y", SWAP)
    flip = 1 if name == "z0" else 2
    return lax.ppermute(array, "z", [(i, i ^ flip) for i in range(LINE)])


def half_index(name):
    z = lax.axis_index("z")
    return lax.axis_index("y") if name == "y" else lax.rem(z, 2) if name == "z0" else lax.div(z, 2)


def half_of(term, more=()):
    array, names = term
    cut = 1 in names
    if 0 in names and 1 not in names and len(names + more) > 1:
        array = array.reshape(2, 2, 2, 2, -1, array.shape[-1])
        cut = True
    for name in names + more:
        if name in (0, 1):
            array = array if name else array[0]
            continue
        if name[0] == "at":
            array = pick(array, name[1:])
            continue
        name, other = name if isinstance(name, tuple) else (name, False)
        if array.ndim == 3 and not cut:
            array = array.reshape(2, 2, 2, -1, array.shape[-1])
        cut = True
        i = half_index(name)
        array = lax.dynamic_index_in_dim(array, 1 - i if other else i, 0, keepdims=False)
    return array


def halve(terms, name):
    theirs = add([half_of(term, ((name, True),)) for term in terms])
    got = exchange(theirs, name)
    return [(array, names + (name,)) for array, names in terms] + [(got, (1,))]


def both_halves(terms, name):
    mine = add([half_of(term) for term in terms])
    got = exchange(mine, name)
    mine = lax.optimization_barrier(mine)
    return mine, got


def double(part, name):
    other = exchange(part, name)
    first = half_index(name) == 0
    return jnp.where(first, jnp.concatenate([part, other], axis=0), jnp.concatenate([other, part], axis=0))


def standard(values):
    center = values - jnp.mean(values, axis=-1, keepdims=True)
    inverse = lax.rsqrt(jnp.mean(center * center, axis=-1, keepdims=True) + NORM_EPSILON)
    return center * inverse, inverse


def norm_back(dnormed, values, gain):
    z, inverse = standard(values)
    a = dnormed * gain
    dvalues = (
        a - jnp.mean(a, axis=-1, keepdims=True) - z * jnp.mean(a * z, axis=-1, keepdims=True)
    ) * inverse
    return dvalues, jnp.sum(dnormed * z, axis=0, keepdims=True), jnp.sum(dnormed, axis=0, keepdims=True)


def column_sum(values):
    return jnp.sum(values.astype(F32), axis=0, keepdims=True)


GAIN, BIAS, UP, DOWN = 0, 3, 12, 13
TABLE = 24
PAIR_AT, REST_AT, LAST_AT = (0, 0, 0, 0), (2, 2, 0, 0), (4, 4, 2, 2)


def vector(vec_ref, row):
    return vec_ref[row : row + 1, :]


def start_packed(pieces, slot_ref, full_ref, sems):
    n, rows = full_ref.shape[0], full_ref.shape[1] // 4
    copies = []
    for j, piece in enumerate(pieces):
        place = pl.ds(pl.multiple_of(slot_ref[j] * rows, rows), rows)
        for i in range(n):
            copy = pltpu.make_async_copy(
                piece.at[pl.ds(i * rows, rows), :], full_ref.at[i, place, :], sems.at[j * n + i]
            )
            copy.start()
            copies.append(copy)
    return copies


def start_copies(pieces, firsts, slot_ref, full_ref, sems, base):
    copies = []
    for j, piece in enumerate(pieces):
        rows = piece.shape[-2]
        place = pl.ds(pl.multiple_of(slot_ref[j] * rows, rows), rows)
        if len(piece.shape) == 3:
            source, target = piece.at[pl.ds(firsts[j], full_ref.shape[0])], full_ref.at[:, place, :]
        else:
            source, target = piece, full_ref.at[place, :]
        copy = pltpu.make_async_copy(source, target, sems.at[base + j])
        copy.start()
        copies.append(copy)
    return copies


def wait_all(copies):
    for copy in copies:
        copy.wait()


def put_grad(unit, turned, right, slot_ref, keep_ref, send_ref):
    rows = turned.shape[0] // 4
    for j in range(4):
        place = pl.ds(pl.multiple_of(slot_ref[j] * rows, rows), rows)
        block = dot(turned[place, :], right).astype(BF)
        target = send_ref if j % 2 else keep_ref
        target[j // 2, unit] = block


def self_in_kernel(ready, slot_ref, x_ref, *refs):
    pieces, (n_ref, query_ref, kv_ref, vec_ref, full_ref, parts_ref, sems) = refs[:4], refs[4:]
    weights, shard = full_ref.shape[0], full_ref.shape[1] // 4
    extra = parts_ref.shape[1]
    small = []
    for j, piece in enumerate(pieces):
        copy = pltpu.make_async_copy(
            piece.at[pl.ds(weights * shard, extra), :], parts_ref.at[j], sems.at[4 * weights + j]
        )
        copy.start()
        small.append(copy)
    copies = start_packed(pieces, slot_ref, full_ref, sems)
    ready()
    z = standard(x_ref[...].astype(F32))[0]
    wait_all(small)
    parts = [parts_ref[lax.bitwise_xor(slot_ref[0], p)].astype(F32)[:, :shard] for p in range(4)]
    own = parts_ref[0].astype(F32)[:, :shard]
    table = jnp.concatenate(parts, axis=1)
    vec_ref[0:UP, :] = table[0:UP]
    vec_ref[UP:DOWN, :] = jnp.concatenate([own[UP + i : UP + i + 1] for i in range(4)], axis=1)
    vec_ref[DOWN : DOWN + 1, :] = table[UP + 4 : UP + 5]
    normed = (z * table[GAIN : GAIN + 1] + table[BIAS + 6 : BIAS + 7]).astype(BF)
    n_ref[...] = normed
    wait_all(copies)
    kv_ref[0] = dot(normed, full_ref[1]).astype(BF)
    kv_ref[1] = (dot(normed, full_ref[2]) + table[BIAS + 1 : BIAS + 2]).astype(BF)
    query_ref[...] = (dot(normed, full_ref[0]) + table[BIAS : BIAS + 1]).astype(BF)


def cross_in_kernel(ready, slot_ref, vec_ref, enc_ref, *refs):
    pieces, (kv_ref, full_ref, sems) = refs[:4], refs[4:]
    copies = start_copies(pieces, PAIR_AT, slot_ref, full_ref, sems, 0)
    ready()
    enc = enc_ref[...]
    wait_all(copies)
    kv_ref[0] = dot(enc, full_ref[0]).astype(BF)
    kv_ref[1] = (dot(enc, full_ref[1]) + vector(vec_ref, BIAS + 4)).astype(BF)


def middle_kernel(ready, slot_ref, vec_ref, mixed_ref, x_ref, *refs):
    pieces, (res_ref, n_ref, query_ref, full_ref, sems) = refs[:4], refs[4:]
    copies = start_copies(pieces, REST_AT, slot_ref, full_ref, sems, 0)
    ready()
    wait_all(copies)
    res = x_ref[...].astype(F32) + dot(mixed_ref[...], full_ref[1]) + vector(vec_ref, BIAS + 2)
    res_ref[...] = res
    normed = (standard(res)[0] * vector(vec_ref, GAIN + 1) + vector(vec_ref, BIAS + 7)).astype(BF)
    n_ref[...] = normed
    query_ref[...] = (dot(normed, full_ref[0]) + vector(vec_ref, BIAS + 3)).astype(BF)


def before_feed_kernel(ready, slot_ref, vec_ref, mixed_ref, res_ref, *refs):
    pieces, (out_ref, n_ref, full_ref, sems) = refs[:4], refs[4:]
    copies = start_copies(pieces, LAST_AT, slot_ref, full_ref, sems, 0)
    ready()
    wait_all(copies)
    res = res_ref[...] + dot(mixed_ref[...], full_ref[0]) + vector(vec_ref, BIAS + 5)
    out_ref[...] = res
    n_ref[...] = (standard(res)[0] * vector(vec_ref, GAIN + 2) + vector(vec_ref, BIAS + 8)).astype(BF)


def feed_kernel(ready, vec_ref, up_ref, down_ref, *refs):
    normed_refs, cot_refs = refs[:2], refs[2:4]
    dn_keep, dn_send, out_keep, out_send, act_ref, dpre_ref, rows_ref = refs[4:]
    ready()
    bias = vector(vec_ref, UP)
    total = None
    for j in (1, 0):
        pre = dot(normed_refs[j][...], up_ref[...]) + bias
        phi = 0.5 * (1.0 + lax.erf(pre * math.sqrt(0.5)))
        slope = phi + pre * (jnp.exp(-0.5 * pre * pre) * (1.0 / math.sqrt(2.0 * math.pi)))
        act = (pre * phi).astype(BF)
        dpre = (dot_t(cot_refs[j][...], down_ref[...]) * slope).astype(BF)
        out, dn = (out_send, dn_send) if j else (out_keep, dn_keep)
        dn[...] = dot_t(dpre, up_ref[...]).astype(BF)
        out[...] = dot(act, down_ref[...]).astype(BF)
        act_ref[j] = act
        dpre_ref[j] = dpre
        sums = column_sum(dpre)
        total = sums if total is None else total + sums
    rows_ref[0:1, :] = total


def feed_grad_kernel(ready, act_a, act_b, dpre_a, dpre_b, *refs):
    normed_refs, cot_refs, (up_ref, down_ref) = refs[:4], refs[4:8], refs[8:]
    quarter, half = up_ref.shape[-2:]
    ready()

    def put(grad, cut_ref):
        for p in range(4):
            for q in range(4):
                rows = grad[(4 * p + q) * quarter : (4 * p + q + 1) * quarter].astype(BF)
                cut_ref[q, 0, p] = rows[:, :half]
                cut_ref[q, 1, p] = rows[:, half:]

    total = None
    for j in range(4):
        part = t_dot(normed_refs[j][...], (dpre_b if j > 1 else dpre_a)[j % 2])
        total = part if total is None else total + part
    put(total, up_ref)
    total = None
    for j in range(4):
        part = t_dot((act_b if j > 1 else act_a)[j % 2], cot_refs[j][...])
        total = part if total is None else total + part
    put(total, down_ref)


def after_feed_kernel(ready, slot_ref, vec_ref, dn_ref, dn_near_ref, dn_far_ref, res_ref, cot_ref, *refs):
    pieces, (dres_ref, dout_ref, rows_ref, full_ref, sems) = refs[:4], refs[4:]
    copies = start_copies(pieces, LAST_AT, slot_ref, full_ref, sems, 0)
    ready()
    dn = dn_ref[...].astype(F32) + dn_near_ref[...].astype(F32) + dn_far_ref[...].astype(F32)
    cot = cot_ref[...].astype(F32)
    dvalues, dgain, dshift = norm_back(dn, res_ref[...], vector(vec_ref, GAIN + 2))
    dres = cot + dvalues
    dres_ref[...] = dres
    branch = dres.astype(BF)
    wait_all(copies)
    dout_ref[...] = dot_t(branch, full_ref[0]).astype(BF)
    rows_ref[0:1, :] = dgain
    rows_ref[1:2, :] = dshift
    rows_ref[2:3, :] = column_sum(branch)
    rows_ref[3:4, :] = column_sum(cot)


def middle_back_kernel(ready, slot_ref, vec_ref, dquery_ref, n_ref, res_ref, dres_ref, mixed_ref, cmixed_ref, *refs):
    pieces, (dout_res_ref, dout_ref, keep_ref, send_ref, rows_ref, full_ref, turned_ref, sems) = refs[:4], refs[4:]
    copies = start_copies(pieces, REST_AT, slot_ref, full_ref, sems, 0)
    ready()
    turned_ref[...] = n_ref[...].T
    dquery = dquery_ref[...]
    put_grad(0, turned_ref, dquery, slot_ref, keep_ref, send_ref)
    wait_all(copies)
    dn = dot_t(dquery, full_ref[0])
    dvalues, dgain, dshift = norm_back(dn, res_ref[...], vector(vec_ref, GAIN + 1))
    turned_ref[...] = cmixed_ref[...].T
    put_grad(2, turned_ref, dres_ref[...].astype(BF), slot_ref, keep_ref, send_ref)
    dres = dres_ref[...] + dvalues
    dout_res_ref[...] = dres
    branch = dres.astype(BF)
    dout_ref[...] = dot_t(branch, full_ref[1]).astype(BF)
    turned_ref[...] = mixed_ref[...].T
    put_grad(1, turned_ref, branch, slot_ref, keep_ref, send_ref)
    rows_ref[0:1, :] = dgain
    rows_ref[1:2, :] = dshift
    rows_ref[2:3, :] = column_sum(dquery)
    rows_ref[3:4, :] = column_sum(branch)


def total_of(parts):
    total = parts[0][0].astype(F32) + parts[1][0].astype(F32)
    for part in parts[2:]:
        total = total + part[...].astype(F32)
    return total.astype(BF)


def cross_back_kernel(count, ready, slot_ref, vec_ref, enc_ref, n_ref, dquery_ref, res_ref, out_ref, out_near_ref, out_far_ref, *refs):
    parts, pieces = refs[:count], refs[count : count + 4]
    denc_ref, layer_ref, keep_ref, send_ref, rows_ref, full_ref, turned_ref, turned_enc_ref, sems = refs[count + 4 :]
    copies = start_copies(pieces, PAIR_AT, slot_ref, full_ref, sems, 0)
    ready()
    turned_ref[...] = n_ref[...].T
    put_grad(2, turned_ref, dquery_ref[...], slot_ref, keep_ref, send_ref)
    dkv = total_of(parts)
    turned_enc_ref[...] = enc_ref[...].T
    put_grad(0, turned_enc_ref, dkv[0], slot_ref, keep_ref, send_ref)
    put_grad(1, turned_enc_ref, dkv[1], slot_ref, keep_ref, send_ref)
    rows_ref[0:1, :] = column_sum(dkv[1])
    out = out_ref[...].astype(F32) + out_near_ref[...].astype(F32) + out_far_ref[...].astype(F32)
    layer_ref[...] = (res_ref[...] + out + vector(vec_ref, DOWN)).astype(BF)
    wait_all(copies)
    denc_ref[...] = (dot_t(dkv[0], full_ref[0]) + dot_t(dkv[1], full_ref[1])).astype(BF)


def self_back_kernel(count, ready, slot_ref, vec_ref, x_ref, n_ref, dquery_ref, dres_ref, up_ref, up_far_ref, ffn_ref, mid_ref, enc_ref, *refs):
    parts, pieces = refs[:count], refs[count : count + 4]
    dx_ref, keep_ref, send_ref, full_ref, turned_ref, sems = refs[count + 4 :]
    copies = start_packed(pieces, slot_ref, full_ref, sems)
    ready()
    dkv = total_of(parts)
    dquery = dquery_ref[...]
    turned_ref[...] = n_ref[...].T
    shard = turned_ref.shape[0] // 4
    for j in range(4):
        place = pl.ds(pl.multiple_of(slot_ref[j] * shard, shard), shard)
        target = send_ref if j % 2 else keep_ref
        target[j // 2, 0:shard] = dot(turned_ref[place, :], dkv[0]).astype(BF)
        target[j // 2, shard : 2 * shard] = dot(turned_ref[place, :], dkv[1]).astype(BF)
    wait_all(copies)
    dn = dot_t(dquery, full_ref[0]) + dot_t(dkv[0], full_ref[1]) + dot_t(dkv[1], full_ref[2])
    dvalues, dgain, dshift = norm_back(dn, x_ref[...].astype(F32), vector(vec_ref, GAIN))
    dx_ref[...] = (dres_ref[...] + dvalues).astype(BF)
    rows = [
        dgain,
        mid_ref[0:1, :],
        ffn_ref[0:1, :],
        column_sum(dquery),
        column_sum(dkv[1]),
        mid_ref[3:4, :],
        mid_ref[2:3, :],
        enc_ref[0:1, :],
        ffn_ref[2:3, :],
        dshift,
        mid_ref[1:2, :],
        ffn_ref[1:2, :],
    ]
    common = jnp.concatenate(rows + [ffn_ref[3:4, :]], axis=0)
    rest = keep_ref.shape[1] - 2 * shard
    for p in range(4):
        up = jnp.where(slot_ref[0] == p, up_ref[0:1, :] + up_far_ref[0:1, :], 0.0)
        parts = [common[i : i + 1, p * shard : (p + 1) * shard] for i in range(common.shape[0])]
        parts += [up[:, i * shard : (i + 1) * shard] for i in range(4)]
        parts += [jnp.zeros_like(parts[0])] * (-len(parts) % 4)
        lines = [jnp.concatenate(parts[i : i + 4], axis=1) for i in range(0, len(parts), 4)]
        lines.append(jnp.zeros((rest - len(lines), common.shape[1]), F32))
        lines = jnp.concatenate(lines, axis=0).astype(BF)
        flip = lax.bitwise_xor(slot_ref[0], p)

        @pl.when(lax.rem(flip, 2) == 0)
        def _():
            keep_ref[lax.div(flip, 2), 2 * shard :] = lines

        @pl.when(lax.rem(flip, 2) == 1)
        def _():
            send_ref[lax.div(flip, 2), 2 * shard :] = lines


def last_kernel(ready, flag_ref, late_a, late_b, middle_a, middle_b, own_ref, attn_ref, out_ref, gain_ref, bias_ref, up_ref, down_ref):
    ready()
    shard = attn_ref.shape[1]

    def join(first, a_ref, b_ref):
        a, b = a_ref[...].astype(F32), b_ref[...].astype(F32)
        first = first == 0
        return jnp.concatenate([jnp.where(first, a, b), jnp.where(first, b, a)], axis=0)

    late, middle = join(flag_ref[0], late_a, late_b), join(flag_ref[1], middle_a, middle_b)
    own = own_ref[...].astype(F32)

    def part(whole, i):
        return whole[i * shard : (i + 1) * shard, :]

    for i, (whole, j) in enumerate([(late, 2), (own, 0), (own, 1), (middle, 0), (late, 0), (late, 1)]):
        attn_ref[i] = part(whole, j)
    out_ref[0] = part(middle, 1)
    out_ref[1] = part(middle, 2)
    sums = own[2 * shard :, :]

    def row(i):
        return sums[i // 4 : i // 4 + 1, (i % 4) * shard : (i % 4 + 1) * shard]

    gain_ref[...] = jnp.concatenate([row(i) for i in range(3)], axis=0)
    bias_ref[...] = jnp.concatenate([row(i) for i in range(3, 12)], axis=0)
    down_ref[...] = row(12)
    up_ref[...] = jnp.concatenate([row(i) for i in range(13, 17)], axis=1)


ROWS_CUT = 32
ROWS_SUM = 64
WHOLE = pl.BlockSpec(memory_space=pltpu.VMEM)
LEFT = pl.BlockSpec(memory_space=pltpu.HBM)
SCALARS = pl.BlockSpec(memory_space=pltpu.SMEM)


def cost(microseconds):
    return pl.CostEstimate(flops=0, bytes_accessed=int(microseconds * 3.5e6), transcendentals=0)


def dense(kernel, scalars, blocks, pieces, outs, scratch, microseconds, copies=None):
    copies = len(pieces) if copies is None else copies
    held = 2 * sum(math.prod(b.shape) * b.dtype.itemsize for b in blocks)
    held += sum(math.prod(shape) * jnp.dtype(kind).itemsize for shape, kind in outs)
    held += sum(math.prod(ref.shape) * jnp.dtype(ref.dtype).itemsize for ref in scratch)
    n_s, n_b, n_p, n_o = len(scalars), len(blocks), len(pieces), len(outs)

    def body(*refs):
        near, refs = refs[:n_s], refs[n_s:]
        far, refs = refs[:n_b], refs[n_b:]
        rest, refs = refs[: n_p + n_o], refs[n_p + n_o :]
        local, sems, refs = refs[:n_b], refs[n_b], refs[n_b + 1 :]
        fetches = [pltpu.make_async_copy(far[i], local[i], sems.at[i]) for i in range(n_b)]
        for fetch in fetches:
            fetch.start()

        def ready():
            for fetch in fetches:
                fetch.wait()

        kernel(ready, *near, *local, *rest, *refs)

    return pl.pallas_call(
        body,
        in_specs=[SCALARS] * n_s + [LEFT] * (n_b + n_p),
        out_specs=[pl.BlockSpec(shape, lambda d=len(shape): (0,) * d) for shape, _ in outs],
        out_shape=[jax.ShapeDtypeStruct(shape, kind) for shape, kind in outs],
        scratch_shapes=[pltpu.VMEM(b.shape, b.dtype) for b in blocks]
        + [pltpu.SemaphoreType.DMA((n_b,))]
        + scratch
        + ([pltpu.SemaphoreType.DMA((copies,))] if pieces else []),
        compiler_params=pltpu.CompilerParams(vmem_limit_bytes=60 * MIB),
        cost_estimate=cost(microseconds),
    )(*scalars, *blocks, *pieces)


def hold(*values):
    return lax.optimization_barrier(values)


def per_device(
    layer_in,
    encoded,
    pairing,
    attn_weight,
    out_weight,
    up_weight,
    down_weight,
    norm_gains,
    bias_rows,
    up_bias,
    down_bias,
    out_cotangent,
):
    seqs, local_rows, width = layer_in.shape
    outer = lax.axis_size("o")
    groups = outer * 2
    half = local_rows // 2
    shard = attn_weight.shape[1]
    hidden = up_weight.shape[1]
    blocks = hidden // width
    rows = LINE * half
    enc_rows = LINE * (encoded.shape[1] // 2)
    fx, y, z, o, core = (lax.axis_index(a) for a in ("fx", "y", "z", "o", "core"))

    vectors = jnp.concatenate(
        [norm_gains, bias_rows, up_bias.reshape(blocks, shard), down_bias.reshape(1, shard)], axis=0
    )
    vectors = jnp.pad(vectors, ((0, ROWS_CUT - vectors.shape[0]), (0, width - shard)))
    slots = jnp.stack([2 * fx + core, 2 * fx + 1 - core, 2 - 2 * fx + core, 3 - 2 * fx - core])
    qkv_shard = jnp.concatenate([attn_weight[:3].reshape(3 * shard, width), vectors], axis=0)
    qkv_other = lax.ppermute(qkv_shard, "fx", SWAP)
    qkv_near = between_cores(qkv_shard)
    qkv_near, layer_in, encoded = hold(qkv_near, layer_in, encoded)
    x_bf, enc_bf = deal([layer_in, encoded])

    def places_of(pairing):
        group = o * 2 + y
        spots = []
        for step in range(groups):
            source = lax.rem(group - step + groups, groups)
            for flip in range(2):
                c = core if flip == 0 else 1 - core
                k = 2 * lax.rem(z, 2) + c
                for r in range(LINE):
                    line = lax.rem(r - k + LINE, LINE)
                    spots.append((((source // 2) * LINE + line) * 2 + lax.rem(source, 2)) * 2 + c)
        spans = jnp.take(pairing.reshape(-1), jnp.stack(spots), axis=0)
        return (spans[:, None] * half + jnp.arange(half, dtype=jnp.int32)[None, :]).reshape(-1, 1)

    product = 2 * rows * width * width
    square = (width, width)
    act, real = ((rows, width), BF), ((rows, width), F32)
    turned = pltpu.VMEM((width, rows), BF)

    def weights(n):
        return pltpu.VMEM((n,) + square, BF)

    def grads(n):
        return [((2, n, shard, width), BF)] * 2

    note = ((16, width), F32)

    x_bf, enc_bf, qkv_other, qkv_near, attn_weight, out_weight, up_weight, out_cotangent, pairing = hold(
        x_bf, enc_bf, qkv_other, qkv_near, attn_weight, out_weight, up_weight, out_cotangent, pairing
    )
    pair_shard = attn_weight[4:]
    key_places = places_of(pairing)
    mid_shard = jnp.concatenate([attn_weight[4:], attn_weight[3:4], out_weight], axis=0)
    rest_shard = jnp.concatenate([attn_weight[3:4], out_weight], axis=0)
    w_qkv = (qkv_shard, qkv_near, qkv_other, between_cores(qkv_other))
    pair_other = lax.ppermute(pair_shard, "fx", SWAP)
    mid_near = between_cores(mid_shard)
    extra = ROWS_CUT
    n1, query, kv, vec = dense(
        self_in_kernel,
        [slots],
        [x_bf],
        w_qkv,
        [act, act, ((2, rows, width), BF), ((TABLE, width), F32)],
        [weights(3), pltpu.VMEM((4, extra, width), BF)],
        4,
        copies=16,
    )
    n1, query, kv, vec, up_weight, key_places, out_cotangent = hold(
        n1, query, kv, vec, up_weight, key_places, out_cotangent
    )
    places = (key_places, key_places[:rows].reshape(1, -1))
    kv_self = to_others(kv, groups)
    near_self = between_cores(kv)
    up_cut = up_weight.reshape(shard, 4, width).transpose(1, 0, 2)
    cot_halves = deal_halves(out_cotangent)
    pair_other, rest_shard, mid_near = hold(pair_other, rest_shard, mid_near)
    rest_other = lax.ppermute(rest_shard, "fx", SWAP)
    w_pair = (mid_shard, mid_near, pair_other, between_cores(pair_other))
    (kv,) = dense(
        cross_in_kernel, [slots], [vec, enc_bf], w_pair, [((2, enc_rows, width), BF)], [weights(2)], 3.5
    )
    kv_self, near_self, kv, cot_halves, up_cut = hold(kv_self, near_self, kv, cot_halves, up_cut)
    cot = deal_line(*cot_halves)
    kv_cross = to_others(kv, groups)
    near_cross = between_cores(kv)
    kv_self = [kv_self[0], near_self] + with_cores(kv_self[1:])
    mixed, mass = attention(query, kv_self, places)
    mixed, mass, up_cut, rest_other, kv_cross, near_cross, cot = hold(
        mixed, mass, up_cut, rest_other, kv_cross, near_cross, cot
    )
    cot = deal_order(cot)
    cot_other = lax.ppermute(cot, "fx", SWAP)
    cot_near = between_cores(cot)
    w_rest = (mid_shard, mid_near, rest_other, between_cores(rest_other))
    kv_cross = [kv_cross[0], near_cross] + with_cores(kv_cross[1:])
    r1, n2, cquery = dense(middle_kernel, [slots], [vec, mixed, x_bf], w_rest, [real, act, act], [weights(2)], 3.3)
    r1, n2, cquery, kv_cross, up_cut, cot_other, cot_near = hold(r1, n2, cquery, kv_cross, up_cut, cot_other, cot_near)
    up_own = lax.all_to_all(up_cut, ("fx", "core"), 0, 0, tiled=True).reshape(width, width)
    cmixed, cmass = attention(cquery, kv_cross, None)
    cmixed, cmass, cot_other, cot_near = hold(cmixed, cmass, cot_other, cot_near)
    r2, n3 = dense(before_feed_kernel, [slots], [vec, cmixed, r1], w_rest, [real, act], [weights(1)], 2.7)
    r2, n3, cot_other = hold(r2, n3, cot_other)
    n3_other = lax.ppermute(n3, "fx", SWAP)
    n3_near, cot_far = between_cores(n3), between_cores(cot_other)
    n3_near, cot_far, n3, cot = hold(n3_near, cot_far, n3, cot)
    two = ((2, rows, width), BF)

    def feed_two(normed, cots):
        return dense(
            feed_kernel,
            [],
            [vec, up_own, down_weight] + normed + cots,
            [],
            [act, act, act, act, two, two, ((8, width), F32)],
            [],
            5,
        )

    dn_keep, dn_send, out_keep, out_send, act_a, dpre_a, rows_a = feed_two([n3, n3_near], [cot, cot_near])
    n3_other, act_a, dpre_a, rows_a, dn_keep, dn_send, out_keep, out_send = hold(
        n3_other, act_a, dpre_a, rows_a, dn_keep, dn_send, out_keep, out_send
    )
    n3_far = between_cores(n3_other)
    dn_got, out_got = between_cores(dn_send), between_cores(out_send)
    cots, n3s = [cot, cot_near, cot_other, cot_far], [n3, n3_near, n3_other, n3_far]
    dn_other, dn_send_b, out_other, out_send_b, act_b, dpre_b, rows_b = feed_two(n3s[2:], cots[2:])

    single = outer == 1

    def step(terms, name):
        return halve(terms, name) if single else terms

    def hold_all(*values):
        flat = hold([[term[0] for term in v] if isinstance(v, list) else v for v in values])[0]
        return [
            [(array, term[1]) for array, term in zip(new, old)] if isinstance(old, list) else new
            for new, old in zip(flat, values)
        ]

    dn_other_got = between_cores(dn_send_b)
    dn_other, dn_other_got, act_b, dpre_b, dn_got, out_got, out_send_b = hold(
        dn_other, dn_other_got, act_b, dpre_b, dn_got, out_got, out_send_b
    )
    dn_far = lax.ppermute(add([dn_other, dn_other_got]), "fx", SWAP)
    cut = ((4, 2, 4, shard // 4, width // 2), BF)
    up, down = dense(
        feed_grad_kernel, [], [act_a, act_b, dpre_a, dpre_b] + n3s + cots, [], [cut, cut], [], 6
    )
    dn_far, up, down, out_other, out_send_b = hold(dn_far, up, down, out_other, out_send_b)
    up, down = ([(part.reshape((2, 2, 2) + part.shape[2:]), ())] for part in (up, down))
    up, down = step(up, "y"), step(down, "z0")
    out_other_got = between_cores(out_send_b)
    dr2, doc, ffn_rows = dense(
        after_feed_kernel, [slots], [vec, dn_keep, dn_got, dn_far, r2, cot], w_rest, [real, act, note], [weights(1)], 2.7
    )

    dcq, cmine, ctheirs = attention_back(cquery, doc, cmixed, cmass, kv_cross, None)
    dcq, cmine, ctheirs, dr2, ffn_rows, out_other, out_other_got, up, down = hold_all(
        dcq, cmine, ctheirs, dr2, ffn_rows, out_other, out_other_got, up, down
    )
    cgot = between_cores(ctheirs)
    dr1, dos, middle_keep, middle_send, mid_rows = dense(
        middle_back_kernel,
        [slots],
        [vec, dcq, n2, r1, dr2, mixed, cmixed],
        w_rest,
        [real, act] + grads(3) + [note],
        [weights(2), turned],
        6,
    )
    dr1, dos, middle_keep, middle_send, mid_rows, cgot, cmine, up, down, out_other, out_other_got = hold_all(
        dr1, dos, middle_keep, middle_send, mid_rows, cgot, cmine, up, down, out_other, out_other_got
    )
    dckv = collect(cmine, cgot, groups)
    middle = over_cores(middle_keep, middle_send)
    up, down = step(up, "z0"), step(down, "z1")
    out_far = lax.ppermute(add([out_other, out_other_got]), "fx", SWAP)
    dq, mine, theirs = attention_back(query, dos, mixed, mass, kv_self, places)
    dq, mine, theirs, middle, up, down, out_far, dckv_a = hold_all(dq, mine, theirs, middle, up, down, out_far, dckv[-1])
    dckv = dckv[:-1] + [dckv_a]
    got = between_cores(theirs)
    grad_encoded, layer_out, late_keep, late_send, enc_rows_sum = dense(
        functools.partial(cross_back_kernel, len(dckv)),
        [slots],
        [vec, enc_bf, n1, dq, r2, out_keep, out_got, out_far] + dckv,
        w_pair,
        [((enc_rows, width), BF), act] + grads(3) + [note],
        [weights(2), turned, pltpu.VMEM((width, enc_rows), BF)],
        6,
    )
    mine, got, grad_encoded, layer_out, late_keep, late_send, enc_rows_sum, up, down, middle = hold_all(
        mine, got, grad_encoded, layer_out, late_keep, late_send, enc_rows_sum, up, down, middle
    )
    dkv = collect(mine, got, groups)
    late = over_cores(late_keep, late_send)
    late = over_x(late)
    if single:
        at = {name: half_index(name) for name in HALVES}
        middle = [array.reshape(2, 2, 2, 2, -1, width) for array, _ in middle]
        middle_z0 = exchange(add([pick(array, (1, 1 - at["z0"])) for array in middle]), "z0")
        up, down = both_halves(up, "z1"), both_halves(down, "y")
        dkv_last, up, down, late, middle, middle_z0 = hold_all(
            dkv[-1], [(part, ()) for part in up], [(part, ()) for part in down], late, [(part, ()) for part in middle], middle_z0
        )
        home = undeal_line([grad_encoded, layer_out])
        middle = [(array, (1, ("at", 1, at["z0"]))) for array, _ in middle] + [(middle_z0, (1,))]
        middle_x = lax.ppermute(add([half_of(term)[1] for term in middle]), "fx", SWAP)
        late = halve(late, "y")
    else:
        middle = over_x(middle)
        dkv_last, late, middle = hold_all(dkv[-1], late, middle)
    dkv = dkv[:-1] + [dkv_last]
    grad_layer, keep, send = dense(
        functools.partial(self_back_kernel, len(dkv)),
        [slots],
        [vec, x_bf, n1, dq, dr1, rows_a, rows_b, ffn_rows, mid_rows, enc_rows_sum] + dkv,
        w_qkv,
        [act] + [((2, 2 * shard + ROWS_SUM, width), BF)] * 2,
        [weights(3), turned],
        7,
        copies=12,
    )
    if single:
        grad_layer, keep, send, late, up, down, middle_x = hold_all(
            grad_layer, keep, send, late, up, down, middle_x
        )
        up, down = (add([part for part, _ in parts]) for parts in (up, down))
        up = lax.all_to_all(up, ("fx", "core"), 1, 1, tiled=True)
        own = over_cores(keep, send)
        middle = [(array, names + (0,)) for array, names in middle] + [(middle_x, (1,))]
        home = undeal_cores(home)
        down, late, middle = double(down, "z1"), halve(late, "z0"), halve(middle, "y")
        own, up, home, down, grad_layer = hold_all(own, up, [(p, ()) for p in home], down, grad_layer)
        own = over_x(own)
        last = undeal_line([grad_layer])
        up = double(up, "z0")
        late, middle = both_halves(late, "z1"), both_halves(middle, "z1")
        own, home, up, down, last = hold_all(own, home, up, down, last)
        late, middle = [(p, ()) for p in late], [(p, ()) for p in middle]
        grad_encoded, layer_out = undealt([p for p, _ in home], [F32, BF])
        last = undeal_cores(last)
        late, middle = (add([part for part, _ in parts]) for parts in (late, middle))
        own = add([array[0] if 0 in names else array for array, names in own]).reshape(2 * LINE, -1, width)
        own = lax.all_to_all(own, ("z", "y"), 0, 0, tiled=True)
        late, middle = double(late, "z0"), double(middle, "y")
        up, down = double(up, "y"), double(down, "z0")
        own, late, middle, last = hold(own, late, middle, last)
        own = jnp.sum(own.astype(F32), axis=0, keepdims=True).astype(BF)
        own = lax.all_to_all(jnp.broadcast_to(own, (2 * LINE,) + own.shape[1:]), ("z", "y"), 0, 0, tiled=True)
        late, middle = (late, exchange(late, "y")), (middle, exchange(middle, "z0"))
        flags = jnp.stack([half_index("y"), half_index("z0")])
        (grad_layer,) = undealt(last, [F32])
        grad_attn, grad_out, *total = dense(
            last_kernel,
            [flags],
            [part.reshape(-1, width) for part in late + middle + (own,)],
            [],
            [((6, shard, width), F32), ((2, shard, width), F32), ((3, shard), F32), ((9, shard), F32)]
            + [((1, blocks * shard), F32), ((1, shard), F32)],
            [],
            3,
        )
        up, down = (part.astype(F32).reshape(2, 2, 2, 4, shard // 4, width // 2) for part in (up, down))
    else:
        own = over_cores(keep, send)
        (grad_layer,) = undeal([grad_layer], [F32])
        (grad_encoded,), (layer_out,) = undeal([grad_encoded], [F32]), undeal([layer_out], [BF])

        def over_ctx(terms, n):
            total = add([array[0] if 0 in names else array for array, names in terms])
            return lax.psum(total, ("o", "z", "y")).astype(F32).reshape(n, -1, width)

        own, middle, late = over_ctx(over_x(own), 1)[0], over_ctx(middle, 3), over_ctx(late, 3)
        up, down = (lax.psum(part[0][0], ("o", "z", "y")).astype(F32) for part in (up, down))
        up = lax.all_to_all(up.astype(BF), ("fx", "core"), 3, 3, tiled=True).astype(F32)
        total = own[2 * shard : 2 * shard + 5].reshape(-1, shard)
        total = [total[:3], total[3:12], total[13 : 13 + blocks].reshape(1, -1), total[12:13]]
        own = own[: 2 * shard].reshape(2, shard, width)
        grad_attn = jnp.concatenate([late[2:], own, middle[:1], late[:2]], axis=0)
        grad_out = middle[1:]
    g_up = up.transpose(0, 1, 4, 3, 2, 5).reshape(shard, hidden)
    g_down = down.transpose(3, 0, 1, 4, 2, 5).reshape(hidden // 4, width)
    return (
        layer_out,
        grad_layer,
        grad_encoded,
        grad_attn,
        grad_out,
        g_up,
        g_down,
        total[0],
        total[1],
        total[2].reshape(-1),
        total[3].reshape(-1),
    )


def solution(mesh):
    ctx = mesh.shape["ctx"]
    grid = Mesh(mesh.devices.reshape(2, 2, ctx // (2 * LINE), LINE, 2), ("fx", "core", "o", "z", "y"))
    fsdp = ("fx", "core")
    rows = P(fsdp, ("o", "z", "y"), None)
    weights = (
        P(None, fsdp, None),
        P(None, fsdp, None),
        P(fsdp, None),
        P(fsdp, None),
        P(None, fsdp),
        P(None, fsdp),
        P(fsdp),
        P(fsdp),
    )
    return jax.shard_map(
        per_device,
        mesh=grid,
        in_specs=(rows, rows, P()) + weights + (rows,),
        out_specs=(rows, rows, rows) + weights,
        check_vma=False,
    )
```

```python
import functools
import math

import jax
import jax.numpy as jnp
from jax import lax
from jax.experimental import pallas as pl
from jax.experimental.pallas import tpu as pltpu
from jax.sharding import Mesh
from jax.sharding import PartitionSpec as P

HEADS = 12
HD = 64
PAIR = 2 * HD
SCORE_SCALE = 0.125
MASK_FILL = -1e30
NORM_EPSILON = 1e-05
LINE = 4
SWAP = [(0, 1), (1, 0)]
BF = jnp.bfloat16
F32 = jnp.float32
MIB = 1 << 20


def dot(left, right):
    return jnp.dot(left, right, preferred_element_type=F32)


def dot_t(left, right):
    return lax.dot_general(left, right, (((1,), (1,)), ((), ())), preferred_element_type=F32)


def t_dot(left, right):
    return lax.dot_general(left, right, (((0,), (0,)), ((), ())), preferred_element_type=F32)


def split_heads(block):
    lane = lax.broadcasted_iota(jnp.int32, block.shape, 1)
    zero = jnp.zeros_like(block)
    return jnp.concatenate([jnp.where(lane < HD, block, zero), jnp.where(lane < HD, zero, block)], axis=0)


def join_heads(columns):
    rows = columns.shape[1] // 2
    return jnp.concatenate([columns[:HD, :rows], columns[HD:, rows:]], axis=0).T


def forward_kernel(masked, pieces, *refs):
    if masked:
        key_place_ref, query_place_ref, refs = refs[0], refs[1], refs[2:]
    query_ref, kv_refs = refs[0], refs[1 : 1 + pieces]
    out_ref, mass_ref, scores_ref = refs[1 + pieces :]
    query = split_heads(query_ref[...] * jnp.asarray(SCORE_SCALE, BF))
    piece = kv_refs[0].shape[1]
    if masked:
        query_place = query_place_ref[...]
        query_place = jnp.concatenate([query_place, query_place], axis=1)
    top = None
    for i in range(pieces):
        scores = dot_t(kv_refs[i][0], query)
        if masked:
            scores = jnp.where(key_place_ref[pl.ds(i * piece, piece), :] <= query_place, scores, MASK_FILL)
        scores_ref[pl.ds(i * piece, piece), :] = scores
        high = jnp.max(scores, axis=0, keepdims=True)
        top = high if top is None else jnp.maximum(top, high)
    mass = jnp.zeros_like(top)
    mixed = None
    for i in range(pieces):
        probs = jnp.exp(scores_ref[pl.ds(i * piece, piece), :] - top)
        mass = mass + jnp.sum(probs, axis=0, keepdims=True)
        part = t_dot(kv_refs[i][1], probs.astype(BF))
        mixed = part if mixed is None else mixed + part
    out_ref[...] = join_heads(mixed * (1.0 / mass)).astype(BF)
    mass_ref[0] = top + jnp.log(mass)


def backward_kernel(masked, pieces, *refs):
    if masked:
        key_place_ref, query_place_ref, refs = refs[0], refs[1], refs[2:]
    query_ref, dout_ref, out_ref, mass_ref = refs[:4]
    kv_refs = refs[4 : 4 + pieces]
    dquery_ref, mine_ref, theirs_ref = refs[4 + pieces :]
    query = split_heads(query_ref[...] * jnp.asarray(SCORE_SCALE, BF))
    dout = dout_ref[...]
    prod = (dout.astype(F32) * out_ref[...].astype(F32)).T
    delta = jnp.concatenate(
        [jnp.sum(prod[:HD], axis=0, keepdims=True), jnp.sum(prod[HD:], axis=0, keepdims=True)], axis=1
    )
    dout = split_heads(dout)
    log_mass = mass_ref[0]
    piece = kv_refs[0].shape[1]
    if masked:
        query_place = query_place_ref[...]
        query_place = jnp.concatenate([query_place, query_place], axis=1)
    dquery = None
    for i in range(pieces):
        keys = kv_refs[i][0]
        scores = dot_t(keys, query)
        if masked:
            scores = jnp.where(key_place_ref[pl.ds(i * piece, piece), :] <= query_place, scores, MASK_FILL)
        probs = jnp.exp(scores - log_mass)
        dprobs = dot_t(kv_refs[i][1], dout)
        dscores = (probs * (dprobs - delta)).astype(BF)
        dkv_ref = theirs_ref if i % 2 else mine_ref
        dkv_ref[i // 2, 0] = dot(dscores, query).astype(BF)
        dkv_ref[i // 2, 1] = dot(probs.astype(BF), dout).astype(BF)
        part = t_dot(keys, dscores)
        dquery = part if dquery is None else dquery + part
    dquery_ref[...] = (join_heads(dquery) * SCORE_SCALE).astype(BF)


def place_specs(masked, places):
    if not masked:
        return [], []
    key_places, query_places = places
    return [key_places, query_places], [
        pl.BlockSpec(key_places.shape, lambda h: (0, 0)),
        pl.BlockSpec(query_places.shape, lambda h: (0, 0)),
    ]


def attention(query, kv, places):
    masked = places is not None
    rows, width = query.shape
    piece = kv[0].shape[1]
    extra, extra_specs = place_specs(masked, places)
    keys = piece * len(kv)
    return pl.pallas_call(
        functools.partial(forward_kernel, masked, len(kv)),
        grid=(width // PAIR,),
        in_specs=extra_specs
        + [pl.BlockSpec((rows, PAIR), lambda h: (0, h))]
        + [pl.BlockSpec((2, piece, PAIR), lambda h: (0, 0, h))] * len(kv),
        out_specs=[
            pl.BlockSpec((rows, PAIR), lambda h: (0, h)),
            pl.BlockSpec((1, 1, 2 * rows), lambda h: (h, 0, 0)),
        ],
        out_shape=[
            jax.ShapeDtypeStruct((rows, width), BF),
            jax.ShapeDtypeStruct((width // PAIR, 1, 2 * rows), F32),
        ],
        scratch_shapes=[pltpu.VMEM((keys, 2 * rows), F32)],
        compiler_params=pltpu.CompilerParams(vmem_limit_bytes=60 * MIB),
        cost_estimate=cost(8 * rows * keys / 2**18),
    )(*extra, query, *kv)


def attention_back(query, dout, out, mass, kv, places):
    masked = places is not None
    rows, width = query.shape
    piece = kv[0].shape[1]
    extra, extra_specs = place_specs(masked, places)
    keys = piece * len(kv)
    column = pl.BlockSpec((rows, PAIR), lambda h: (0, h))
    pair = pl.BlockSpec((2, piece, PAIR), lambda h: (0, 0, h))
    groups = len(kv) // 2
    blocks = pl.BlockSpec((groups, 2, piece, PAIR), lambda h: (0, 0, 0, h))
    return pl.pallas_call(
        functools.partial(backward_kernel, masked, len(kv)),
        grid=(width // PAIR,),
        in_specs=extra_specs
        + [column, column, column, pl.BlockSpec((1, 1, 2 * rows), lambda h: (h, 0, 0))]
        + [pair] * len(kv),
        out_specs=[column, blocks, blocks],
        out_shape=[jax.ShapeDtypeStruct((rows, width), BF)]
        + [jax.ShapeDtypeStruct((groups, 2, piece, width), BF)] * 2,
        compiler_params=pltpu.CompilerParams(vmem_limit_bytes=60 * MIB),
        cost_estimate=cost(13 * rows * keys / 2**18),
    )(*extra, query, dout, out, mass, *kv)


def deal_perms():
    perms = []
    for r in range(LINE):
        perm = []
        for c in range(2):
            for z in range(LINE):
                k = (r - z) % LINE
                perm.append((c * LINE + z, (k % 2) * LINE + 2 * c + k // 2))
        perms.append(perm)
    return perms


DEAL = deal_perms()


def deal(arrays):
    if len({array.shape for array in arrays}) > 1:
        return [deal([array])[0] for array in arrays]
    _, rows, width = arrays[0].shape
    chunks = [array.reshape(LINE, rows // 2, width) for array in arrays]
    z = lax.axis_index("z")
    got = []
    for r in range(LINE):
        k = lax.rem(r - z + LINE, LINE)
        chunk = jnp.stack([lax.dynamic_index_in_dim(c, k, keepdims=False) for c in chunks])
        got.append(lax.ppermute(chunk, ("core", "z"), DEAL[r]))
    return [jnp.concatenate([g[i] for g in got], axis=0) for i in range(len(arrays))]


def undeal_line(arrays):
    core, z = lax.axis_index("core"), lax.axis_index("z")
    chunks = jnp.stack([array.reshape(LINE, -1, array.shape[-1]) for array in arrays], axis=1)
    start = lax.rem(2 * lax.rem(z, 2) + core, LINE)
    chunks = lax.dynamic_slice_in_dim(jnp.concatenate([chunks, chunks], axis=0), start, LINE, axis=0)
    return lax.all_to_all(chunks, "z", 0, 0, tiled=True)


def undeal_cores(chunks):
    core = lax.axis_index("core")
    chunks = chunks.reshape((2, 2) + chunks.shape[1:])
    mine = lax.dynamic_index_in_dim(chunks, core, 0, keepdims=False)
    return mine, lax.ppermute(lax.dynamic_index_in_dim(chunks, 1 - core, 0, keepdims=False), "core", SWAP)


def undealt(halves, kinds):
    first = lax.axis_index("core") == 0
    outs = []
    for i, kind in enumerate(kinds):
        mine, got = (half[:, i].astype(kind) for half in halves)
        both = jnp.where(first, jnp.stack([mine, got], axis=1), jnp.stack([got, mine], axis=1))
        outs.append(both.reshape(2, -1, both.shape[-1]))
    return outs


def deal_halves(array):
    _, rows, width = array.shape
    parts = array.reshape(2, 2, rows // 2, width)
    core = lax.axis_index("core")
    mine = lax.dynamic_index_in_dim(parts, core, 1, keepdims=False)
    return mine, lax.ppermute(lax.dynamic_index_in_dim(parts, 1 - core, 1, keepdims=False), "core", SWAP)


def deal_line(mine, got):
    first = lax.axis_index("core") == 0
    chunks = jnp.where(first, jnp.concatenate([mine, got], axis=0), jnp.concatenate([got, mine], axis=0))
    return lax.all_to_all(chunks, "z", 0, 0, tiled=True)


def deal_order(chunks):
    core, z = lax.axis_index("core"), lax.axis_index("z")
    start = lax.rem(LINE - 2 * lax.rem(z, 2) - core, LINE)
    mine = lax.dynamic_slice_in_dim(jnp.concatenate([chunks, chunks], axis=0), start, LINE, axis=0)
    return mine.reshape(-1, mine.shape[-1])


def undeal(arrays, kind):
    count = len(arrays)
    half = arrays[0].shape[0] // LINE
    got = []
    for r in range(LINE):
        chunk = jnp.stack([array[r * half : (r + 1) * half] for array in arrays])
        got.append(lax.ppermute(chunk, ("core", "z"), [(b, a) for a, b in DEAL[r]]))
    z = lax.axis_index("z")
    outs = []
    for i in range(count):
        mine = lax.dynamic_slice_in_dim(jnp.stack([g[i] for g in got + got]), z, LINE, axis=0)
        outs.append(mine.reshape(2, 2 * half, arrays[0].shape[1]).astype(kind[i]))
    return outs


def group_perm(groups, step):
    return [(i, (i + step) % groups) for i in range(groups)]


def to_others(own, groups):
    return [own] + [lax.ppermute(own, ("o", "y"), group_perm(groups, step)) for step in range(1, groups)]


def with_cores(blocks):
    pieces = []
    for block in blocks:
        pieces += [block, lax.ppermute(block, "core", SWAP)]
    return pieces


def collect(mine, got, groups):
    terms = [mine, got]
    for step in range(1, groups):
        back = [(b, a) for a, b in group_perm(groups, step)]
        terms.append(lax.ppermute(add([mine[step], got[step]]), ("o", "y"), back))
    return terms


def between_cores(array):
    return lax.ppermute(array, "core", SWAP)


def gather(own, other):
    return own, lax.ppermute(own, "core", SWAP), other, lax.ppermute(other, "core", SWAP)


def after(value, earlier):
    return lax.optimization_barrier((value, earlier))[0]


def add(terms):
    total = terms[0].astype(F32)
    for term in terms[1:]:
        total = total + term.astype(F32)
    return total.astype(BF)


def over_cores(keep, send):
    return [(keep, ()), (lax.ppermute(send, "core", SWAP), ())]


def over_x(terms):
    got = lax.ppermute(add([array[1] for array, _ in terms]), "fx", SWAP)
    return [(array, (0,)) for array, _ in terms] + [(got, ())]


def part_over_x(terms, first, last):
    return lax.ppermute(add([array[1, first:last] for array, _ in terms]), "fx", SWAP)


def pick(array, *path):
    for axis, index in path:
        array = lax.dynamic_index_in_dim(array, index, axis, keepdims=False)
    return array


HALVES = ("y", "z0", "z1")


def exchange(array, name):
    if name == "y":
        return lax.ppermute(array, "y", SWAP)
    flip = 1 if name == "z0" else 2
    return lax.ppermute(array, "z", [(i, i ^ flip) for i in range(LINE)])


def half_index(name):
    z = lax.axis_index("z")
    return lax.axis_index("y") if name == "y" else lax.rem(z, 2) if name == "z0" else lax.div(z, 2)


def half_of(term, more=()):
    array, names = term
    cut = 1 in names
    if 0 in names and 1 not in names and len(names + more) > 1:
        array = array.reshape(2, 2, 2, 2, -1, array.shape[-1])
        cut = True
    for name in names + more:
        if name in (0, 1):
            array = array if name else array[0]
            continue
        if name[0] == "at":
            array = pick(array, name[1:])
            continue
        name, other = name if isinstance(name, tuple) else (name, False)
        if array.ndim == 3 and not cut:
            array = array.reshape(2, 2, 2, -1, array.shape[-1])
        cut = True
        i = half_index(name)
        array = lax.dynamic_index_in_dim(array, 1 - i if other else i, 0, keepdims=False)
    return array


def halve(terms, name):
    theirs = add([half_of(term, ((name, True),)) for term in terms])
    got = exchange(theirs, name)
    return [(array, names + (name,)) for array, names in terms] + [(got, (1,))]


def both_halves(terms, name):
    mine = add([half_of(term) for term in terms])
    got = exchange(mine, name)
    mine = lax.optimization_barrier(mine)
    return mine, got


def double(part, name):
    other = exchange(part, name)
    first = half_index(name) == 0
    return jnp.where(first, jnp.concatenate([part, other], axis=0), jnp.concatenate([other, part], axis=0))


def standard(values):
    center = values - jnp.mean(values, axis=-1, keepdims=True)
    inverse = lax.rsqrt(jnp.mean(center * center, axis=-1, keepdims=True) + NORM_EPSILON)
    return center * inverse, inverse


def norm_back(dnormed, values, gain):
    z, inverse = standard(values)
    a = dnormed * gain
    dvalues = (
        a - jnp.mean(a, axis=-1, keepdims=True) - z * jnp.mean(a * z, axis=-1, keepdims=True)
    ) * inverse
    return dvalues, jnp.sum(dnormed * z, axis=0, keepdims=True), jnp.sum(dnormed, axis=0, keepdims=True)


def column_sum(values):
    return jnp.sum(values.astype(F32), axis=0, keepdims=True)


GAIN, BIAS, UP, DOWN = 0, 3, 12, 13
TABLE = 24
PAIR_AT, REST_AT, LAST_AT = (0, 0, 0, 0), (2, 2, 0, 0), (4, 4, 2, 2)


def vector(vec_ref, row):
    return vec_ref[row : row + 1, :]


def start_packed(pieces, slot_ref, full_ref, sems):
    n, rows = full_ref.shape[0], full_ref.shape[1] // 4
    copies = []
    for j, piece in enumerate(pieces):
        place = pl.ds(pl.multiple_of(slot_ref[j] * rows, rows), rows)
        for i in range(n):
            copy = pltpu.make_async_copy(
                piece.at[pl.ds(i * rows, rows), :], full_ref.at[i, place, :], sems.at[j * n + i]
            )
            copy.start()
            copies.append(copy)
    return copies


def start_copies(pieces, firsts, slot_ref, full_ref, sems, base):
    copies = []
    for j, piece in enumerate(pieces):
        rows = piece.shape[-2]
        place = pl.ds(pl.multiple_of(slot_ref[j] * rows, rows), rows)
        if len(piece.shape) == 3:
            source, target = piece.at[pl.ds(firsts[j], full_ref.shape[0])], full_ref.at[:, place, :]
        else:
            source, target = piece, full_ref.at[place, :]
        copy = pltpu.make_async_copy(source, target, sems.at[base + j])
        copy.start()
        copies.append(copy)
    return copies


def wait_all(copies):
    for copy in copies:
        copy.wait()


def put_grad(unit, turned, right, slot_ref, keep_ref, send_ref):
    rows = turned.shape[0] // 4
    for j in range(4):
        place = pl.ds(pl.multiple_of(slot_ref[j] * rows, rows), rows)
        block = dot(turned[place, :], right).astype(BF)
        target = send_ref if j % 2 else keep_ref
        target[j // 2, unit] = block


def self_in_kernel(ready, slot_ref, x_ref, *refs):
    pieces, (n_ref, query_ref, kv_ref, vec_ref, full_ref, parts_ref, sems) = refs[:4], refs[4:]
    weights, shard = full_ref.shape[0], full_ref.shape[1] // 4
    extra = parts_ref.shape[1]
    small = []
    for j, piece in enumerate(pieces):
        copy = pltpu.make_async_copy(
            piece.at[pl.ds(weights * shard, extra), :], parts_ref.at[j], sems.at[4 * weights + j]
        )
        copy.start()
        small.append(copy)
    copies = start_packed(pieces, slot_ref, full_ref, sems)
    ready()
    z = standard(x_ref[...].astype(F32))[0]
    wait_all(small)
    parts = [parts_ref[lax.bitwise_xor(slot_ref[0], p)].astype(F32)[:, :shard] for p in range(4)]
    own = parts_ref[0].astype(F32)[:, :shard]
    table = jnp.concatenate(parts, axis=1)
    vec_ref[0:UP, :] = table[0:UP]
    vec_ref[UP:DOWN, :] = jnp.concatenate([own[UP + i : UP + i + 1] for i in range(4)], axis=1)
    vec_ref[DOWN : DOWN + 1, :] = table[UP + 4 : UP + 5]
    normed = (z * table[GAIN : GAIN + 1] + table[BIAS + 6 : BIAS + 7]).astype(BF)
    n_ref[...] = normed
    wait_all(copies)
    kv_ref[0] = dot(normed, full_ref[1]).astype(BF)
    kv_ref[1] = (dot(normed, full_ref[2]) + table[BIAS + 1 : BIAS + 2]).astype(BF)
    query_ref[...] = (dot(normed, full_ref[0]) + table[BIAS : BIAS + 1]).astype(BF)


def cross_in_kernel(ready, slot_ref, vec_ref, enc_ref, *refs):
    pieces, (kv_ref, full_ref, sems) = refs[:4], refs[4:]
    copies = start_copies(pieces, PAIR_AT, slot_ref, full_ref, sems, 0)
    ready()
    enc = enc_ref[...]
    wait_all(copies)
    kv_ref[0] = dot(enc, full_ref[0]).astype(BF)
    kv_ref[1] = (dot(enc, full_ref[1]) + vector(vec_ref, BIAS + 4)).astype(BF)


def middle_kernel(ready, slot_ref, vec_ref, mixed_ref, x_ref, *refs):
    pieces, (res_ref, n_ref, query_ref, full_ref, sems) = refs[:4], refs[4:]
    copies = start_copies(pieces, REST_AT, slot_ref, full_ref, sems, 0)
    ready()
    wait_all(copies)
    res = x_ref[...].astype(F32) + dot(mixed_ref[...], full_ref[1]) + vector(vec_ref, BIAS + 2)
    res_ref[...] = res
    normed = (standard(res)[0] * vector(vec_ref, GAIN + 1) + vector(vec_ref, BIAS + 7)).astype(BF)
    n_ref[...] = normed
    query_ref[...] = (dot(normed, full_ref[0]) + vector(vec_ref, BIAS + 3)).astype(BF)


def before_feed_kernel(ready, slot_ref, vec_ref, mixed_ref, res_ref, *refs):
    pieces, (out_ref, n_ref, full_ref, sems) = refs[:4], refs[4:]
    copies = start_copies(pieces, LAST_AT, slot_ref, full_ref, sems, 0)
    ready()
    wait_all(copies)
    res = res_ref[...] + dot(mixed_ref[...], full_ref[0]) + vector(vec_ref, BIAS + 5)
    out_ref[...] = res
    n_ref[...] = (standard(res)[0] * vector(vec_ref, GAIN + 2) + vector(vec_ref, BIAS + 8)).astype(BF)


def feed_kernel(ready, vec_ref, up_ref, down_ref, *refs):
    normed_refs, cot_refs = refs[:2], refs[2:4]
    dn_keep, dn_send, out_keep, out_send, act_ref, dpre_ref, rows_ref = refs[4:]
    ready()
    bias = vector(vec_ref, UP)
    total = None
    for j in (1, 0):
        pre = dot(normed_refs[j][...], up_ref[...]) + bias
        phi = 0.5 * (1.0 + lax.erf(pre * math.sqrt(0.5)))
        slope = phi + pre * (jnp.exp(-0.5 * pre * pre) * (1.0 / math.sqrt(2.0 * math.pi)))
        act = (pre * phi).astype(BF)
        dpre = (dot_t(cot_refs[j][...], down_ref[...]) * slope).astype(BF)
        out, dn = (out_send, dn_send) if j else (out_keep, dn_keep)
        dn[...] = dot_t(dpre, up_ref[...]).astype(BF)
        out[...] = dot(act, down_ref[...]).astype(BF)
        act_ref[j] = act
        dpre_ref[j] = dpre
        sums = column_sum(dpre)
        total = sums if total is None else total + sums
    rows_ref[0:1, :] = total


def feed_grad_kernel(ready, act_a, act_b, dpre_a, dpre_b, *refs):
    normed_refs, cot_refs, (up_ref, down_ref) = refs[:4], refs[4:8], refs[8:]
    quarter, half = up_ref.shape[-2:]
    ready()

    def put(grad, cut_ref):
        for p in range(4):
            for q in range(4):
                rows = grad[(4 * p + q) * quarter : (4 * p + q + 1) * quarter].astype(BF)
                cut_ref[q, 0, p] = rows[:, :half]
                cut_ref[q, 1, p] = rows[:, half:]

    total = None
    for j in range(4):
        part = t_dot(normed_refs[j][...], (dpre_b if j > 1 else dpre_a)[j % 2])
        total = part if total is None else total + part
    put(total, up_ref)
    total = None
    for j in range(4):
        part = t_dot((act_b if j > 1 else act_a)[j % 2], cot_refs[j][...])
        total = part if total is None else total + part
    put(total, down_ref)


def after_feed_kernel(ready, slot_ref, vec_ref, dn_ref, dn_near_ref, dn_far_ref, res_ref, cot_ref, *refs):
    pieces, (dres_ref, dout_ref, rows_ref, full_ref, sems) = refs[:4], refs[4:]
    copies = start_copies(pieces, LAST_AT, slot_ref, full_ref, sems, 0)
    ready()
    dn = dn_ref[...].astype(F32) + dn_near_ref[...].astype(F32) + dn_far_ref[...].astype(F32)
    cot = cot_ref[...].astype(F32)
    dvalues, dgain, dshift = norm_back(dn, res_ref[...], vector(vec_ref, GAIN + 2))
    dres = cot + dvalues
    dres_ref[...] = dres
    branch = dres.astype(BF)
    wait_all(copies)
    dout_ref[...] = dot_t(branch, full_ref[0]).astype(BF)
    rows_ref[0:1, :] = dgain
    rows_ref[1:2, :] = dshift
    rows_ref[2:3, :] = column_sum(branch)
    rows_ref[3:4, :] = column_sum(cot)


def middle_back_kernel(ready, slot_ref, vec_ref, dquery_ref, n_ref, res_ref, dres_ref, mixed_ref, cmixed_ref, *refs):
    pieces, (dout_res_ref, dout_ref, keep_ref, send_ref, rows_ref, full_ref, turned_ref, sems) = refs[:4], refs[4:]
    copies = start_copies(pieces, REST_AT, slot_ref, full_ref, sems, 0)
    ready()
    turned_ref[...] = n_ref[...].T
    dquery = dquery_ref[...]
    put_grad(0, turned_ref, dquery, slot_ref, keep_ref, send_ref)
    wait_all(copies)
    dn = dot_t(dquery, full_ref[0])
    dvalues, dgain, dshift = norm_back(dn, res_ref[...], vector(vec_ref, GAIN + 1))
    turned_ref[...] = cmixed_ref[...].T
    put_grad(2, turned_ref, dres_ref[...].astype(BF), slot_ref, keep_ref, send_ref)
    dres = dres_ref[...] + dvalues
    dout_res_ref[...] = dres
    branch = dres.astype(BF)
    dout_ref[...] = dot_t(branch, full_ref[1]).astype(BF)
    turned_ref[...] = mixed_ref[...].T
    put_grad(1, turned_ref, branch, slot_ref, keep_ref, send_ref)
    rows_ref[0:1, :] = dgain
    rows_ref[1:2, :] = dshift
    rows_ref[2:3, :] = column_sum(dquery)
    rows_ref[3:4, :] = column_sum(branch)


def total_of(parts):
    total = parts[0][0].astype(F32) + parts[1][0].astype(F32)
    for part in parts[2:]:
        total = total + part[...].astype(F32)
    return total.astype(BF)


def cross_back_kernel(count, ready, slot_ref, vec_ref, enc_ref, n_ref, dquery_ref, res_ref, out_ref, out_near_ref, out_far_ref, *refs):
    parts, pieces = refs[:count], refs[count : count + 4]
    denc_ref, layer_ref, keep_ref, send_ref, rows_ref, full_ref, turned_ref, turned_enc_ref, sems = refs[count + 4 :]
    copies = start_copies(pieces, PAIR_AT, slot_ref, full_ref, sems, 0)
    ready()
    turned_ref[...] = n_ref[...].T
    put_grad(2, turned_ref, dquery_ref[...], slot_ref, keep_ref, send_ref)
    dkv = total_of(parts)
    turned_enc_ref[...] = enc_ref[...].T
    put_grad(0, turned_enc_ref, dkv[0], slot_ref, keep_ref, send_ref)
    put_grad(1, turned_enc_ref, dkv[1], slot_ref, keep_ref, send_ref)
    rows_ref[0:1, :] = column_sum(dkv[1])
    out = out_ref[...].astype(F32) + out_near_ref[...].astype(F32) + out_far_ref[...].astype(F32)
    layer_ref[...] = (res_ref[...] + out + vector(vec_ref, DOWN)).astype(BF)
    wait_all(copies)
    denc_ref[...] = (dot_t(dkv[0], full_ref[0]) + dot_t(dkv[1], full_ref[1])).astype(BF)


def self_back_kernel(count, ready, slot_ref, vec_ref, x_ref, n_ref, dquery_ref, dres_ref, up_ref, up_far_ref, ffn_ref, mid_ref, enc_ref, *refs):
    parts, pieces = refs[:count], refs[count : count + 4]
    dx_ref, keep_ref, send_ref, full_ref, turned_ref, sems = refs[count + 4 :]
    copies = start_packed(pieces, slot_ref, full_ref, sems)
    ready()
    dkv = total_of(parts)
    dquery = dquery_ref[...]
    turned_ref[...] = n_ref[...].T
    shard = turned_ref.shape[0] // 4
    for j in range(4):
        place = pl.ds(pl.multiple_of(slot_ref[j] * shard, shard), shard)
        target = send_ref if j % 2 else keep_ref
        target[j // 2, 0:shard] = dot(turned_ref[place, :], dkv[0]).astype(BF)
        target[j // 2, shard : 2 * shard] = dot(turned_ref[place, :], dkv[1]).astype(BF)
    wait_all(copies)
    dn = dot_t(dquery, full_ref[0]) + dot_t(dkv[0], full_ref[1]) + dot_t(dkv[1], full_ref[2])
    dvalues, dgain, dshift = norm_back(dn, x_ref[...].astype(F32), vector(vec_ref, GAIN))
    dx_ref[...] = (dres_ref[...] + dvalues).astype(BF)
    rows = [
        dgain,
        mid_ref[0:1, :],
        ffn_ref[0:1, :],
        column_sum(dquery),
        column_sum(dkv[1]),
        mid_ref[3:4, :],
        mid_ref[2:3, :],
        enc_ref[0:1, :],
        ffn_ref[2:3, :],
        dshift,
        mid_ref[1:2, :],
        ffn_ref[1:2, :],
    ]
    common = jnp.concatenate(rows + [ffn_ref[3:4, :]], axis=0)
    rest = keep_ref.shape[1] - 2 * shard
    for p in range(4):
        up = jnp.where(slot_ref[0] == p, up_ref[0:1, :] + up_far_ref[0:1, :], 0.0)
        parts = [common[i : i + 1, p * shard : (p + 1) * shard] for i in range(common.shape[0])]
        parts += [up[:, i * shard : (i + 1) * shard] for i in range(4)]
        parts += [jnp.zeros_like(parts[0])] * (-len(parts) % 4)
        lines = [jnp.concatenate(parts[i : i + 4], axis=1) for i in range(0, len(parts), 4)]
        lines.append(jnp.zeros((rest - len(lines), common.shape[1]), F32))
        lines = jnp.concatenate(lines, axis=0).astype(BF)
        flip = lax.bitwise_xor(slot_ref[0], p)

        @pl.when(lax.rem(flip, 2) == 0)
        def _():
            keep_ref[lax.div(flip, 2), 2 * shard :] = lines

        @pl.when(lax.rem(flip, 2) == 1)
        def _():
            send_ref[lax.div(flip, 2), 2 * shard :] = lines


def last_kernel(ready, flag_ref, late_a, late_b, middle_a, middle_b, own_ref, attn_ref, out_ref, gain_ref, bias_ref, up_ref, down_ref):
    ready()
    shard = attn_ref.shape[1]

    def join(first, a_ref, b_ref):
        a, b = a_ref[...].astype(F32), b_ref[...].astype(F32)
        first = first == 0
        return jnp.concatenate([jnp.where(first, a, b), jnp.where(first, b, a)], axis=0)

    late, middle = join(flag_ref[0], late_a, late_b), join(flag_ref[1], middle_a, middle_b)
    own = own_ref[...].astype(F32)

    def part(whole, i):
        return whole[i * shard : (i + 1) * shard, :]

    for i, (whole, j) in enumerate([(late, 2), (own, 0), (own, 1), (middle, 0), (late, 0), (late, 1)]):
        attn_ref[i] = part(whole, j)
    out_ref[0] = part(middle, 1)
    out_ref[1] = part(middle, 2)
    sums = own[2 * shard :, :]

    def row(i):
        return sums[i // 4 : i // 4 + 1, (i % 4) * shard : (i % 4 + 1) * shard]

    gain_ref[...] = jnp.concatenate([row(i) for i in range(3)], axis=0)
    bias_ref[...] = jnp.concatenate([row(i) for i in range(3, 12)], axis=0)
    down_ref[...] = row(12)
    up_ref[...] = jnp.concatenate([row(i) for i in range(13, 17)], axis=1)


ROWS_CUT = 32
ROWS_SUM = 64
WHOLE = pl.BlockSpec(memory_space=pltpu.VMEM)
LEFT = pl.BlockSpec(memory_space=pltpu.HBM)
SCALARS = pl.BlockSpec(memory_space=pltpu.SMEM)


def cost(microseconds):
    return pl.CostEstimate(flops=0, bytes_accessed=int(microseconds * 3.5e6), transcendentals=0)


def dense(kernel, scalars, blocks, pieces, outs, scratch, microseconds, copies=None):
    copies = len(pieces) if copies is None else copies
    held = 2 * sum(math.prod(b.shape) * b.dtype.itemsize for b in blocks)
    held += sum(math.prod(shape) * jnp.dtype(kind).itemsize for shape, kind in outs)
    held += sum(math.prod(ref.shape) * jnp.dtype(ref.dtype).itemsize for ref in scratch)
    n_s, n_b, n_p, n_o = len(scalars), len(blocks), len(pieces), len(outs)

    def body(*refs):
        near, refs = refs[:n_s], refs[n_s:]
        far, refs = refs[:n_b], refs[n_b:]
        rest, refs = refs[: n_p + n_o], refs[n_p + n_o :]
        local, sems, refs = refs[:n_b], refs[n_b], refs[n_b + 1 :]
        fetches = [pltpu.make_async_copy(far[i], local[i], sems.at[i]) for i in range(n_b)]
        for fetch in fetches:
            fetch.start()

        def ready():
            for fetch in fetches:
                fetch.wait()

        kernel(ready, *near, *local, *rest, *refs)

    return pl.pallas_call(
        body,
        in_specs=[SCALARS] * n_s + [LEFT] * (n_b + n_p),
        out_specs=[pl.BlockSpec(shape, lambda d=len(shape): (0,) * d) for shape, _ in outs],
        out_shape=[jax.ShapeDtypeStruct(shape, kind) for shape, kind in outs],
        scratch_shapes=[pltpu.VMEM(b.shape, b.dtype) for b in blocks]
        + [pltpu.SemaphoreType.DMA((n_b,))]
        + scratch
        + ([pltpu.SemaphoreType.DMA((copies,))] if pieces else []),
        compiler_params=pltpu.CompilerParams(vmem_limit_bytes=60 * MIB),
        cost_estimate=cost(microseconds),
    )(*scalars, *blocks, *pieces)


def hold(*values):
    return lax.optimization_barrier(values)


def per_device(
    layer_in,
    encoded,
    pairing,
    attn_weight,
    out_weight,
    up_weight,
    down_weight,
    norm_gains,
    bias_rows,
    up_bias,
    down_bias,
    out_cotangent,
):
    seqs, local_rows, width = layer_in.shape
    outer = lax.axis_size("o")
    groups = outer * 2
    half = local_rows // 2
    shard = attn_weight.shape[1]
    hidden = up_weight.shape[1]
    blocks = hidden // width
    rows = LINE * half
    enc_rows = LINE * (encoded.shape[1] // 2)
    fx, y, z, o, core = (lax.axis_index(a) for a in ("fx", "y", "z", "o", "core"))

    vectors = jnp.concatenate(
        [norm_gains, bias_rows, up_bias.reshape(blocks, shard), down_bias.reshape(1, shard)], axis=0
    )
    vectors = jnp.pad(vectors, ((0, ROWS_CUT - vectors.shape[0]), (0, width - shard)))
    slots = jnp.stack([2 * fx + core, 2 * fx + 1 - core, 2 - 2 * fx + core, 3 - 2 * fx - core])
    qkv_shard = jnp.concatenate([attn_weight[:3].reshape(3 * shard, width), vectors], axis=0)
    qkv_other = lax.ppermute(qkv_shard, "fx", SWAP)
    qkv_near = between_cores(qkv_shard)
    qkv_near, layer_in, encoded = hold(qkv_near, layer_in, encoded)
    x_bf, enc_bf = deal([layer_in, encoded])

    def places_of(pairing):
        group = o * 2 + y
        spots = []
        for step in range(groups):
            source = lax.rem(group - step + groups, groups)
            for flip in range(2):
                c = core if flip == 0 else 1 - core
                k = 2 * lax.rem(z, 2) + c
                for r in range(LINE):
                    line = lax.rem(r - k + LINE, LINE)
                    spots.append((((source // 2) * LINE + line) * 2 + lax.rem(source, 2)) * 2 + c)
        spans = jnp.take(pairing.reshape(-1), jnp.stack(spots), axis=0)
        return (spans[:, None] * half + jnp.arange(half, dtype=jnp.int32)[None, :]).reshape(-1, 1)

    product = 2 * rows * width * width
    square = (width, width)
    act, real = ((rows, width), BF), ((rows, width), F32)
    turned = pltpu.VMEM((width, rows), BF)

    def weights(n):
        return pltpu.VMEM((n,) + square, BF)

    def grads(n):
        return [((2, n, shard, width), BF)] * 2

    note = ((16, width), F32)

    x_bf, enc_bf, qkv_other, qkv_near, attn_weight, out_weight, up_weight, out_cotangent, pairing = hold(
        x_bf, enc_bf, qkv_other, qkv_near, attn_weight, out_weight, up_weight, out_cotangent, pairing
    )
    pair_shard = attn_weight[4:]
    key_places = places_of(pairing)
    mid_shard = jnp.concatenate([attn_weight[4:], attn_weight[3:4], out_weight], axis=0)
    rest_shard = jnp.concatenate([attn_weight[3:4], out_weight], axis=0)
    w_qkv = (qkv_shard, qkv_near, qkv_other, between_cores(qkv_other))
    pair_other = lax.ppermute(pair_shard, "fx", SWAP)
    mid_near = between_cores(mid_shard)
    extra = ROWS_CUT
    n1, query, kv, vec = dense(
        self_in_kernel,
        [slots],
        [x_bf],
        w_qkv,
        [act, act, ((2, rows, width), BF), ((TABLE, width), F32)],
        [weights(3), pltpu.VMEM((4, extra, width), BF)],
        4,
        copies=16,
    )
    n1, query, kv, vec, up_weight, key_places, out_cotangent = hold(
        n1, query, kv, vec, up_weight, key_places, out_cotangent
    )
    places = (key_places, key_places[:rows].reshape(1, -1))
    kv_self = to_others(kv, groups)
    near_self = between_cores(kv)
    up_cut = up_weight.reshape(shard, 4, width).transpose(1, 0, 2)
    cot_halves = deal_halves(out_cotangent)
    pair_other, rest_shard, mid_near = hold(pair_other, rest_shard, mid_near)
    rest_other = lax.ppermute(rest_shard, "fx", SWAP)
    w_pair = (mid_shard, mid_near, pair_other, between_cores(pair_other))
    (kv,) = dense(
        cross_in_kernel, [slots], [vec, enc_bf], w_pair, [((2, enc_rows, width), BF)], [weights(2)], 3.5
    )
    kv_self, near_self, kv, cot_halves, up_cut = hold(kv_self, near_self, kv, cot_halves, up_cut)
    cot = deal_line(*cot_halves)
    kv_cross = to_others(kv, groups)
    near_cross = between_cores(kv)
    kv_self = [kv_self[0], near_self] + with_cores(kv_self[1:])
    mixed, mass = attention(query, kv_self, places)
    mixed, mass, up_cut, rest_other, kv_cross, near_cross, cot = hold(
        mixed, mass, up_cut, rest_other, kv_cross, near_cross, cot
    )
    cot = deal_order(cot)
    cot_other = lax.ppermute(cot, "fx", SWAP)
    cot_near = between_cores(cot)
    w_rest = (mid_shard, mid_near, rest_other, between_cores(rest_other))
    kv_cross = [kv_cross[0], near_cross] + with_cores(kv_cross[1:])
    r1, n2, cquery = dense(middle_kernel, [slots], [vec, mixed, x_bf], w_rest, [real, act, act], [weights(2)], 3.3)
    r1, n2, cquery, kv_cross, up_cut, cot_other, cot_near = hold(r1, n2, cquery, kv_cross, up_cut, cot_other, cot_near)
    up_own = lax.all_to_all(up_cut, ("fx", "core"), 0, 0, tiled=True).reshape(width, width)
    cmixed, cmass = attention(cquery, kv_cross, None)
    cmixed, cmass, cot_other, cot_near = hold(cmixed, cmass, cot_other, cot_near)
    r2, n3 = dense(before_feed_kernel, [slots], [vec, cmixed, r1], w_rest, [real, act], [weights(1)], 2.7)
    r2, n3, cot_other = hold(r2, n3, cot_other)
    n3_other = lax.ppermute(n3, "fx", SWAP)
    n3_near, cot_far = between_cores(n3), between_cores(cot_other)
    n3_near, cot_far, n3, cot = hold(n3_near, cot_far, n3, cot)
    two = ((2, rows, width), BF)

    def feed_two(normed, cots):
        return dense(
            feed_kernel,
            [],
            [vec, up_own, down_weight] + normed + cots,
            [],
            [act, act, act, act, two, two, ((8, width), F32)],
            [],
            5,
        )

    dn_keep, dn_send, out_keep, out_send, act_a, dpre_a, rows_a = feed_two([n3, n3_near], [cot, cot_near])
    n3_other, act_a, dpre_a, rows_a, dn_keep, dn_send, out_keep, out_send = hold(
        n3_other, act_a, dpre_a, rows_a, dn_keep, dn_send, out_keep, out_send
    )
    n3_far = between_cores(n3_other)
    dn_got, out_got = between_cores(dn_send), between_cores(out_send)
    cots, n3s = [cot, cot_near, cot_other, cot_far], [n3, n3_near, n3_other, n3_far]
    dn_other, dn_send_b, out_other, out_send_b, act_b, dpre_b, rows_b = feed_two(n3s[2:], cots[2:])

    single = outer == 1

    def step(terms, name):
        return halve(terms, name) if single else terms

    def hold_all(*values):
        flat = hold([[term[0] for term in v] if isinstance(v, list) else v for v in values])[0]
        return [
            [(array, term[1]) for array, term in zip(new, old)] if isinstance(old, list) else new
            for new, old in zip(flat, values)
        ]

    dn_other_got = between_cores(dn_send_b)
    dn_other, dn_other_got, act_b, dpre_b, dn_got, out_got, out_send_b = hold(
        dn_other, dn_other_got, act_b, dpre_b, dn_got, out_got, out_send_b
    )
    dn_far = lax.ppermute(add([dn_other, dn_other_got]), "fx", SWAP)
    cut = ((4, 2, 4, shard // 4, width // 2), BF)
    up, down = dense(
        feed_grad_kernel, [], [act_a, act_b, dpre_a, dpre_b] + n3s + cots, [], [cut, cut], [], 6
    )
    dn_far, up, down, out_other, out_send_b = hold(dn_far, up, down, out_other, out_send_b)
    up, down = ([(part.reshape((2, 2, 2) + part.shape[2:]), ())] for part in (up, down))
    up, down = step(up, "y"), step(down, "z0")
    out_other_got = between_cores(out_send_b)
    dr2, doc, ffn_rows = dense(
        after_feed_kernel, [slots], [vec, dn_keep, dn_got, dn_far, r2, cot], w_rest, [real, act, note], [weights(1)], 2.7
    )

    dcq, cmine, ctheirs = attention_back(cquery, doc, cmixed, cmass, kv_cross, None)
    dcq, cmine, ctheirs, dr2, ffn_rows, out_other, out_other_got, up, down = hold_all(
        dcq, cmine, ctheirs, dr2, ffn_rows, out_other, out_other_got, up, down
    )
    cgot = between_cores(ctheirs)
    dr1, dos, middle_keep, middle_send, mid_rows = dense(
        middle_back_kernel,
        [slots],
        [vec, dcq, n2, r1, dr2, mixed, cmixed],
        w_rest,
        [real, act] + grads(3) + [note],
        [weights(2), turned],
        6,
    )
    dr1, dos, middle_keep, middle_send, mid_rows, cgot, cmine, up, down, out_other, out_other_got = hold_all(
        dr1, dos, middle_keep, middle_send, mid_rows, cgot, cmine, up, down, out_other, out_other_got
    )
    dckv = collect(cmine, cgot, groups)
    middle = over_cores(middle_keep, middle_send)
    up, down = step(up, "z0"), step(down, "z1")
    out_far = lax.ppermute(add([out_other, out_other_got]), "fx", SWAP)
    dq, mine, theirs = attention_back(query, dos, mixed, mass, kv_self, places)
    dq, mine, theirs, middle, up, down, out_far, dckv_a = hold_all(dq, mine, theirs, middle, up, down, out_far, dckv[-1])
    dckv = dckv[:-1] + [dckv_a]
    got = between_cores(theirs)
    grad_encoded, layer_out, late_keep, late_send, enc_rows_sum = dense(
        functools.partial(cross_back_kernel, len(dckv)),
        [slots],
        [vec, enc_bf, n1, dq, r2, out_keep, out_got, out_far] + dckv,
        w_pair,
        [((enc_rows, width), BF), act] + grads(3) + [note],
        [weights(2), turned, pltpu.VMEM((width, enc_rows), BF)],
        6,
    )
    mine, got, grad_encoded, layer_out, late_keep, late_send, enc_rows_sum, up, down, middle = hold_all(
        mine, got, grad_encoded, layer_out, late_keep, late_send, enc_rows_sum, up, down, middle
    )
    dkv = collect(mine, got, groups)
    late = over_cores(late_keep, late_send)
    late = over_x(late)
    if single:
        at = {name: half_index(name) for name in HALVES}
        middle = [array.reshape(2, 2, 2, 2, -1, width) for array, _ in middle]
        middle_z0 = exchange(add([pick(array, (1, 1 - at["z0"])) for array in middle]), "z0")
        up, down = both_halves(up, "z1"), both_halves(down, "y")
        dkv_last, up, down, late, middle, middle_z0 = hold_all(
            dkv[-1], [(part, ()) for part in up], [(part, ()) for part in down], late, [(part, ()) for part in middle], middle_z0
        )
        home = undeal_line([grad_encoded, layer_out])
        middle = [(array, (1, ("at", 1, at["z0"]))) for array, _ in middle] + [(middle_z0, (1,))]
        middle_x = lax.ppermute(add([half_of(term)[1] for term in middle]), "fx", SWAP)
        late = halve(late, "y")
    else:
        middle = over_x(middle)
        dkv_last, late, middle = hold_all(dkv[-1], late, middle)
    dkv = dkv[:-1] + [dkv_last]
    grad_layer, keep, send = dense(
        functools.partial(self_back_kernel, len(dkv)),
        [slots],
        [vec, x_bf, n1, dq, dr1, rows_a, rows_b, ffn_rows, mid_rows, enc_rows_sum] + dkv,
        w_qkv,
        [act] + [((2, 2 * shard + ROWS_SUM, width), BF)] * 2,
        [weights(3), turned],
        7,
        copies=12,
    )
    if single:
        grad_layer, keep, send, late, up, down, middle_x = hold_all(
            grad_layer, keep, send, late, up, down, middle_x
        )
        own = over_cores(keep, send)
        last = undeal_line([grad_layer])
        middle = [(array, names + (0,)) for array, names in middle] + [(middle_x, (1,))]
        home = undeal_cores(home)
        up, down = (add([part for part, _ in parts]) for parts in (up, down))
        down, late, middle = double(down, "z1"), halve(late, "z0"), halve(middle, "y")
        own, up = hold_all(own, up)
        home = [(p, ()) for p in home]
        own = over_x(own)
        up = lax.all_to_all(up, ("fx", "core"), 1, 1, tiled=True)
        late, middle = both_halves(late, "z1"), both_halves(middle, "z1")
        own, home, last, up, down = hold_all(own, home, last, up, down)
        grad_encoded, layer_out = undealt([p for p, _ in home], [F32, BF])
        last = undeal_cores(last)
        late, middle = add(late), add(middle)
        own = add([array[0] if 0 in names else array for array, names in own]).reshape(2 * LINE, -1, width)
        own = lax.all_to_all(own, ("z", "y"), 0, 0, tiled=True)
        late, middle = double(late, "z0"), double(middle, "y")
        up, down = double(up, "z0"), double(down, "z0")
        own, late, middle, last = hold(own, late, middle, last)
        own = jnp.sum(own.astype(F32), axis=0, keepdims=True).astype(BF)
        own = lax.all_to_all(jnp.broadcast_to(own, (2 * LINE,) + own.shape[1:]), ("z", "y"), 0, 0, tiled=True)
        up = double(up, "y")
        late, middle = (late, exchange(late, "y")), (middle, exchange(middle, "z0"))
        flags = jnp.stack([half_index("y"), half_index("z0")])
        (grad_layer,) = undealt(last, [F32])
        grad_attn, grad_out, *total = dense(
            last_kernel,
            [flags],
            [part.reshape(-1, width) for part in late + middle + (own,)],
            [],
            [((6, shard, width), F32), ((2, shard, width), F32), ((3, shard), F32), ((9, shard), F32)]
            + [((1, blocks * shard), F32), ((1, shard), F32)],
            [],
            3,
        )
        up, down = (part.astype(F32).reshape(2, 2, 2, 4, shard // 4, width // 2) for part in (up, down))
    else:
        own = over_cores(keep, send)
        (grad_layer,) = undeal([grad_layer], [F32])
        (grad_encoded,), (layer_out,) = undeal([grad_encoded], [F32]), undeal([layer_out], [BF])

        def over_ctx(terms, n):
            total = add([array[0] if 0 in names else array for array, names in terms])
            return lax.psum(total, ("o", "z", "y")).astype(F32).reshape(n, -1, width)

        own, middle, late = over_ctx(over_x(own), 1)[0], over_ctx(middle, 3), over_ctx(late, 3)
        up, down = (lax.psum(part[0][0], ("o", "z", "y")).astype(F32) for part in (up, down))
        up = lax.all_to_all(up.astype(BF), ("fx", "core"), 3, 3, tiled=True).astype(F32)
        total = own[2 * shard : 2 * shard + 5].reshape(-1, shard)
        total = [total[:3], total[3:12], total[13 : 13 + blocks].reshape(1, -1), total[12:13]]
        own = own[: 2 * shard].reshape(2, shard, width)
        grad_attn = jnp.concatenate([late[2:], own, middle[:1], late[:2]], axis=0)
        grad_out = middle[1:]
    g_up = up.transpose(0, 1, 4, 3, 2, 5).reshape(shard, hidden)
    g_down = down.transpose(3, 0, 1, 4, 2, 5).reshape(hidden // 4, width)
    return (
        layer_out,
        grad_layer,
        grad_encoded,
        grad_attn,
        grad_out,
        g_up,
        g_down,
        total[0],
        total[1],
        total[2].reshape(-1),
        total[3].reshape(-1),
    )


def solution(mesh):
    ctx = mesh.shape["ctx"]
    grid = Mesh(mesh.devices.reshape(2, 2, ctx // (2 * LINE), LINE, 2), ("fx", "core", "o", "z", "y"))
    fsdp = ("fx", "core")
    rows = P(fsdp, ("o", "z", "y"), None)
    weights = (
        P(None, fsdp, None),
        P(None, fsdp, None),
        P(fsdp, None),
        P(fsdp, None),
        P(None, fsdp),
        P(None, fsdp),
        P(fsdp),
        P(fsdp),
    )
    return jax.shard_map(
        per_device,
        mesh=grid,
        in_specs=(rows, rows, P()) + weights + (rows,),
        out_specs=(rows, rows, rows) + weights,
        check_vma=False,
    )
```

```python
import functools
import math

import jax
import jax.numpy as jnp
from jax import lax
from jax.experimental import pallas as pl
from jax.experimental.pallas import tpu as pltpu
from jax.sharding import Mesh
from jax.sharding import PartitionSpec as P

HEADS = 12
HD = 64
PAIR = 2 * HD
SCORE_SCALE = 0.125
MASK_FILL = -1e30
NORM_EPSILON = 1e-05
LINE = 4
SWAP = [(0, 1), (1, 0)]
BF = jnp.bfloat16
F32 = jnp.float32
MIB = 1 << 20


def dot(left, right):
    return jnp.dot(left, right, preferred_element_type=F32)


def dot_t(left, right):
    return lax.dot_general(left, right, (((1,), (1,)), ((), ())), preferred_element_type=F32)


def t_dot(left, right):
    return lax.dot_general(left, right, (((0,), (0,)), ((), ())), preferred_element_type=F32)


def split_heads(block):
    lane = lax.broadcasted_iota(jnp.int32, block.shape, 1)
    zero = jnp.zeros_like(block)
    return jnp.concatenate([jnp.where(lane < HD, block, zero), jnp.where(lane < HD, zero, block)], axis=0)


def join_heads(columns):
    rows = columns.shape[1] // 2
    return jnp.concatenate([columns[:HD, :rows], columns[HD:, rows:]], axis=0).T


def forward_kernel(masked, pieces, *refs):
    if masked:
        key_place_ref, query_place_ref, refs = refs[0], refs[1], refs[2:]
    query_ref, kv_refs = refs[0], refs[1 : 1 + pieces]
    out_ref, mass_ref, scores_ref = refs[1 + pieces :]
    query = split_heads(query_ref[...] * jnp.asarray(SCORE_SCALE, BF))
    piece = kv_refs[0].shape[1]
    if masked:
        query_place = query_place_ref[...]
        query_place = jnp.concatenate([query_place, query_place], axis=1)
    top = None
    for i in range(pieces):
        scores = dot_t(kv_refs[i][0], query)
        if masked:
            scores = jnp.where(key_place_ref[pl.ds(i * piece, piece), :] <= query_place, scores, MASK_FILL)
        scores_ref[pl.ds(i * piece, piece), :] = scores
        high = jnp.max(scores, axis=0, keepdims=True)
        top = high if top is None else jnp.maximum(top, high)
    mass = jnp.zeros_like(top)
    mixed = None
    for i in range(pieces):
        probs = jnp.exp(scores_ref[pl.ds(i * piece, piece), :] - top)
        mass = mass + jnp.sum(probs, axis=0, keepdims=True)
        part = t_dot(kv_refs[i][1], probs.astype(BF))
        mixed = part if mixed is None else mixed + part
    out_ref[...] = join_heads(mixed * (1.0 / mass)).astype(BF)
    mass_ref[0] = top + jnp.log(mass)


def backward_kernel(masked, pieces, *refs):
    if masked:
        key_place_ref, query_place_ref, refs = refs[0], refs[1], refs[2:]
    query_ref, dout_ref, out_ref, mass_ref = refs[:4]
    kv_refs = refs[4 : 4 + pieces]
    dquery_ref, mine_ref, theirs_ref = refs[4 + pieces :]
    query = split_heads(query_ref[...] * jnp.asarray(SCORE_SCALE, BF))
    dout = dout_ref[...]
    prod = (dout.astype(F32) * out_ref[...].astype(F32)).T
    delta = jnp.concatenate(
        [jnp.sum(prod[:HD], axis=0, keepdims=True), jnp.sum(prod[HD:], axis=0, keepdims=True)], axis=1
    )
    dout = split_heads(dout)
    log_mass = mass_ref[0]
    piece = kv_refs[0].shape[1]
    if masked:
        query_place = query_place_ref[...]
        query_place = jnp.concatenate([query_place, query_place], axis=1)
    dquery = None
    for i in range(pieces):
        keys = kv_refs[i][0]
        scores = dot_t(keys, query)
        if masked:
            scores = jnp.where(key_place_ref[pl.ds(i * piece, piece), :] <= query_place, scores, MASK_FILL)
        probs = jnp.exp(scores - log_mass)
        dprobs = dot_t(kv_refs[i][1], dout)
        dscores = (probs * (dprobs - delta)).astype(BF)
        dkv_ref = theirs_ref if i % 2 else mine_ref
        dkv_ref[i // 2, 0] = dot(dscores, query).astype(BF)
        dkv_ref[i // 2, 1] = dot(probs.astype(BF), dout).astype(BF)
        part = t_dot(keys, dscores)
        dquery = part if dquery is None else dquery + part
    dquery_ref[...] = (join_heads(dquery) * SCORE_SCALE).astype(BF)


def place_specs(masked, places):
    if not masked:
        return [], []
    key_places, query_places = places
    return [key_places, query_places], [
        pl.BlockSpec(key_places.shape, lambda h: (0, 0)),
        pl.BlockSpec(query_places.shape, lambda h: (0, 0)),
    ]


def attention(query, kv, places):
    masked = places is not None
    rows, width = query.shape
    piece = kv[0].shape[1]
    extra, extra_specs = place_specs(masked, places)
    keys = piece * len(kv)
    return pl.pallas_call(
        functools.partial(forward_kernel, masked, len(kv)),
        grid=(width // PAIR,),
        in_specs=extra_specs
        + [pl.BlockSpec((rows, PAIR), lambda h: (0, h))]
        + [pl.BlockSpec((2, piece, PAIR), lambda h: (0, 0, h))] * len(kv),
        out_specs=[
            pl.BlockSpec((rows, PAIR), lambda h: (0, h)),
            pl.BlockSpec((1, 1, 2 * rows), lambda h: (h, 0, 0)),
        ],
        out_shape=[
            jax.ShapeDtypeStruct((rows, width), BF),
            jax.ShapeDtypeStruct((width // PAIR, 1, 2 * rows), F32),
        ],
        scratch_shapes=[pltpu.VMEM((keys, 2 * rows), F32)],
        compiler_params=pltpu.CompilerParams(vmem_limit_bytes=56 * MIB),
        cost_estimate=cost(8 * rows * keys / 2**18),
    )(*extra, query, *kv)


def attention_back(query, dout, out, mass, kv, places):
    masked = places is not None
    rows, width = query.shape
    piece = kv[0].shape[1]
    extra, extra_specs = place_specs(masked, places)
    keys = piece * len(kv)
    column = pl.BlockSpec((rows, PAIR), lambda h: (0, h))
    pair = pl.BlockSpec((2, piece, PAIR), lambda h: (0, 0, h))
    groups = len(kv) // 2
    blocks = pl.BlockSpec((groups, 2, piece, PAIR), lambda h: (0, 0, 0, h))
    return pl.pallas_call(
        functools.partial(backward_kernel, masked, len(kv)),
        grid=(width // PAIR,),
        in_specs=extra_specs
        + [column, column, column, pl.BlockSpec((1, 1, 2 * rows), lambda h: (h, 0, 0))]
        + [pair] * len(kv),
        out_specs=[column, blocks, blocks],
        out_shape=[jax.ShapeDtypeStruct((rows, width), BF)]
        + [jax.ShapeDtypeStruct((groups, 2, piece, width), BF)] * 2,
        compiler_params=pltpu.CompilerParams(vmem_limit_bytes=56 * MIB),
        cost_estimate=cost(13 * rows * keys / 2**18),
    )(*extra, query, dout, out, mass, *kv)


def forward_whole(pieces, *refs):
    far, (out_ref, mass_ref), refs = refs[: 1 + pieces], refs[1 + pieces : 3 + pieces], refs[3 + pieces :]
    local, refs = refs[: 1 + pieces], refs[1 + pieces :]
    scores_ref, sems = refs
    fetches = [pltpu.make_async_copy(far[i], local[i], sems.at[i]) for i in range(1 + pieces)]
    for fetch in fetches:
        fetch.start()
    query_ref, kv_refs = local[0], local[1:]
    piece = kv_refs[0].shape[1]
    for pair in range(query_ref.shape[1] // PAIR):
        columns = pl.ds(pair * PAIR, PAIR)
        if pair == 0:
            fetches[0].wait()
        query = split_heads(query_ref[:, columns] * jnp.asarray(SCORE_SCALE, BF))
        top = None
        for i in range(pieces):
            if pair == 0:
                fetches[1 + i].wait()
            scores = dot_t(kv_refs[i][0, :, columns], query)
            scores_ref[pl.ds(i * piece, piece), :] = scores
            high = jnp.max(scores, axis=0, keepdims=True)
            top = high if top is None else jnp.maximum(top, high)
        mass, mixed = jnp.zeros_like(top), None
        for i in range(pieces):
            probs = jnp.exp(scores_ref[pl.ds(i * piece, piece), :] - top)
            mass = mass + jnp.sum(probs, axis=0, keepdims=True)
            part = t_dot(kv_refs[i][1, :, columns], probs.astype(BF))
            mixed = part if mixed is None else mixed + part
        out_ref[:, columns] = join_heads(mixed * (1.0 / mass)).astype(BF)
        mass_ref[pair] = top + jnp.log(mass)


WHOLE_KEYS = 2048


def attention_whole(query, kv):
    rows, width = query.shape
    keys = kv[0].shape[1] * len(kv)
    operands = [query] + list(kv)
    outs = [((rows, width), BF), ((width // PAIR, 1, 2 * rows), F32)]
    return pl.pallas_call(
        functools.partial(forward_whole, len(kv)),
        in_specs=[LEFT] * len(operands),
        out_specs=[WHOLE] * len(outs),
        out_shape=[jax.ShapeDtypeStruct(shape, kind) for shape, kind in outs],
        scratch_shapes=[pltpu.VMEM(a.shape, a.dtype) for a in operands]
        + [pltpu.VMEM((keys, 2 * rows), F32), pltpu.SemaphoreType.DMA((len(operands),))],
        compiler_params=pltpu.CompilerParams(vmem_limit_bytes=56 * MIB),
        cost_estimate=cost(8),
    )(*operands)


def deal_perms():
    perms = []
    for r in range(LINE):
        perm = []
        for c in range(2):
            for z in range(LINE):
                k = (r - z) % LINE
                perm.append((c * LINE + z, (k % 2) * LINE + 2 * c + k // 2))
        perms.append(perm)
    return perms


DEAL = deal_perms()


def deal(arrays):
    if len({array.shape for array in arrays}) > 1:
        return [deal([array])[0] for array in arrays]
    _, rows, width = arrays[0].shape
    chunks = [array.reshape(LINE, rows // 2, width) for array in arrays]
    z = lax.axis_index("z")
    got = []
    for r in range(LINE):
        k = lax.rem(r - z + LINE, LINE)
        chunk = jnp.stack([lax.dynamic_index_in_dim(c, k, keepdims=False) for c in chunks])
        got.append(lax.ppermute(chunk, ("core", "z"), DEAL[r]))
    return [jnp.concatenate([g[i] for g in got], axis=0) for i in range(len(arrays))]


def undeal_line(arrays):
    core, z = lax.axis_index("core"), lax.axis_index("z")
    chunks = jnp.stack([array.reshape(LINE, -1, array.shape[-1]) for array in arrays], axis=1)
    start = lax.rem(2 * lax.rem(z, 2) + core, LINE)
    chunks = lax.dynamic_slice_in_dim(jnp.concatenate([chunks, chunks], axis=0), start, LINE, axis=0)
    return lax.all_to_all(chunks, "z", 0, 0, tiled=True)


def undeal_cores(chunks):
    core = lax.axis_index("core")
    chunks = chunks.reshape((2, 2) + chunks.shape[1:])
    mine = lax.dynamic_index_in_dim(chunks, core, 0, keepdims=False)
    return mine, lax.ppermute(lax.dynamic_index_in_dim(chunks, 1 - core, 0, keepdims=False), "core", SWAP)


def undealt(halves, kinds):
    first = lax.axis_index("core") == 0
    outs = []
    for i, kind in enumerate(kinds):
        mine, got = (half[:, i].astype(kind) for half in halves)
        both = jnp.where(first, jnp.stack([mine, got], axis=1), jnp.stack([got, mine], axis=1))
        outs.append(both.reshape(2, -1, both.shape[-1]))
    return outs


def deal_halves(array):
    _, rows, width = array.shape
    parts = array.reshape(2, 2, rows // 2, width)
    core = lax.axis_index("core")
    mine = lax.dynamic_index_in_dim(parts, core, 1, keepdims=False)
    return mine, lax.ppermute(lax.dynamic_index_in_dim(parts, 1 - core, 1, keepdims=False), "core", SWAP)


def deal_line(mine, got):
    first = lax.axis_index("core") == 0
    chunks = jnp.where(first, jnp.concatenate([mine, got], axis=0), jnp.concatenate([got, mine], axis=0))
    return lax.all_to_all(chunks, "z", 0, 0, tiled=True)


def deal_order(chunks):
    core, z = lax.axis_index("core"), lax.axis_index("z")
    start = lax.rem(LINE - 2 * lax.rem(z, 2) - core, LINE)
    mine = lax.dynamic_slice_in_dim(jnp.concatenate([chunks, chunks], axis=0), start, LINE, axis=0)
    return mine.reshape(-1, mine.shape[-1])


def undeal(arrays, kind):
    count = len(arrays)
    half = arrays[0].shape[0] // LINE
    got = []
    for r in range(LINE):
        chunk = jnp.stack([array[r * half : (r + 1) * half] for array in arrays])
        got.append(lax.ppermute(chunk, ("core", "z"), [(b, a) for a, b in DEAL[r]]))
    z = lax.axis_index("z")
    outs = []
    for i in range(count):
        mine = lax.dynamic_slice_in_dim(jnp.stack([g[i] for g in got + got]), z, LINE, axis=0)
        outs.append(mine.reshape(2, 2 * half, arrays[0].shape[1]).astype(kind[i]))
    return outs


def group_perm(groups, step):
    return [(i, (i + step) % groups) for i in range(groups)]


def to_others(own, groups):
    return [own] + [lax.ppermute(own, ("o", "y"), group_perm(groups, step)) for step in range(1, groups)]


def with_cores(blocks):
    pieces = []
    for block in blocks:
        pieces += [block, lax.ppermute(block, "core", SWAP)]
    return pieces


def collect(mine, got, groups):
    terms = [mine, got]
    for step in range(1, groups):
        back = [(b, a) for a, b in group_perm(groups, step)]
        terms.append(lax.ppermute(add([mine[step], got[step]]), ("o", "y"), back))
    return terms


def between_cores(array):
    return lax.ppermute(array, "core", SWAP)


def gather(own, other):
    return own, lax.ppermute(own, "core", SWAP), other, lax.ppermute(other, "core", SWAP)


def after(value, earlier):
    return lax.optimization_barrier((value, earlier))[0]


def add(terms):
    total = terms[0].astype(F32)
    for term in terms[1:]:
        total = total + term.astype(F32)
    return total.astype(BF)


def over_cores(keep, send):
    return [(keep, ()), (lax.ppermute(send, "core", SWAP), ())]


def over_x(terms):
    got = lax.ppermute(add([array[1] for array, _ in terms]), "fx", SWAP)
    return [(array, (0,)) for array, _ in terms] + [(got, ())]


def part_over_x(terms, first, last):
    return lax.ppermute(add([array[1, first:last] for array, _ in terms]), "fx", SWAP)


def pick(array, *path):
    for axis, index in path:
        array = lax.dynamic_index_in_dim(array, index, axis, keepdims=False)
    return array


HALVES = ("y", "z0", "z1")


def exchange(array, name):
    if name == "y":
        return lax.ppermute(array, "y", SWAP)
    flip = 1 if name == "z0" else 2
    return lax.ppermute(array, "z", [(i, i ^ flip) for i in range(LINE)])


def half_index(name):
    z = lax.axis_index("z")
    return lax.axis_index("y") if name == "y" else lax.rem(z, 2) if name == "z0" else lax.div(z, 2)


def half_of(term, more=()):
    array, names = term
    cut = 1 in names
    if 0 in names and 1 not in names and len(names + more) > 1:
        array = array.reshape(2, 2, 2, 2, -1, array.shape[-1])
        cut = True
    for name in names + more:
        if name in (0, 1):
            array = array if name else array[0]
            continue
        if name[0] == "at":
            array = pick(array, name[1:])
            continue
        name, other = name if isinstance(name, tuple) else (name, False)
        if array.ndim == 3 and not cut:
            array = array.reshape(2, 2, 2, -1, array.shape[-1])
        cut = True
        i = half_index(name)
        array = lax.dynamic_index_in_dim(array, 1 - i if other else i, 0, keepdims=False)
    return array


def halve(terms, name):
    theirs = add([half_of(term, ((name, True),)) for term in terms])
    got = exchange(theirs, name)
    return [(array, names + (name,)) for array, names in terms] + [(got, (1,))]


def both_halves(terms, name):
    mine = add([half_of(term) for term in terms])
    got = exchange(mine, name)
    mine = lax.optimization_barrier(mine)
    return mine, got


def double(part, name):
    other = exchange(part, name)
    first = half_index(name) == 0
    return jnp.where(first, jnp.concatenate([part, other], axis=0), jnp.concatenate([other, part], axis=0))


def standard(values):
    center = values - jnp.mean(values, axis=-1, keepdims=True)
    inverse = lax.rsqrt(jnp.mean(center * center, axis=-1, keepdims=True) + NORM_EPSILON)
    return center * inverse, inverse


def norm_back(dnormed, values, gain):
    z, inverse = standard(values)
    a = dnormed * gain
    dvalues = (
        a - jnp.mean(a, axis=-1, keepdims=True) - z * jnp.mean(a * z, axis=-1, keepdims=True)
    ) * inverse
    return dvalues, jnp.sum(dnormed * z, axis=0, keepdims=True), jnp.sum(dnormed, axis=0, keepdims=True)


def column_sum(values):
    return jnp.sum(values.astype(F32), axis=0, keepdims=True)


GAIN, BIAS, UP, DOWN = 0, 3, 12, 13
TABLE = 24
PAIR_AT, REST_AT, LAST_AT = (0, 0, 0, 0), (2, 2, 0, 0), (4, 4, 2, 2)


def vector(vec_ref, row):
    return vec_ref[row : row + 1, :]


def start_packed(pieces, slot_ref, full_ref, sems):
    n, rows = full_ref.shape[0], full_ref.shape[1] // 4
    copies = []
    for j, piece in enumerate(pieces):
        place = pl.ds(pl.multiple_of(slot_ref[j] * rows, rows), rows)
        for i in range(n):
            copy = pltpu.make_async_copy(
                piece.at[pl.ds(i * rows, rows), :], full_ref.at[i, place, :], sems.at[j * n + i]
            )
            copy.start()
            copies.append(copy)
    return copies


def start_copies(pieces, firsts, slot_ref, full_ref, sems, base):
    copies = []
    for j, piece in enumerate(pieces):
        rows = piece.shape[-2]
        place = pl.ds(pl.multiple_of(slot_ref[j] * rows, rows), rows)
        if len(piece.shape) == 3:
            source, target = piece.at[pl.ds(firsts[j], full_ref.shape[0])], full_ref.at[:, place, :]
        else:
            source, target = piece, full_ref.at[place, :]
        copy = pltpu.make_async_copy(source, target, sems.at[base + j])
        copy.start()
        copies.append(copy)
    return copies


def wait_all(copies):
    for copy in copies:
        copy.wait()


def put_grad(unit, turned, right, slot_ref, keep_ref, send_ref):
    rows = turned.shape[0] // 4
    for j in range(4):
        place = pl.ds(pl.multiple_of(slot_ref[j] * rows, rows), rows)
        block = dot(turned[place, :], right).astype(BF)
        target = send_ref if j % 2 else keep_ref
        target[j // 2, unit] = block


def self_in_kernel(ready, slot_ref, x_ref, *refs):
    pieces, (n_ref, query_ref, kv_ref, vec_ref, full_ref, parts_ref, sems) = refs[:4], refs[4:]
    weights, shard = full_ref.shape[0], full_ref.shape[1] // 4
    extra = parts_ref.shape[1]
    small = []
    for j, piece in enumerate(pieces):
        copy = pltpu.make_async_copy(
            piece.at[pl.ds(weights * shard, extra), :], parts_ref.at[j], sems.at[4 * weights + j]
        )
        copy.start()
        small.append(copy)
    copies = start_packed(pieces, slot_ref, full_ref, sems)
    ready()
    z = standard(x_ref[...].astype(F32))[0]
    wait_all(small)
    parts = [parts_ref[lax.bitwise_xor(slot_ref[0], p)].astype(F32)[:, :shard] for p in range(4)]
    own = parts_ref[0].astype(F32)[:, :shard]
    table = jnp.concatenate(parts, axis=1)
    vec_ref[0:UP, :] = table[0:UP]
    vec_ref[UP:DOWN, :] = jnp.concatenate([own[UP + i : UP + i + 1] for i in range(4)], axis=1)
    vec_ref[DOWN : DOWN + 1, :] = table[UP + 4 : UP + 5]
    normed = (z * table[GAIN : GAIN + 1] + table[BIAS + 6 : BIAS + 7]).astype(BF)
    n_ref[...] = normed
    wait_all(copies)
    kv_ref[0] = dot(normed, full_ref[1]).astype(BF)
    kv_ref[1] = (dot(normed, full_ref[2]) + table[BIAS + 1 : BIAS + 2]).astype(BF)
    query_ref[...] = (dot(normed, full_ref[0]) + table[BIAS : BIAS + 1]).astype(BF)


def cross_in_kernel(ready, slot_ref, vec_ref, enc_ref, *refs):
    pieces, (kv_ref, full_ref, sems) = refs[:4], refs[4:]
    copies = start_copies(pieces, PAIR_AT, slot_ref, full_ref, sems, 0)
    ready()
    enc = enc_ref[...]
    wait_all(copies)
    kv_ref[0] = dot(enc, full_ref[0]).astype(BF)
    kv_ref[1] = (dot(enc, full_ref[1]) + vector(vec_ref, BIAS + 4)).astype(BF)


def middle_kernel(ready, slot_ref, vec_ref, mixed_ref, x_ref, *refs):
    pieces, (res_ref, n_ref, query_ref, full_ref, sems) = refs[:4], refs[4:]
    copies = start_copies(pieces, REST_AT, slot_ref, full_ref, sems, 0)
    ready()
    wait_all(copies)
    res = x_ref[...].astype(F32) + dot(mixed_ref[...], full_ref[1]) + vector(vec_ref, BIAS + 2)
    res_ref[...] = res
    normed = (standard(res)[0] * vector(vec_ref, GAIN + 1) + vector(vec_ref, BIAS + 7)).astype(BF)
    n_ref[...] = normed
    query_ref[...] = (dot(normed, full_ref[0]) + vector(vec_ref, BIAS + 3)).astype(BF)


def before_feed_kernel(ready, slot_ref, vec_ref, mixed_ref, res_ref, *refs):
    pieces, (out_ref, n_ref, full_ref, sems) = refs[:4], refs[4:]
    copies = start_copies(pieces, LAST_AT, slot_ref, full_ref, sems, 0)
    ready()
    wait_all(copies)
    res = res_ref[...] + dot(mixed_ref[...], full_ref[0]) + vector(vec_ref, BIAS + 5)
    out_ref[...] = res
    n_ref[...] = (standard(res)[0] * vector(vec_ref, GAIN + 2) + vector(vec_ref, BIAS + 8)).astype(BF)


def feed_kernel(ready, vec_ref, up_ref, down_ref, *refs):
    normed_refs, cot_refs = refs[:2], refs[2:4]
    dn_keep, dn_send, out_keep, out_send, act_ref, dpre_ref, rows_ref = refs[4:]
    ready()
    bias = vector(vec_ref, UP)
    total = None
    for j in (1, 0):
        pre = dot(normed_refs[j][...], up_ref[...]) + bias
        phi = 0.5 * (1.0 + lax.erf(pre * math.sqrt(0.5)))
        slope = phi + pre * (jnp.exp(-0.5 * pre * pre) * (1.0 / math.sqrt(2.0 * math.pi)))
        act = (pre * phi).astype(BF)
        dpre = (dot_t(cot_refs[j][...], down_ref[...]) * slope).astype(BF)
        out, dn = (out_send, dn_send) if j else (out_keep, dn_keep)
        dn[...] = dot_t(dpre, up_ref[...]).astype(BF)
        out[...] = dot(act, down_ref[...]).astype(BF)
        act_ref[j] = act
        dpre_ref[j] = dpre
        sums = column_sum(dpre)
        total = sums if total is None else total + sums
    rows_ref[0:1, :] = total


def feed_grad_kernel(ready, act_a, act_b, dpre_a, dpre_b, *refs):
    normed_refs, cot_refs, (up_ref, down_ref) = refs[:4], refs[4:8], refs[8:]
    quarter, half = up_ref.shape[-2:]
    ready()

    def put(grad, cut_ref):
        for p in range(4):
            for q in range(4):
                rows = grad[(4 * p + q) * quarter : (4 * p + q + 1) * quarter].astype(BF)
                cut_ref[q, 0, p] = rows[:, :half]
                cut_ref[q, 1, p] = rows[:, half:]

    total = None
    for j in range(4):
        part = t_dot(normed_refs[j][...], (dpre_b if j > 1 else dpre_a)[j % 2])
        total = part if total is None else total + part
    put(total, up_ref)
    total = None
    for j in range(4):
        part = t_dot((act_b if j > 1 else act_a)[j % 2], cot_refs[j][...])
        total = part if total is None else total + part
    put(total, down_ref)


def after_feed_kernel(ready, slot_ref, vec_ref, dn_ref, dn_near_ref, dn_far_ref, res_ref, cot_ref, *refs):
    pieces, (dres_ref, dout_ref, rows_ref, full_ref, sems) = refs[:4], refs[4:]
    copies = start_copies(pieces, LAST_AT, slot_ref, full_ref, sems, 0)
    ready()
    dn = dn_ref[...].astype(F32) + dn_near_ref[...].astype(F32) + dn_far_ref[...].astype(F32)
    cot = cot_ref[...].astype(F32)
    dvalues, dgain, dshift = norm_back(dn, res_ref[...], vector(vec_ref, GAIN + 2))
    dres = cot + dvalues
    dres_ref[...] = dres
    branch = dres.astype(BF)
    wait_all(copies)
    dout_ref[...] = dot_t(branch, full_ref[0]).astype(BF)
    rows_ref[0:1, :] = dgain
    rows_ref[1:2, :] = dshift
    rows_ref[2:3, :] = column_sum(branch)
    rows_ref[3:4, :] = column_sum(cot)


def middle_back_kernel(ready, slot_ref, vec_ref, dquery_ref, n_ref, res_ref, dres_ref, mixed_ref, cmixed_ref, *refs):
    pieces, (dout_res_ref, dout_ref, keep_ref, send_ref, rows_ref, full_ref, turned_ref, sems) = refs[:4], refs[4:]
    copies = start_copies(pieces, REST_AT, slot_ref, full_ref, sems, 0)
    ready()
    turned_ref[...] = n_ref[...].T
    dquery = dquery_ref[...]
    put_grad(0, turned_ref, dquery, slot_ref, keep_ref, send_ref)
    wait_all(copies)
    dn = dot_t(dquery, full_ref[0])
    dvalues, dgain, dshift = norm_back(dn, res_ref[...], vector(vec_ref, GAIN + 1))
    turned_ref[...] = cmixed_ref[...].T
    put_grad(2, turned_ref, dres_ref[...].astype(BF), slot_ref, keep_ref, send_ref)
    dres = dres_ref[...] + dvalues
    dout_res_ref[...] = dres
    branch = dres.astype(BF)
    dout_ref[...] = dot_t(branch, full_ref[1]).astype(BF)
    turned_ref[...] = mixed_ref[...].T
    put_grad(1, turned_ref, branch, slot_ref, keep_ref, send_ref)
    rows_ref[0:1, :] = dgain
    rows_ref[1:2, :] = dshift
    rows_ref[2:3, :] = column_sum(dquery)
    rows_ref[3:4, :] = column_sum(branch)


def total_of(parts):
    total = parts[0][0].astype(F32) + parts[1][0].astype(F32)
    for part in parts[2:]:
        total = total + part[...].astype(F32)
    return total.astype(BF)


def cross_back_kernel(count, ready, slot_ref, vec_ref, enc_ref, n_ref, dquery_ref, res_ref, out_ref, out_near_ref, out_far_ref, *refs):
    parts, pieces = refs[:count], refs[count : count + 4]
    denc_ref, layer_ref, keep_ref, send_ref, rows_ref, full_ref, turned_ref, turned_enc_ref, sems = refs[count + 4 :]
    copies = start_copies(pieces, PAIR_AT, slot_ref, full_ref, sems, 0)
    ready()
    turned_ref[...] = n_ref[...].T
    put_grad(2, turned_ref, dquery_ref[...], slot_ref, keep_ref, send_ref)
    dkv = total_of(parts)
    turned_enc_ref[...] = enc_ref[...].T
    put_grad(0, turned_enc_ref, dkv[0], slot_ref, keep_ref, send_ref)
    put_grad(1, turned_enc_ref, dkv[1], slot_ref, keep_ref, send_ref)
    rows_ref[0:1, :] = column_sum(dkv[1])
    out = out_ref[...].astype(F32) + out_near_ref[...].astype(F32) + out_far_ref[...].astype(F32)
    layer_ref[...] = (res_ref[...] + out + vector(vec_ref, DOWN)).astype(BF)
    wait_all(copies)
    denc_ref[...] = (dot_t(dkv[0], full_ref[0]) + dot_t(dkv[1], full_ref[1])).astype(BF)


def self_back_kernel(count, ready, slot_ref, vec_ref, x_ref, n_ref, dquery_ref, dres_ref, up_ref, up_far_ref, ffn_ref, mid_ref, enc_ref, *refs):
    parts, pieces = refs[:count], refs[count : count + 4]
    dx_ref, keep_ref, send_ref, full_ref, turned_ref, sems = refs[count + 4 :]
    copies = start_packed(pieces, slot_ref, full_ref, sems)
    ready()
    dkv = total_of(parts)
    dquery = dquery_ref[...]
    turned_ref[...] = n_ref[...].T
    shard = turned_ref.shape[0] // 4
    for j in range(4):
        place = pl.ds(pl.multiple_of(slot_ref[j] * shard, shard), shard)
        target = send_ref if j % 2 else keep_ref
        target[j // 2, 0:shard] = dot(turned_ref[place, :], dkv[0]).astype(BF)
        target[j // 2, shard : 2 * shard] = dot(turned_ref[place, :], dkv[1]).astype(BF)
    wait_all(copies)
    dn = dot_t(dquery, full_ref[0]) + dot_t(dkv[0], full_ref[1]) + dot_t(dkv[1], full_ref[2])
    dvalues, dgain, dshift = norm_back(dn, x_ref[...].astype(F32), vector(vec_ref, GAIN))
    dx_ref[...] = (dres_ref[...] + dvalues).astype(BF)
    rows = [
        dgain,
        mid_ref[0:1, :],
        ffn_ref[0:1, :],
        column_sum(dquery),
        column_sum(dkv[1]),
        mid_ref[3:4, :],
        mid_ref[2:3, :],
        enc_ref[0:1, :],
        ffn_ref[2:3, :],
        dshift,
        mid_ref[1:2, :],
        ffn_ref[1:2, :],
    ]
    common = jnp.concatenate(rows + [ffn_ref[3:4, :]], axis=0)
    rest = keep_ref.shape[1] - 2 * shard
    for p in range(4):
        up = jnp.where(slot_ref[0] == p, up_ref[0:1, :] + up_far_ref[0:1, :], 0.0)
        parts = [common[i : i + 1, p * shard : (p + 1) * shard] for i in range(common.shape[0])]
        parts += [up[:, i * shard : (i + 1) * shard] for i in range(4)]
        parts += [jnp.zeros_like(parts[0])] * (-len(parts) % 4)
        lines = [jnp.concatenate(parts[i : i + 4], axis=1) for i in range(0, len(parts), 4)]
        lines.append(jnp.zeros((rest - len(lines), common.shape[1]), F32))
        lines = jnp.concatenate(lines, axis=0).astype(BF)
        flip = lax.bitwise_xor(slot_ref[0], p)

        @pl.when(lax.rem(flip, 2) == 0)
        def _():
            keep_ref[lax.div(flip, 2), 2 * shard :] = lines

        @pl.when(lax.rem(flip, 2) == 1)
        def _():
            send_ref[lax.div(flip, 2), 2 * shard :] = lines


def last_kernel(ready, flag_ref, late_a, late_b, middle_a, middle_b, own_ref, attn_ref, out_ref, gain_ref, bias_ref, up_ref, down_ref):
    ready()
    shard = attn_ref.shape[1]

    def join(first, a_ref, b_ref):
        a, b = a_ref[...].astype(F32), b_ref[...].astype(F32)
        first = first == 0
        return jnp.concatenate([jnp.where(first, a, b), jnp.where(first, b, a)], axis=0)

    late, middle = join(flag_ref[0], late_a, late_b), join(flag_ref[1], middle_a, middle_b)
    own = own_ref[...].astype(F32)

    def part(whole, i):
        return whole[i * shard : (i + 1) * shard, :]

    for i, (whole, j) in enumerate([(late, 2), (own, 0), (own, 1), (middle, 0), (late, 0), (late, 1)]):
        attn_ref[i] = part(whole, j)
    out_ref[0] = part(middle, 1)
    out_ref[1] = part(middle, 2)
    sums = own[2 * shard :, :]

    def row(i):
        return sums[i // 4 : i // 4 + 1, (i % 4) * shard : (i % 4 + 1) * shard]

    gain_ref[...] = jnp.concatenate([row(i) for i in range(3)], axis=0)
    bias_ref[...] = jnp.concatenate([row(i) for i in range(3, 12)], axis=0)
    down_ref[...] = row(12)
    up_ref[...] = jnp.concatenate([row(i) for i in range(13, 17)], axis=1)


ROWS_CUT = 32
ROWS_SUM = 64
WHOLE = pl.BlockSpec(memory_space=pltpu.VMEM)
LEFT = pl.BlockSpec(memory_space=pltpu.HBM)
SCALARS = pl.BlockSpec(memory_space=pltpu.SMEM)


def cost(microseconds):
    return pl.CostEstimate(flops=0, bytes_accessed=int(microseconds * 3.5e6), transcendentals=0)


def dense(kernel, scalars, blocks, pieces, outs, scratch, microseconds, copies=None):
    copies = len(pieces) if copies is None else copies
    held = 2 * sum(math.prod(b.shape) * b.dtype.itemsize for b in blocks)
    held += sum(math.prod(shape) * jnp.dtype(kind).itemsize for shape, kind in outs)
    held += sum(math.prod(ref.shape) * jnp.dtype(ref.dtype).itemsize for ref in scratch)
    n_s, n_b, n_p, n_o = len(scalars), len(blocks), len(pieces), len(outs)

    def body(*refs):
        near, refs = refs[:n_s], refs[n_s:]
        far, refs = refs[:n_b], refs[n_b:]
        rest, refs = refs[: n_p + n_o], refs[n_p + n_o :]
        local, sems, refs = refs[:n_b], refs[n_b], refs[n_b + 1 :]
        fetches = [pltpu.make_async_copy(far[i], local[i], sems.at[i]) for i in range(n_b)]
        for fetch in fetches:
            fetch.start()

        def ready():
            for fetch in fetches:
                fetch.wait()

        kernel(ready, *near, *local, *rest, *refs)

    return pl.pallas_call(
        body,
        in_specs=[SCALARS] * n_s + [LEFT] * (n_b + n_p),
        out_specs=[pl.BlockSpec(shape, lambda d=len(shape): (0,) * d) for shape, _ in outs],
        out_shape=[jax.ShapeDtypeStruct(shape, kind) for shape, kind in outs],
        scratch_shapes=[pltpu.VMEM(b.shape, b.dtype) for b in blocks]
        + [pltpu.SemaphoreType.DMA((n_b,))]
        + scratch
        + ([pltpu.SemaphoreType.DMA((copies,))] if pieces else []),
        compiler_params=pltpu.CompilerParams(vmem_limit_bytes=56 * MIB),
        cost_estimate=cost(microseconds),
    )(*scalars, *blocks, *pieces)


def hold(*values):
    return lax.optimization_barrier(values)


def per_device(
    layer_in,
    encoded,
    pairing,
    attn_weight,
    out_weight,
    up_weight,
    down_weight,
    norm_gains,
    bias_rows,
    up_bias,
    down_bias,
    out_cotangent,
):
    seqs, local_rows, width = layer_in.shape
    outer = lax.axis_size("o")
    groups = outer * 2
    half = local_rows // 2
    shard = attn_weight.shape[1]
    hidden = up_weight.shape[1]
    blocks = hidden // width
    rows = LINE * half
    enc_rows = LINE * (encoded.shape[1] // 2)
    fx, y, z, o, core = (lax.axis_index(a) for a in ("fx", "y", "z", "o", "core"))

    vectors = jnp.concatenate(
        [norm_gains, bias_rows, up_bias.reshape(blocks, shard), down_bias.reshape(1, shard)], axis=0
    )
    vectors = jnp.pad(vectors, ((0, ROWS_CUT - vectors.shape[0]), (0, width - shard)))
    slots = jnp.stack([2 * fx + core, 2 * fx + 1 - core, 2 - 2 * fx + core, 3 - 2 * fx - core])
    qkv_shard = jnp.concatenate([attn_weight[:3].reshape(3 * shard, width), vectors], axis=0)
    qkv_other = lax.ppermute(qkv_shard, "fx", SWAP)
    qkv_near = between_cores(qkv_shard)
    qkv_near, layer_in, encoded = hold(qkv_near, layer_in, encoded)
    x_bf, enc_bf = deal([layer_in, encoded])

    def places_of(pairing):
        group = o * 2 + y
        spots = []
        for step in range(groups):
            source = lax.rem(group - step + groups, groups)
            for flip in range(2):
                c = core if flip == 0 else 1 - core
                k = 2 * lax.rem(z, 2) + c
                for r in range(LINE):
                    line = lax.rem(r - k + LINE, LINE)
                    spots.append((((source // 2) * LINE + line) * 2 + lax.rem(source, 2)) * 2 + c)
        spans = jnp.take(pairing.reshape(-1), jnp.stack(spots), axis=0)
        return (spans[:, None] * half + jnp.arange(half, dtype=jnp.int32)[None, :]).reshape(-1, 1)

    product = 2 * rows * width * width
    square = (width, width)
    act, real = ((rows, width), BF), ((rows, width), F32)
    turned = pltpu.VMEM((width, rows), BF)

    def weights(n):
        return pltpu.VMEM((n,) + square, BF)

    def grads(n):
        return [((2, n, shard, width), BF)] * 2

    note = ((16, width), F32)

    x_bf, enc_bf, qkv_other, qkv_near, attn_weight, out_weight, up_weight, out_cotangent, pairing = hold(
        x_bf, enc_bf, qkv_other, qkv_near, attn_weight, out_weight, up_weight, out_cotangent, pairing
    )
    pair_shard = attn_weight[4:]
    key_places = places_of(pairing)
    mid_shard = jnp.concatenate([attn_weight[4:], attn_weight[3:4], out_weight], axis=0)
    rest_shard = jnp.concatenate([attn_weight[3:4], out_weight], axis=0)
    w_qkv = (qkv_shard, qkv_near, qkv_other, between_cores(qkv_other))
    pair_other = lax.ppermute(pair_shard, "fx", SWAP)
    mid_near = between_cores(mid_shard)
    extra = ROWS_CUT
    n1, query, kv, vec = dense(
        self_in_kernel,
        [slots],
        [x_bf],
        w_qkv,
        [act, act, ((2, rows, width), BF), ((TABLE, width), F32)],
        [weights(3), pltpu.VMEM((4, extra, width), BF)],
        4,
        copies=16,
    )
    n1, query, kv, vec, up_weight, key_places, out_cotangent = hold(
        n1, query, kv, vec, up_weight, key_places, out_cotangent
    )
    places = (key_places, key_places[:rows].reshape(1, -1))
    kv_self = to_others(kv, groups)
    near_self = between_cores(kv)
    up_cut = up_weight.reshape(shard, 4, width).transpose(1, 0, 2)
    cot_halves = deal_halves(out_cotangent)
    pair_other, rest_shard, mid_near = hold(pair_other, rest_shard, mid_near)
    rest_other = lax.ppermute(rest_shard, "fx", SWAP)
    w_pair = (mid_shard, mid_near, pair_other, between_cores(pair_other))
    (kv,) = dense(
        cross_in_kernel, [slots], [vec, enc_bf], w_pair, [((2, enc_rows, width), BF)], [weights(2)], 3.5
    )
    kv_self, near_self, kv, cot_halves, up_cut = hold(kv_self, near_self, kv, cot_halves, up_cut)
    cot = deal_line(*cot_halves)
    kv_cross = to_others(kv, groups)
    near_cross = between_cores(kv)
    kv_self = [kv_self[0], near_self] + with_cores(kv_self[1:])
    mixed, mass = attention(query, kv_self, places)
    mixed, mass, up_cut, rest_other, kv_cross, near_cross, cot = hold(
        mixed, mass, up_cut, rest_other, kv_cross, near_cross, cot
    )
    cot = deal_order(cot)
    cot_other = lax.ppermute(cot, "fx", SWAP)
    cot_near = between_cores(cot)
    w_rest = (mid_shard, mid_near, rest_other, between_cores(rest_other))
    kv_cross = [kv_cross[0], near_cross] + with_cores(kv_cross[1:])
    r1, n2, cquery = dense(middle_kernel, [slots], [vec, mixed, x_bf], w_rest, [real, act, act], [weights(2)], 3.3)
    r1, n2, cquery, kv_cross, up_cut, cot_other, cot_near = hold(r1, n2, cquery, kv_cross, up_cut, cot_other, cot_near)
    up_own = lax.all_to_all(up_cut, ("fx", "core"), 0, 0, tiled=True).reshape(width, width)
    whole = kv_cross[0].shape[1] * len(kv_cross) <= WHOLE_KEYS and enc_rows == rows
    cmixed, cmass = attention_whole(cquery, kv_cross) if whole else attention(cquery, kv_cross, None)
    cmixed, cmass, cot_other, cot_near = hold(cmixed, cmass, cot_other, cot_near)
    r2, n3 = dense(before_feed_kernel, [slots], [vec, cmixed, r1], w_rest, [real, act], [weights(1)], 2.7)
    r2, n3, cot_other = hold(r2, n3, cot_other)
    n3_other = lax.ppermute(n3, "fx", SWAP)
    n3_near, cot_far = between_cores(n3), between_cores(cot_other)
    n3_near, cot_far, n3, cot = hold(n3_near, cot_far, n3, cot)
    two = ((2, rows, width), BF)

    def feed_two(normed, cots):
        return dense(
            feed_kernel,
            [],
            [vec, up_own, down_weight] + normed + cots,
            [],
            [act, act, act, act, two, two, ((8, width), F32)],
            [],
            5,
        )

    dn_keep, dn_send, out_keep, out_send, act_a, dpre_a, rows_a = feed_two([n3, n3_near], [cot, cot_near])
    n3_other, act_a, dpre_a, rows_a, dn_keep, dn_send, out_keep, out_send = hold(
        n3_other, act_a, dpre_a, rows_a, dn_keep, dn_send, out_keep, out_send
    )
    n3_far = between_cores(n3_other)
    dn_got, out_got = between_cores(dn_send), between_cores(out_send)
    cots, n3s = [cot, cot_near, cot_other, cot_far], [n3, n3_near, n3_other, n3_far]
    dn_other, dn_send_b, out_other, out_send_b, act_b, dpre_b, rows_b = feed_two(n3s[2:], cots[2:])

    single = outer == 1

    def step(terms, name):
        return halve(terms, name) if single else terms

    def hold_all(*values):
        flat = hold([[term[0] for term in v] if isinstance(v, list) else v for v in values])[0]
        return [
            [(array, term[1]) for array, term in zip(new, old)] if isinstance(old, list) else new
            for new, old in zip(flat, values)
        ]

    dn_other_got = between_cores(dn_send_b)
    dn_other, dn_other_got, act_b, dpre_b, dn_got, out_got, out_send_b = hold(
        dn_other, dn_other_got, act_b, dpre_b, dn_got, out_got, out_send_b
    )
    dn_far = lax.ppermute(add([dn_other, dn_other_got]), "fx", SWAP)
    cut = ((4, 2, 4, shard // 4, width // 2), BF)
    up, down = dense(
        feed_grad_kernel, [], [act_a, act_b, dpre_a, dpre_b] + n3s + cots, [], [cut, cut], [], 6
    )
    dn_far, up, down, out_other, out_send_b = hold(dn_far, up, down, out_other, out_send_b)
    up, down = ([(part.reshape((2, 2, 2) + part.shape[2:]), ())] for part in (up, down))
    up, down = step(up, "y"), step(down, "z0")
    out_other_got = between_cores(out_send_b)
    dr2, doc, ffn_rows = dense(
        after_feed_kernel, [slots], [vec, dn_keep, dn_got, dn_far, r2, cot], w_rest, [real, act, note], [weights(1)], 2.7
    )

    dcq, cmine, ctheirs = attention_back(cquery, doc, cmixed, cmass, kv_cross, None)
    dcq, cmine, ctheirs, dr2, ffn_rows, out_other, out_other_got, up, down = hold_all(
        dcq, cmine, ctheirs, dr2, ffn_rows, out_other, out_other_got, up, down
    )
    cgot = between_cores(ctheirs)
    dr1, dos, middle_keep, middle_send, mid_rows = dense(
        middle_back_kernel,
        [slots],
        [vec, dcq, n2, r1, dr2, mixed, cmixed],
        w_rest,
        [real, act] + grads(3) + [note],
        [weights(2), turned],
        6,
    )
    dr1, dos, middle_keep, middle_send, mid_rows, cgot, cmine, up, down, out_other, out_other_got = hold_all(
        dr1, dos, middle_keep, middle_send, mid_rows, cgot, cmine, up, down, out_other, out_other_got
    )
    dckv = collect(cmine, cgot, groups)
    middle = over_cores(middle_keep, middle_send)
    up, down = step(up, "z0"), step(down, "z1")
    out_far = lax.ppermute(add([out_other, out_other_got]), "fx", SWAP)
    dq, mine, theirs = attention_back(query, dos, mixed, mass, kv_self, places)
    dq, mine, theirs, middle, up, down, out_far, dckv_a = hold_all(dq, mine, theirs, middle, up, down, out_far, dckv[-1])
    dckv = dckv[:-1] + [dckv_a]
    got = between_cores(theirs)
    grad_encoded, layer_out, late_keep, late_send, enc_rows_sum = dense(
        functools.partial(cross_back_kernel, len(dckv)),
        [slots],
        [vec, enc_bf, n1, dq, r2, out_keep, out_got, out_far] + dckv,
        w_pair,
        [((enc_rows, width), BF), act] + grads(3) + [note],
        [weights(2), turned, pltpu.VMEM((width, enc_rows), BF)],
        6,
    )
    mine, got, grad_encoded, layer_out, late_keep, late_send, enc_rows_sum, up, down, middle = hold_all(
        mine, got, grad_encoded, layer_out, late_keep, late_send, enc_rows_sum, up, down, middle
    )
    dkv = collect(mine, got, groups)
    late = over_cores(late_keep, late_send)
    late = over_x(late)
    if single:
        at = {name: half_index(name) for name in HALVES}
        middle = [array.reshape(2, 2, 2, 2, -1, width) for array, _ in middle]
        middle_z0 = exchange(add([pick(array, (1, 1 - at["z0"])) for array in middle]), "z0")
        up, down = both_halves(up, "z1"), both_halves(down, "y")
        dkv_last, up, down, late, middle, middle_z0 = hold_all(
            dkv[-1], [(part, ()) for part in up], [(part, ()) for part in down], late, [(part, ()) for part in middle], middle_z0
        )
        home = undeal_line([grad_encoded, layer_out])
        middle = [(array, (1, ("at", 1, at["z0"]))) for array, _ in middle] + [(middle_z0, (1,))]
        middle_x = lax.ppermute(add([half_of(term)[1] for term in middle]), "fx", SWAP)
        late = halve(late, "y")
    else:
        middle = over_x(middle)
        dkv_last, late, middle = hold_all(dkv[-1], late, middle)
    dkv = dkv[:-1] + [dkv_last]
    grad_layer, keep, send = dense(
        functools.partial(self_back_kernel, len(dkv)),
        [slots],
        [vec, x_bf, n1, dq, dr1, rows_a, rows_b, ffn_rows, mid_rows, enc_rows_sum] + dkv,
        w_qkv,
        [act] + [((2, 2 * shard + ROWS_SUM, width), BF)] * 2,
        [weights(3), turned],
        7,
        copies=12,
    )
    if single:
        grad_layer, keep, send, late, up, down, middle_x = hold_all(
            grad_layer, keep, send, late, up, down, middle_x
        )
        own = over_cores(keep, send)
        last = undeal_line([grad_layer])
        middle = [(array, names + (0,)) for array, names in middle] + [(middle_x, (1,))]
        home = undeal_cores(home)
        up, down = (add([part for part, _ in parts]) for parts in (up, down))
        down, late, middle = double(down, "z1"), halve(late, "z0"), halve(middle, "y")
        own, up = hold_all(own, up)
        home = [(p, ()) for p in home]
        own = over_x(own)
        up = lax.all_to_all(up, ("fx", "core"), 1, 1, tiled=True)
        late, middle = both_halves(late, "z1"), both_halves(middle, "z1")
        own, home, last, up, down = hold_all(own, home, last, up, down)
        grad_encoded, layer_out = undealt([p for p, _ in home], [F32, BF])
        last = undeal_cores(last)
        late, middle = add(late), add(middle)
        own = add([array[0] if 0 in names else array for array, names in own]).reshape(2 * LINE, -1, width)
        own = lax.all_to_all(own, ("z", "y"), 0, 0, tiled=True)
        late, middle = double(late, "z0"), double(middle, "y")
        up, down = double(up, "z0"), double(down, "z0")
        own, late, middle, last = hold(own, late, middle, last)
        own = jnp.sum(own.astype(F32), axis=0, keepdims=True).astype(BF)
        own = lax.all_to_all(jnp.broadcast_to(own, (2 * LINE,) + own.shape[1:]), ("z", "y"), 0, 0, tiled=True)
        up = double(up, "y")
        late, middle = (late, exchange(late, "y")), (middle, exchange(middle, "z0"))
        flags = jnp.stack([half_index("y"), half_index("z0")])
        (grad_layer,) = undealt(last, [F32])
        grad_attn, grad_out, *total = dense(
            last_kernel,
            [flags],
            [part.reshape(-1, width) for part in late + middle + (own,)],
            [],
            [((6, shard, width), F32), ((2, shard, width), F32), ((3, shard), F32), ((9, shard), F32)]
            + [((1, blocks * shard), F32), ((1, shard), F32)],
            [],
            3,
        )
        up, down = (part.astype(F32).reshape(2, 2, 2, 4, shard // 4, width // 2) for part in (up, down))
    else:
        own = over_cores(keep, send)
        (grad_layer,) = undeal([grad_layer], [F32])
        (grad_encoded,), (layer_out,) = undeal([grad_encoded], [F32]), undeal([layer_out], [BF])

        def over_ctx(terms, n):
            total = add([array[0] if 0 in names else array for array, names in terms])
            return lax.psum(total, ("o", "z", "y")).astype(F32).reshape(n, -1, width)

        own, middle, late = over_ctx(over_x(own), 1)[0], over_ctx(middle, 3), over_ctx(late, 3)
        up, down = (lax.psum(part[0][0], ("o", "z", "y")).astype(F32) for part in (up, down))
        up = lax.all_to_all(up.astype(BF), ("fx", "core"), 3, 3, tiled=True).astype(F32)
        total = own[2 * shard : 2 * shard + 5].reshape(-1, shard)
        total = [total[:3], total[3:12], total[13 : 13 + blocks].reshape(1, -1), total[12:13]]
        own = own[: 2 * shard].reshape(2, shard, width)
        grad_attn = jnp.concatenate([late[2:], own, middle[:1], late[:2]], axis=0)
        grad_out = middle[1:]
    g_up = up.transpose(0, 1, 4, 3, 2, 5).reshape(shard, hidden)
    g_down = down.transpose(3, 0, 1, 4, 2, 5).reshape(hidden // 4, width)
    return (
        layer_out,
        grad_layer,
        grad_encoded,
        grad_attn,
        grad_out,
        g_up,
        g_down,
        total[0],
        total[1],
        total[2].reshape(-1),
        total[3].reshape(-1),
    )


def solution(mesh):
    ctx = mesh.shape["ctx"]
    grid = Mesh(mesh.devices.reshape(2, 2, ctx // (2 * LINE), LINE, 2), ("fx", "core", "o", "z", "y"))
    fsdp = ("fx", "core")
    rows = P(fsdp, ("o", "z", "y"), None)
    weights = (
        P(None, fsdp, None),
        P(None, fsdp, None),
        P(fsdp, None),
        P(fsdp, None),
        P(None, fsdp),
        P(None, fsdp),
        P(fsdp),
        P(fsdp),
    )
    return jax.shard_map(
        per_device,
        mesh=grid,
        in_specs=(rows, rows, P()) + weights + (rows,),
        out_specs=(rows, rows, rows) + weights,
        check_vma=False,
    )
```
